256 devices in a mesh: member: 4 (over x), grid: 64 (over y, z, core).
Axes of the slice: x: 4, y: 4, z: 8, core: 2. Of those that a mesh axis runs over, the one named last changes fastest.
Arguments:
- states: bfloat16 [16, 2048, 1024], P('member', 'grid')
- ln_gain: float32 [1024], replicated, may hold values from 0.1 to 1.9
- w_qkv: bfloat16 [1024, 3072], replicated
- w_out: bfloat16 [1024, 1024], replicated, may hold values from -0.75 to 0.75
- w_head: bfloat16 [1024, 100], replicated, may hold values from -0.1875 to 0.1875
- targets: float32 [2048, 100], P('grid'), may hold values from -6 to 6
- neighbours: int32 [128, 4], P('grid'), may hold values from 0 to 127, as said below
- counts: int32 [64], P('grid'), may hold values from 16 to 32
Outputs:
- loss: float32 [], replicated
- grad_states: bfloat16 [16, 2048, 1024], P('member', 'grid')
- head_grad: float32 [1024, 100], replicated
The draws below stay inside these ranges and needn't reach their ends.
Inputs may be any that keep to these rules, and one draw needn't show every extreme that they name: neighbours[t, 0] is t; the other entries of row t are distinct tiles within 2 of t, except near the first and last tiles, where an entry beyond the grid is reflected to the other side of t and may then repeat.
All inputs are finite; a program needn't handle non-finite values.
Results may differ from the reference program's by a relative error of at most 0.02.
The reference program's roundings to bfloat16 on the way count: a program that leaves them out, or rounds other values in their place, can miss the bound.
Values may be sent and summed in bfloat16 or wider, within the bound.
A program may use at most 128 MiB of HBM per device.

```python
import math
import jax
import jax.numpy as jnp
from jax import lax

D = 1024
HEADS = 16
VARS = 100
POINTS_DEV = 32
TILE = 16
REACH = 2
NB = 4
MEMBERS = 16
POINTS = 2048
TILES = 128
SHARDS = 64


def draw_states(key, part):
    key = jax.random.fold_in(key, 1)
    first = jax.random.fold_in(key, 0)
    base = jax.random.normal(first, (MEMBERS, POINTS, D), jnp.float32)
    return jnp.clip(base, -8.0, 8.0).astype(jnp.bfloat16)


def draw_w_qkv(key, part):
    key = jax.random.fold_in(key, 2)
    first = jax.random.fold_in(key, 0)
    base = jax.random.normal(first, (D, 3 * D), jnp.float32) / math.sqrt(D)
    return base.astype(jnp.bfloat16)


def draw_neighbours(key, part):
    key = jax.random.fold_in(key, 3)
    tiles = jnp.arange(TILES, dtype=jnp.int32)[:, None]
    raw = jax.random.randint(key, (TILES, 2 * REACH), 0, 1 << 20, jnp.int32) * (2 * REACH) + jnp.arange(2 * REACH, dtype=jnp.int32)[None, :]
    order = jnp.argsort(raw, axis=1, stable=True).astype(jnp.int32)
    offsets = jnp.where(order < REACH, order - REACH, order - REACH + 1)[:, :NB - 1]
    landing = tiles + offsets
    offsets = jnp.where((landing < 0) | (landing >= TILES), -offsets, offsets)
    return jnp.concatenate([tiles, tiles + offsets], axis=1).astype(jnp.int32)


def draw_counts(key, part):
    key = jax.random.fold_in(key, 4)
    first, second = jax.random.split(key, 2)
    values = jax.random.randint(first, (SHARDS,), POINTS_DEV // 2, POINTS_DEV + 1, jnp.int32)
    order = jax.random.permutation(second, SHARDS)
    places = jnp.arange(SHARDS, dtype=jnp.int32)
    values = jnp.where(places == order[0], POINTS_DEV, values)
    values = jnp.where(places == order[1], POINTS_DEV // 2, values)
    return values.astype(jnp.int32)


def levels(key, dims, cuts, smallest, largest):
    gain = 1.0
    for axis_at, blocks in cuts:
        draws = jax.random.uniform(jax.random.fold_in(jax.random.fold_in(key, 6), axis_at), (blocks,), jnp.float32, smallest / len(cuts), largest / len(cuts))
        gain = gain * jnp.repeat(jnp.exp(draws), dims[axis_at] // blocks).reshape((-1,) + (1,) * (len(dims) - 1 - axis_at))
    return gain


def noise(rng, extent, deviation, reach, shards=(), held_as=jnp.bfloat16):
    result = jax.random.normal(rng, extent, jnp.float32) * deviation
    if len(shards) > 0:
        result = levels(rng, extent, shards, -0.22, 0.18) * result
    return jnp.clip(result, min=-reach, max=reach).astype(held_as)


def setup_inputs(seed: int = 0) -> dict:
    arg_keys = jax.random.split(jax.random.key(seed), 9)
    states = draw_states(jax.random.fold_in(arg_keys[8], 71), 0)
    ln_gain = jnp.clip(1.0 + 0.18 * jax.random.normal(arg_keys[1], (D,), jnp.float32), 0.1, 1.9)
    w_qkv = draw_w_qkv(jax.random.fold_in(arg_keys[8], 71), 0)
    w_out = noise(arg_keys[3], (D, D), (D // 16) ** -0.5, 0.75)
    w_head = noise(arg_keys[4], (D, VARS), D ** -0.5, 0.1875)
    targets = noise(arg_keys[5], (POINTS, VARS), 1.0, 6.0, ((0, 64),), jnp.float32)
    neighbours = draw_neighbours(jax.random.fold_in(arg_keys[8], 71), 0)
    counts = draw_counts(jax.random.fold_in(arg_keys[8], 71), 0)
    return {"states": states, "ln_gain": ln_gain, "w_qkv": w_qkv, "w_out": w_out, "w_head": w_head, "targets": targets, "neighbours": neighbours, "counts": counts}


EPS = 1e-05
DELTA = 0.1

def normalize(states, ln_gain):
    values = states.astype(jnp.float32)
    centre = lax.optimization_barrier(jnp.mean(values, axis=-1, keepdims=True))
    centred = values - centre
    spread = lax.optimization_barrier(jnp.mean(centred * centred, axis=-1, keepdims=True))
    inverse = lax.rsqrt(spread + EPS)
    normed = centred * inverse
    return (normed, inverse, (normed * ln_gain).astype(jnp.bfloat16))

def to_bf16_f32(values):
    return lax.optimization_barrier(values.astype(jnp.bfloat16)).astype(jnp.float32)

def crps_terms(ensemble, target, valid):
    count = ensemble.shape[0]
    miss = ensemble - target[None]
    spread_one = jnp.sqrt(miss * miss + DELTA * DELTA)
    pairs = ensemble[:, None] - ensemble[None]
    spread_two = jnp.sqrt(pairs * pairs + DELTA * DELTA)
    weight = valid.astype(jnp.float32)[:, None]
    fair = lax.optimization_barrier(jnp.mean(spread_one, axis=0)) - (lax.optimization_barrier(jnp.sum(spread_two, axis=(0, 1))) - count * DELTA) / (2.0 * count * (count - 1))
    terms = weight * count * fair
    grad = weight[None] * (miss / spread_one - lax.optimization_barrier(jnp.sum(pairs / spread_two, axis=1)) / (count - 1))
    return (terms, grad)

def reference(states, ln_gain, w_qkv, w_out, w_head, targets, neighbours, counts):
    members, points, width = states.shape
    hdim = width // HEADS
    scale = hdim ** (-0.5)
    flat = members * points
    normed, inverse, hidden = normalize(states, ln_gain)
    qkv = jnp.dot(hidden.reshape(flat, width), w_qkv, preferred_element_type=jnp.float32)
    qkv = qkv.astype(jnp.bfloat16).reshape(members, points, 3 * width)
    query = qkv[..., :width]
    keyval = qkv[..., width:]
    key_rows = (neighbours[:, :, None] * TILE + jnp.arange(TILE, dtype=jnp.int32)[None, None, :]).reshape(TILES, -1)

    def prepare(q_m, kv_m):
        query5 = q_m.reshape(TILES, TILE, HEADS, hdim).astype(jnp.float32)
        picked = kv_m[key_rows]
        keys5 = picked[..., :width].reshape(TILES, -1, HEADS, hdim).astype(jnp.float32)
        values5 = picked[..., width:].reshape(TILES, -1, HEADS, hdim).astype(jnp.float32)
        scores = jnp.einsum('tqhd,tkhd->thqk', query5, keys5) * scale
        top = lax.optimization_barrier(jnp.max(scores, axis=-1, keepdims=True))
        expo = jnp.exp(scores - top)
        probs = expo / lax.optimization_barrier(jnp.sum(expo, axis=-1, keepdims=True))
        return (query5, keys5, values5, probs, to_bf16_f32(probs))

    def forward_one(pair):
        query5, keys5, values5, probs, probs_b = prepare(pair[0], pair[1])
        out = jnp.einsum('thqk,tkhd->tqhd', probs_b, values5)
        return out.astype(jnp.bfloat16).reshape(points, width)
    attn = lax.map(forward_one, (query, keyval))
    proj = jnp.dot(attn.reshape(flat, width), w_out, preferred_element_type=jnp.float32)
    mixed = (states.astype(jnp.float32).reshape(flat, width) + proj).astype(jnp.bfloat16)
    pred = jnp.dot(mixed, w_head, preferred_element_type=jnp.float32).reshape(members, points, VARS)
    shard_pred = pred.reshape(members, SHARDS, POINTS_DEV, VARS).transpose(1, 0, 2, 3)
    shard_target = targets.reshape(SHARDS, POINTS_DEV, VARS)
    valid = jnp.arange(POINTS_DEV, dtype=jnp.int32)[None, :] < counts[:, None]
    terms, grads = lax.map(lambda item: crps_terms(item[0], item[1], item[2]), (shard_pred, shard_target, valid))
    loss = jnp.sum(terms) / (POINTS * VARS * members)
    grad = grads.transpose(1, 0, 2, 3).reshape(flat, VARS)
    grad_b = grad.astype(jnp.bfloat16)
    head_grad = lax.dot_general(mixed, grad_b, (((0,), (0,)), ((), ())), preferred_element_type=jnp.float32) / POINTS
    dmixed = lax.dot_general(grad_b, w_head, (((1,), (1,)), ((), ())), preferred_element_type=jnp.float32)
    dattn = lax.dot_general(dmixed.astype(jnp.bfloat16), w_out, (((1,), (1,)), ((), ())), preferred_element_type=jnp.float32)
    dattn = dattn.astype(jnp.bfloat16).reshape(members, points, width)
    w_query = w_qkv[:, :width]
    w_kv32 = w_qkv[:, width:].astype(jnp.float32)

    def backward_one(triple):
        query5, keys5, values5, probs, probs_b = prepare(triple[0], triple[1])
        dattn5 = triple[2].reshape(TILES, TILE, HEADS, hdim).astype(jnp.float32)
        dprobs = jnp.einsum('tqhd,tkhd->thqk', dattn5, values5)
        dscores = to_bf16_f32(probs * (dprobs - lax.optimization_barrier(jnp.sum(dprobs * probs, axis=-1, keepdims=True))) * scale)
        dquery = jnp.einsum('thqk,tkhd->tqhd', dscores, keys5).astype(jnp.bfloat16).reshape(points, width)
        dkeys = jnp.einsum('thqk,tqhd->tkhd', dscores, query5).reshape(TILES, -1, width)
        dvalues = jnp.einsum('thqk,tqhd->tkhd', probs_b, dattn5).reshape(TILES, -1, width)
        contrib = jnp.concatenate([dkeys, dvalues], axis=-1).reshape(-1, 2 * width)
        dkv = jnp.zeros((points, 2 * width), jnp.float32).at[key_rows.reshape(-1)].add(contrib)
        part_q = lax.dot_general(dquery, w_query, (((1,), (1,)), ((), ())), preferred_element_type=jnp.float32)
        part_kv = lax.dot_general(dkv, w_kv32, (((1,), (1,)), ((), ())), precision=lax.Precision.HIGHEST, preferred_element_type=jnp.float32)
        return part_q + part_kv
    dhidden = lax.map(backward_one, (query, keyval, dattn))
    dnormed = dhidden * ln_gain
    dstates = inverse * (dnormed - lax.optimization_barrier(jnp.mean(dnormed, axis=-1, keepdims=True)) - normed * lax.optimization_barrier(jnp.mean(dnormed * normed, axis=-1, keepdims=True)))
    grad_states = (dstates + dmixed.reshape(members, points, width)).astype(jnp.bfloat16)
    return (loss, grad_states, head_grad)
```

```python
import functools

import jax
import jax.numpy as jnp
from jax import lax
from jax.experimental import pallas as pl
from jax.experimental.pallas import tpu as pltpu
from jax.sharding import PartitionSpec as P

HEADS = 16
VARS = 100
TILE = 16
EPS = 1e-05
DELTA = 0.1
LANES = 128
PACK = 4
INNER = 16
BLOCK = 256
MESH = pl.DeviceIdType.MESH
F32 = jnp.float32
BF16 = jnp.bfloat16

NN = (((1,), (0,)), ((), ()))
NT = (((1,), (1,)), ((), ()))
TN = (((0,), (0,)), ((), ()))


def dot(a, b, dims):
    return lax.dot_general(a, b, dims, preferred_element_type=F32)


def kernel(
    sizes,
    states,
    gain,
    wqkv_hbm,
    wout_hbm,
    whead,
    targets,
    neighbours,
    counts,
    loss,
    grad,
    head_out,
    wqkv,
    wout,
    wpad,
    tpad,
    hall,
    query,
    kv,
    normed,
    inverse,
    cnt,
    hmask,
    probs,
    attn,
    mixed,
    ens,
    gradb,
    local,
    part,
    plane,
    full,
    dmixed,
    dmixedb,
    dattn,
    dquery,
    dkv,
    dsend,
    drecv,
    dhid,
    wsem,
    halo_s,
    halo_r,
    pred_s,
    pred_r,
    part_s,
    part_r,
    plane_s,
    plane_r,
    full_s,
    full_r,
    back_s,
    back_r,
):
    n_member, n_grid, n_inner = sizes
    n_outer = n_grid // n_inner
    group = n_member * n_outer
    members, points, width = states.shape
    window = hall.shape[1]
    flat = members * points
    cols = PACK * (width // HEADS)
    chunks = width // BLOCK
    packs = HEADS // PACK
    total_members = members * n_member
    piece = width // group

    me_m = lax.axis_index("member")
    me_g = lax.axis_index("grid")
    outer = me_g // n_inner
    inner = lax.rem(me_g, n_inner)
    up = lax.rem(me_g + 1, n_grid)
    down = lax.rem(me_g + n_grid - 1, n_grid)
    mine = me_m * n_outer + outer

    def group_peer(k):
        m = lax.rem(me_m + k // n_outer, n_member)
        o = lax.rem(outer + lax.rem(k, n_outer), n_outer)
        return m, o

    def inner_peer(k):
        return (me_m, outer * n_inner + lax.rem(inner + k, n_inner))

    barrier = pltpu.get_barrier_semaphore()

    def greet_group(k, c):
        m, o = group_peer(k)
        pl.semaphore_signal(barrier, inc=1, device_id=(m, o * n_inner + inner), device_id_type=MESH)
        return c

    def greet_inner(k, c):
        pl.semaphore_signal(barrier, inc=1, device_id=inner_peer(k), device_id_type=MESH)
        return c

    for side in (up, down):
        pl.semaphore_signal(barrier, inc=1, device_id=(me_m, side), device_id_type=MESH)
    lax.fori_loop(1, group, greet_group, 0)
    lax.fori_loop(1, n_inner, greet_inner, 0)

    wide = 2 * BLOCK
    n_wide = 3 * width // wide
    weight_copies = [
        pltpu.make_async_copy(
            wqkv_hbm.at[:, pl.ds(c * wide, wide)], wqkv.at[:, pl.ds(c * wide, wide)], wsem.at[c]
        )
        for c in range(n_wide)
    ]
    weight_copies.append(pltpu.make_async_copy(wout_hbm, wout, wsem.at[n_wide]))
    for copy in weight_copies:
        copy.start()

    for m in range(members):
        values = states[m].astype(F32)
        centre = jnp.mean(values, axis=-1, keepdims=True)
        centred = values - centre
        spread = jnp.mean(centred * centred, axis=-1, keepdims=True)
        inv = lax.rsqrt(spread + EPS)
        norm = centred * inv
        normed[m] = norm
        inverse[m] = inv
        hall[m, pl.ds(points, points), :] = (norm * gain[...]).astype(BF16)

    pl.semaphore_wait(barrier, 2 + (group - 1) + (n_inner - 1))

    own_rows = hall.at[:, pl.ds(points, points), :]
    halo = [
        pltpu.make_async_remote_copy(
            src_ref=own_rows,
            dst_ref=hall.at[:, pl.ds(start, points), :],
            send_sem=halo_s.at[i],
            recv_sem=halo_r.at[i],
            device_id=(me_m, side),
            device_id_type=MESH,
        )
        for i, (start, side) in enumerate(((0, up), (2 * points, down)))
    ]
    for copy in halo:
        copy.start()

    key_tile = 2 * me_g - 2 + lax.broadcasted_iota(jnp.int32, (window, LANES), 0) // TILE
    lane = lax.broadcasted_iota(jnp.int32, (window, LANES), 1)
    query_tile = lax.rem(lane, points) // TILE
    number = jnp.zeros((window, LANES), F32)
    for t in range(points // TILE):
        for e in range(neighbours.shape[1]):
            hit = (key_tile == neighbours[t, e]) & (query_tile == t)
            number = number + jnp.where(hit, 1.0, 0.0)
    cnt[...] = number
    rows_i = lax.broadcasted_iota(jnp.int32, (PACK * points, cols), 0) // points
    cols_i = lax.broadcasted_iota(jnp.int32, (PACK * points, cols), 1) // (cols // PACK)
    hmask[...] = jnp.where(rows_i == cols_i, 1.0, 0.0)
    wpad[...] = jnp.zeros_like(wpad)
    wpad[:, pl.ds(0, VARS)] = whead[...]
    tpad[...] = jnp.zeros_like(tpad)
    tpad[:, pl.ds(0, VARS)] = targets[...]

    own = hall[:, pl.ds(points, points), :].reshape(flat, width)
    for c in range(width // wide):
        weight_copies[c].wait()
        q = dot(own, wqkv[:, pl.ds(c * wide, wide)], NN).astype(BF16)
        query[:, pl.ds(c * wide, wide)] = q * jnp.asarray((width // HEADS) ** -0.5, BF16)

    for c in range(width // wide, n_wide):
        weight_copies[c].wait()
    weight_copies[n_wide].wait()
    for copy in halo:
        copy.wait_recv()

    def keys_values(c, carry):
        here = pl.ds(pl.multiple_of(c * BLOCK, BLOCK), BLOCK)
        there = pl.ds(pl.multiple_of(width + c * BLOCK, BLOCK), BLOCK)
        rows = hall[...].reshape(members * window, width)
        kv[:, here] = dot(rows, wqkv[:, there], NN).astype(BF16)
        return carry

    lax.fori_loop(0, 2 * width // BLOCK, keys_values, 0)

    def spread_heads(rows):
        return jnp.concatenate([rows] * PACK, axis=0) * hmask[...].astype(BF16)

    def pick_heads(rows):
        rows = rows * hmask[...]
        return jnp.sum(rows.reshape(PACK, points, cols), axis=0)

    def forward(m, carry):
        rows = pl.ds(pl.multiple_of(m * points, points), points)
        keys = pl.ds(pl.multiple_of(m * window, TILE), window)
        number = cnt[...]
        for h in range(packs):
            here = pl.ds(h * cols, cols)
            there = pl.ds(width + h * cols, cols)
            scores = dot(kv[keys, here], spread_heads(query[rows, here]), NT)
            scores = jnp.where(number > 0.0, scores, -3e38)
            top = jnp.max(scores, axis=0, keepdims=True)
            expo = jnp.exp(scores - top)
            prob = expo / jnp.sum(number * expo, axis=0, keepdims=True)
            probs[m, h] = prob
            weight = (number * prob.astype(BF16).astype(F32)).astype(BF16)
            attn[rows, here] = pick_heads(dot(weight, kv[keys, there], TN)).astype(BF16)
        return carry

    lax.fori_loop(0, members, forward, 0)

    flat_states = states[...].reshape(flat, width)
    for c in range(chunks):
        here = pl.ds(c * BLOCK, BLOCK)
        proj = dot(attn[...], wout[:, here], NN)
        mixed[:, here] = (flat_states[:, c * BLOCK : (c + 1) * BLOCK].astype(F32) + proj).astype(BF16)
    ens[0] = dot(mixed[...], wpad[...], NN).astype(BF16)

    def pred_copy(k):
        return pltpu.make_async_remote_copy(
            src_ref=ens.at[0],
            dst_ref=ens.at[k],
            send_sem=pred_s.at[k],
            recv_sem=pred_r.at[k],
            device_id=(lax.rem(me_m + k, n_member), me_g),
            device_id_type=MESH,
        )

    for k in range(1, n_member):
        pred_copy(k).start()
    for k in range(1, n_member):
        pred_copy(k).wait_recv()

    row = lax.broadcasted_iota(jnp.int32, (points, LANES), 0)
    column = lax.broadcasted_iota(jnp.int32, (points, LANES), 1)
    valid = (row < counts[0]) & (column < VARS)

    def crps(i, total):
        rows = pl.ds(pl.multiple_of(i * points, points), points)
        one = ens[0, rows, :].astype(F32)
        pull = jnp.zeros((points, LANES), F32)
        apart = jnp.zeros((points, LANES), F32)
        for k in range(n_member):
            for j in range(members):
                gap = one - ens[k, pl.ds(j * points, points), :].astype(F32)
                square = gap * gap + DELTA * DELTA
                root = lax.rsqrt(square)
                pull = pull + gap * root
                apart = apart + square * root
        miss = one - tpad[...]
        square = miss * miss + DELTA * DELTA
        root = lax.rsqrt(square)
        slope = miss * root - pull * (1.0 / (total_members - 1))
        gradb[rows, :] = jnp.where(valid, slope, 0.0).astype(BF16)
        term = square * root - (apart - DELTA) * (0.5 / (total_members - 1))
        return total + jnp.where(valid, term, 0.0)

    terms = lax.fori_loop(0, members, crps, jnp.zeros((points, LANES), F32))
    loss_part = jnp.sum(jnp.sum(terms, axis=1, keepdims=True), axis=0, keepdims=True)

    def with_loss(value):
        spot = lax.broadcasted_iota(jnp.int32, (1, LANES), 1)
        high = value.astype(BF16).astype(F32)
        return jnp.where(spot == VARS, high, jnp.where(spot == VARS + 1, value - high, 0.0))

    def loss_of(rows):
        spot = lax.broadcasted_iota(jnp.int32, (1, LANES), 1)
        kept = jnp.where((spot == VARS) | (spot == VARS + 1), rows[0:1, :], 0.0)
        return jnp.sum(kept, axis=1, keepdims=True)

    tail = with_loss(loss_part)
    per = BLOCK // piece
    for c in range(chunks):
        here = pl.ds(c * BLOCK, BLOCK)
        part_sum = dot(mixed[:, here], gradb[...], TN) + tail
        if piece <= BLOCK:
            local[pl.ds(c * per, per)] = part_sum.reshape(per, piece, LANES).astype(BF16)

    def part_copy(k):
        m, o = group_peer(k)
        return pltpu.make_async_remote_copy(
            src_ref=local.at[m * n_outer + o],
            dst_ref=part.at[k],
            send_sem=part_s.at[k],
            recv_sem=part_r.at[k],
            device_id=(m, o * n_inner + inner),
            device_id_type=MESH,
        )

    def plane_copy(k):
        return pltpu.make_async_remote_copy(
            src_ref=plane.at[inner],
            dst_ref=plane.at[inner],
            send_sem=plane_s.at[k],
            recv_sem=plane_r.at[k],
            device_id=inner_peer(k),
            device_id_type=MESH,
        )

    def full_copy(k):
        m, o = group_peer(k)
        return pltpu.make_async_remote_copy(
            src_ref=full.at[mine],
            dst_ref=full.at[mine],
            send_sem=full_s.at[k],
            recv_sem=full_r.at[k],
            device_id=(m, o * n_inner + inner),
            device_id_type=MESH,
        )

    def each(count, make, act):
        def step(k, c):
            getattr(make(k), act)()
            return c

        lax.fori_loop(1, count, step, 0)

    each(group, part_copy, "start")

    for c in range(chunks):
        here = pl.ds(c * BLOCK, BLOCK)
        step = dot(gradb[...], wpad[here, :], NT)
        dmixed[:, here] = step
        dmixedb[:, here] = step.astype(BF16)
    for c in range(chunks):
        here = pl.ds(c * BLOCK, BLOCK)
        dattn[:, here] = dot(dmixedb[...], wout[here, :], NT).astype(BF16)

    scale = (width // HEADS) ** -0.5

    def backward(m, carry):
        rows = pl.ds(pl.multiple_of(m * points, points), points)
        keys = pl.ds(pl.multiple_of(m * window, TILE), window)
        number = cnt[...]
        for h in range(packs):
            here = pl.ds(h * cols, cols)
            there = pl.ds(width + h * cols, cols)
            out = spread_heads(dattn[rows, here])
            prob = probs[m, h]
            dprob = dot(kv[keys, there], out, NT)
            lean = jnp.sum(number * dprob * prob, axis=0, keepdims=True)
            dscore = (prob * (dprob - lean)).astype(BF16)
            dscore = (number * dscore.astype(F32)).astype(BF16)
            weight = (number * prob.astype(BF16).astype(F32)).astype(BF16)
            dquery[rows, here] = (pick_heads(dot(dscore, kv[keys, here], TN)) * scale).astype(BF16)
            dkv[keys, here] = dot(dscore, spread_heads(query[rows, here]), NN).astype(BF16)
            dkv[keys, there] = dot(weight, out, NN).astype(BF16)
        return carry

    lax.fori_loop(0, members, backward, 0)

    each(group, part_copy, "wait_recv")
    piece_sum = local[mine].astype(F32)
    for k in range(1, group):
        piece_sum = piece_sum + part[k].astype(F32)
    spare = lax.broadcasted_iota(jnp.int32, (1, LANES), 1) >= VARS
    plane[inner] = jnp.where(spare, with_loss(loss_of(piece_sum)), piece_sum).astype(BF16)
    each(n_inner, plane_copy, "start")

    def back_copy(side, c):
        return pltpu.make_async_remote_copy(
            src_ref=dsend.at[side, c],
            dst_ref=drecv.at[side, c],
            send_sem=back_s.at[side, c],
            recv_sem=back_r.at[side, c],
            device_id=(me_m, down if side == 0 else up),
            device_id_type=MESH,
        )

    for c in range(chunks):
        here = pl.ds(c * BLOCK, BLOCK)
        step = dot(dkv[...], wqkv[here, pl.ds(width, 2 * width)], NT)
        step = step.reshape(members, window, BLOCK)
        for side, start in ((0, 0), (1, 2 * points)):
            dsend[side, c] = step[:, start : start + points].astype(BF16)
            back_copy(side, c).start()
        dhid[:, :, here] = step[:, points : 2 * points]

    each(n_inner, plane_copy, "wait_recv")
    plane_sum = plane[0].astype(F32)
    for k in range(1, n_inner):
        plane_sum = plane_sum + plane[k].astype(F32)
    plane_loss = loss_of(plane_sum)
    plane_sum = plane_sum * (1.0 / (points * n_grid))
    full[mine] = plane_sum.astype(BF16)
    loss[...] = plane_loss * (1.0 / (points * n_grid * VARS * total_members))
    each(group, full_copy, "start")

    for c in range(chunks):
        here = pl.ds(c * BLOCK, BLOCK)
        step = dot(dquery[...], wqkv[here, pl.ds(0, width)], NT)
        dhid[:, :, here] = dhid[:, :, here] + step.reshape(members, points, BLOCK)

    for c in range(chunks):
        here = pl.ds(c * BLOCK, BLOCK)
        for side in range(2):
            back_copy(side, c).wait_recv()
        extra = drecv[0, c].astype(F32) + drecv[1, c].astype(F32)
        dhid[:, :, here] = dhid[:, :, here] + extra

    for m in range(members):
        dnormed = dhid[m] * gain[...]
        norm = normed[m]
        first = jnp.mean(dnormed, axis=-1, keepdims=True)
        second = jnp.mean(dnormed * norm, axis=-1, keepdims=True)
        dstates = inverse[m] * (dnormed - first - norm * second)
        grad[m] = (dstates + dmixed[pl.ds(m * points, points), :]).astype(BF16)

    each(group, full_copy, "wait_recv")
    for k in range(group):
        head_out[pl.ds(k * piece, piece), :] = full[k][:, :VARS].astype(F32)

    for copy in halo:
        copy.wait_send()
    for k in range(1, n_member):
        pred_copy(k).wait_send()
    each(group, part_copy, "wait_send")
    each(n_inner, plane_copy, "wait_send")
    each(group, full_copy, "wait_send")
    for c in range(chunks):
        for side in range(2):
            back_copy(side, c).wait_send()


def body(sizes, states, ln_gain, w_qkv, w_out, w_head, targets, neighbours, counts):
    n_member, n_grid, n_inner = sizes
    members, points, width = states.shape
    flat = members * points
    window = 3 * points
    group = n_member * (n_grid // n_inner)
    chunks = width // BLOCK
    piece = width // group
    cols = PACK * (width // HEADS)
    vmem = pl.BlockSpec(memory_space=pltpu.VMEM)
    smem = pl.BlockSpec(memory_space=pltpu.SMEM)
    hbm = pl.BlockSpec(memory_space=pl.ANY)
    dma = pltpu.SemaphoreType.DMA
    loss, grad, head = pl.pallas_call(
        functools.partial(kernel, sizes),
        out_shape=(
            jax.ShapeDtypeStruct((1, 1), F32),
            jax.ShapeDtypeStruct((members, points, width), BF16),
            jax.ShapeDtypeStruct((width, VARS), F32),
        ),
        in_specs=[vmem, vmem, hbm, hbm, vmem, vmem, smem, smem],
        out_specs=(vmem, vmem, vmem),
        scratch_shapes=[
            pltpu.VMEM((width, 3 * width), BF16),
            pltpu.VMEM((width, width), BF16),
            pltpu.VMEM((width, LANES), BF16),
            pltpu.VMEM((points, LANES), F32),
            pltpu.VMEM((members, window, width), BF16),
            pltpu.VMEM((flat, width), BF16),
            pltpu.VMEM((members * window, 2 * width), BF16),
            pltpu.VMEM((members, points, width), F32),
            pltpu.VMEM((members, points, 1), F32),
            pltpu.VMEM((window, LANES), F32),
            pltpu.VMEM((PACK * points, cols), F32),
            pltpu.VMEM((members, HEADS // PACK, window, PACK * points), F32),
            pltpu.VMEM((flat, width), BF16),
            pltpu.VMEM((flat, width), BF16),
            pltpu.VMEM((n_member, flat, LANES), BF16),
            pltpu.VMEM((flat, LANES), BF16),
            pltpu.VMEM((group, piece, LANES), BF16),
            pltpu.VMEM((group, piece, LANES), BF16),
            pltpu.VMEM((n_inner, piece, LANES), BF16),
            pltpu.VMEM((group, piece, LANES), BF16),
            pltpu.VMEM((flat, width), F32),
            pltpu.VMEM((flat, width), BF16),
            pltpu.VMEM((flat, width), BF16),
            pltpu.VMEM((flat, width), BF16),
            pltpu.VMEM((members * window, 2 * width), BF16),
            pltpu.VMEM((2, chunks, members, points, BLOCK), BF16),
            pltpu.VMEM((2, chunks, members, points, BLOCK), BF16),
            pltpu.VMEM((members, points, width), F32),
            dma((3 * width // (2 * BLOCK) + 1,)),
            dma((2,)),
            dma((2,)),
            dma((n_member,)),
            dma((n_member,)),
            dma((group,)),
            dma((group,)),
            dma((n_inner,)),
            dma((n_inner,)),
            dma((group,)),
            dma((group,)),
            dma((2, chunks)),
            dma((2, chunks)),
        ],
        compiler_params=pltpu.CompilerParams(
            collective_id=0, has_side_effects=True, vmem_limit_bytes=48 * 1024 * 1024
        ),
    )(states, ln_gain.reshape(1, width), w_qkv, w_out, w_head, targets, neighbours, counts)
    return (loss.reshape(()), grad, head)


def solution(mesh):
    placed = (
        P("member", "grid", None),
        P(),
        P(),
        P(),
        P(),
        P("grid", None),
        P("grid", None),
        P("grid"),
    )
    n_member, n_grid = mesh.shape["member"], mesh.shape["grid"]
    sizes = (n_member, n_grid, min(INNER, n_grid // 2))
    return jax.shard_map(
        functools.partial(body, sizes),
        mesh=mesh,
        in_specs=placed,
        out_specs=(P(), P("member", "grid", None), P()),
        check_vma=False,
    )
```

```python
import functools

import jax
import jax.numpy as jnp
from jax import lax
from jax.experimental import pallas as pl
from jax.experimental.pallas import tpu as pltpu
from jax.sharding import PartitionSpec as P

HEADS = 16
VARS = 100
TILE = 16
EPS = 1e-05
DELTA = 0.1
LANES = 128
PACK = 4
VMEM_BYTES = 62 * 1024 * 1024
BLOCK = 256
MESH = pl.DeviceIdType.MESH
F32 = jnp.float32
BF16 = jnp.bfloat16

NN = (((1,), (0,)), ((), ()))
NT = (((1,), (1,)), ((), ()))
TN = (((0,), (0,)), ((), ()))


def dot(a, b, dims):
    return lax.dot_general(a, b, dims, preferred_element_type=F32)


def kernel(
    sizes,
    states_hbm,
    gain_hbm,
    wqkv_hbm,
    wout_hbm,
    whead_hbm,
    targets_hbm,
    neighbours_hbm,
    counts_hbm,
    loss,
    grad,
    head_out,
    states,
    gain,
    wqkv,
    wout,
    whead,
    targets,
    neighbours,
    counts,
    wpad,
    tpad,
    hall,
    query,
    kv,
    normed,
    inverse,
    cnt,
    hmask,
    probs,
    attn,
    mixed,
    ens,
    gradb,
    local,
    part,
    plane,
    full,
    dmixed,
    dmixedb,
    dattn,
    dquery,
    dkv,
    dsend,
    drecv,
    dhid,
    insem,
    wsem,
    halo_s,
    halo_r,
    pred_s,
    pred_r,
    part_s,
    part_r,
    plane_s,
    plane_r,
    full_s,
    full_r,
    back_s,
    back_r,
):
    n_member, n_y, n_z, n_core = sizes
    n_grid = n_y * n_z * n_core
    group = n_member * n_y * n_core
    members, points, width = states.shape
    window = hall.shape[1]
    flat = members * points
    cols = PACK * (width // HEADS)
    chunks = width // BLOCK
    packs = HEADS // PACK
    total_members = members * n_member
    per = local.shape[1]
    bands = width // LANES

    me_m = lax.axis_index("member")
    me_g = lax.axis_index("grid")
    core = lax.rem(me_g, n_core)
    me_z = lax.rem(me_g // n_core, n_z)
    me_y = me_g // (n_core * n_z)
    up = lax.rem(me_g + 1, n_grid)
    down = lax.rem(me_g + n_grid - 1, n_grid)
    mine = (me_m * n_y + me_y) * n_core + core

    def grid_at(y, z, c):
        return (y * n_z + z) * n_core + c

    def group_peer(k):
        m = lax.rem(me_m + k // (n_y * n_core), n_member)
        y = lax.rem(me_y + lax.rem(k // n_core, n_y), n_y)
        c = lax.rem(core + lax.rem(k, n_core), n_core)
        return (m, grid_at(y, me_z, c)), (m * n_y + y) * n_core + c

    def plane_peer(k):
        return (me_m, grid_at(me_y, lax.rem(me_z + k, n_z), core))

    barrier = pltpu.get_barrier_semaphore()

    def greet(device):
        pl.semaphore_signal(barrier, inc=1, device_id=device, device_id_type=MESH)

    def greet_group(k, c):
        greet(group_peer(k)[0])
        return c

    def greet_plane(k, c):
        greet(plane_peer(k))
        return c

    greet((me_m, up))
    greet((me_m, down))
    lax.fori_loop(1, n_z, greet_plane, 0)
    lax.fori_loop(1, group, greet_group, 0)

    wide = 2 * BLOCK
    n_wide = 3 * width // wide
    small_copies = [
        pltpu.make_async_copy(source, target, insem.at[i])
        for i, (source, target) in enumerate(
            (
                (states_hbm, states),
                (gain_hbm, gain),
                (neighbours_hbm, neighbours),
                (counts_hbm, counts),
                (whead_hbm, whead),
                (targets_hbm, targets),
            )
        )
    ]
    weight_copies = [
        pltpu.make_async_copy(
            wqkv_hbm.at[:, pl.ds(c * wide, wide)], wqkv.at[:, pl.ds(c * wide, wide)], wsem.at[c]
        )
        for c in range(n_wide)
    ]
    weight_copies.append(pltpu.make_async_copy(wout_hbm, wout, wsem.at[n_wide]))
    for copy in small_copies + weight_copies:
        copy.start()
    small_copies[0].wait()
    small_copies[1].wait()

    for m in range(members):
        values = states[m].astype(F32)
        centre = jnp.mean(values, axis=-1, keepdims=True)
        centred = values - centre
        spread = jnp.mean(centred * centred, axis=-1, keepdims=True)
        inv = lax.rsqrt(spread + EPS)
        norm = centred * inv
        normed[m] = norm
        inverse[m] = inv
        hall[m, pl.ds(points, points), :] = (norm * gain[...]).astype(BF16)

    pl.semaphore_wait(barrier, 2 + (group - 1) + (n_z - 1))

    own_rows = hall.at[:, pl.ds(points, points), :]
    halo = [
        pltpu.make_async_remote_copy(
            src_ref=own_rows,
            dst_ref=hall.at[:, pl.ds(start, points), :],
            send_sem=halo_s.at[i],
            recv_sem=halo_r.at[i],
            device_id=(me_m, side),
            device_id_type=MESH,
        )
        for i, (start, side) in enumerate(((0, up), (2 * points, down)))
    ]
    for copy in halo:
        copy.start()

    for copy in small_copies[2:]:
        copy.wait()

    key_tile = 2 * me_g - 2 + lax.broadcasted_iota(jnp.int32, (window, LANES), 0) // TILE
    lane = lax.broadcasted_iota(jnp.int32, (window, LANES), 1)
    query_tile = lax.rem(lane, points) // TILE
    number = jnp.zeros((window, LANES), F32)
    for t in range(points // TILE):
        for e in range(neighbours.shape[1]):
            hit = (key_tile == neighbours[t, e]) & (query_tile == t)
            number = number + jnp.where(hit, 1.0, 0.0)
    cnt[...] = number
    rows_i = lax.broadcasted_iota(jnp.int32, (PACK * points, cols), 0) // points
    cols_i = lax.broadcasted_iota(jnp.int32, (PACK * points, cols), 1) // (cols // PACK)
    hmask[...] = jnp.where(rows_i == cols_i, 1.0, 0.0)
    wpad[...] = jnp.zeros_like(wpad)
    wpad[pl.ds(0, VARS), :] = whead[...]
    tpad[...] = jnp.zeros_like(tpad)
    tpad[:, pl.ds(0, VARS)] = targets[...]

    own = hall[:, pl.ds(points, points), :].reshape(flat, width)
    for c in range(n_wide):
        weight_copies[c].wait()
        step = dot(own, wqkv[:, pl.ds(c * wide, wide)], NN).astype(BF16)
        if c * wide < width:
            query[:, pl.ds(c * wide, wide)] = step * jnp.asarray((width // HEADS) ** -0.5, BF16)
        else:
            there = pl.ds(c * wide - width, wide)
            kv[:, pl.ds(points, points), there] = step.reshape(members, points, wide)

    for copy in halo:
        copy.wait_recv()

    def keys_values(c, carry):
        here = pl.ds(pl.multiple_of(c * BLOCK, BLOCK), BLOCK)
        there = pl.ds(pl.multiple_of(width + c * BLOCK, BLOCK), BLOCK)
        rows = jnp.concatenate(
            [hall[:, pl.ds(0, points), :], hall[:, pl.ds(2 * points, points), :]], axis=0
        )
        step = dot(rows.reshape(2 * flat, width), wqkv[:, there], NN).astype(BF16)
        step = step.reshape(2, members, points, BLOCK)
        kv[:, pl.ds(0, points), here] = step[0]
        kv[:, pl.ds(2 * points, points), here] = step[1]
        return carry

    lax.fori_loop(0, 2 * width // BLOCK, keys_values, 0)

    def spread_heads(rows):
        return jnp.concatenate([rows] * PACK, axis=0) * hmask[...].astype(BF16)

    def pick_heads(rows):
        rows = rows * hmask[...]
        return jnp.sum(rows.reshape(PACK, points, cols), axis=0)

    pack_range = range(packs)
    heres = [pl.ds(h * cols, cols) for h in pack_range]
    theres = [pl.ds(width + h * cols, cols) for h in pack_range]

    def forward(m, carry):
        rows = pl.ds(pl.multiple_of(m * points, points), points)
        number = cnt[...]
        scores = [dot(kv[m, :, here], spread_heads(query[rows, here]), NT) for here in heres]
        scores = [jnp.where(number > 0.0, one, -3e38) for one in scores]
        tops = [jnp.max(one, axis=0, keepdims=True) for one in scores]
        expos = [jnp.exp(one - top) for one, top in zip(scores, tops)]
        totals = [jnp.sum(number * expo, axis=0, keepdims=True) for expo in expos]
        shares = [expo / total for expo, total in zip(expos, totals)]
        weights = [(number * one.astype(BF16).astype(F32)).astype(BF16) for one in shares]
        outs = [dot(one, kv[m, :, there], TN) for one, there in zip(weights, theres)]
        for h in pack_range:
            probs[m, h] = shares[h]
            attn[rows, heres[h]] = pick_heads(outs[h]).astype(BF16)
        return carry

    lax.fori_loop(0, members, forward, 0)
    weight_copies[n_wide].wait()

    flat_states = states[...].reshape(flat, width)
    for c in range(chunks):
        here = pl.ds(c * BLOCK, BLOCK)
        proj = dot(attn[...], wout[:, here], NN)
        mixed[:, here] = (flat_states[:, c * BLOCK : (c + 1) * BLOCK].astype(F32) + proj).astype(BF16)
    ens[0] = dot(mixed[...], wpad[...], NT).astype(BF16)

    def pred_copy(k):
        return pltpu.make_async_remote_copy(
            src_ref=ens.at[0],
            dst_ref=ens.at[k],
            send_sem=pred_s.at[k],
            recv_sem=pred_r.at[k],
            device_id=(lax.rem(me_m + k, n_member), me_g),
            device_id_type=MESH,
        )

    for k in range(1, n_member):
        pred_copy(k).start()

    row = lax.broadcasted_iota(jnp.int32, (points, LANES), 0)
    column = lax.broadcasted_iota(jnp.int32, (points, LANES), 1)
    valid = (row < counts[0]) & (column < VARS)

    def pair_sums(k, carry):
        def add(j, sums):
            other = ens[k, pl.ds(pl.multiple_of(j * points, points), points), :].astype(F32)
            pulls, apart = sums
            new = []
            for i in range(members):
                gap = ens[0, pl.ds(i * points, points), :].astype(F32) - other
                square = gap * gap + DELTA * DELTA
                root = lax.rsqrt(square)
                new.append(pulls[i] + gap * root)
                apart = apart + square * root
            return (tuple(new), apart)

        return lax.fori_loop(0, members, add, carry)

    blank = jnp.zeros((points, LANES), F32)
    sums = pair_sums(0, ((blank,) * members, blank))
    for k in sorted(range(1, n_member), key=lambda k: min(k, n_member - k)):
        pred_copy(k).wait_recv()
        sums = pair_sums(k, sums)
    pulls, apart = sums
    terms = (members * DELTA - apart) * (0.5 / (total_members - 1))
    for i in range(members):
        rows = pl.ds(i * points, points)
        miss = ens[0, rows, :].astype(F32) - tpad[...]
        square = miss * miss + DELTA * DELTA
        root = lax.rsqrt(square)
        slope = miss * root - pulls[i] * (1.0 / (total_members - 1))
        gradb[rows, :] = jnp.where(valid, slope, 0.0).astype(BF16)
        terms = terms + square * root
    terms = jnp.where(valid, terms, 0.0)
    loss_part = jnp.sum(jnp.sum(terms, axis=1, keepdims=True), axis=0, keepdims=True)

    tile_row = lax.broadcasted_iota(jnp.int32, (per, 32, LANES), 1)
    tile_at = mine * per + lax.broadcasted_iota(jnp.int32, (per, 32, LANES), 0)
    variable = (tile_at // bands) * 32 + tile_row
    spot = VARS % 32

    def split_loss(tiles):
        value = tiles[:, spot : spot + 1, :] + tiles[:, spot + 1 : spot + 2, :]
        high = value.astype(BF16).astype(F32)
        return jnp.where(
            variable == VARS, high, jnp.where(variable == VARS + 1, value - high, tiles)
        )

    row_all = lax.broadcasted_iota(jnp.int32, (LANES, 1), 0)
    loss_high = loss_part.astype(BF16).astype(F32)
    tail = jnp.where(
        row_all == VARS, loss_high, jnp.where(row_all == VARS + 1, loss_part - loss_high, 0.0)
    )
    for b in range(bands):
        band = dot(gradb[...], mixed[:, pl.ds(b * LANES, LANES)], TN) + tail
        for r in range(LANES // 32):
            t = r * bands + b
            local[t // per, t % per] = band[r * 32 : (r + 1) * 32].astype(BF16)

    def part_copy(k):
        device, owner = group_peer(k)
        return pltpu.make_async_remote_copy(
            src_ref=local.at[owner],
            dst_ref=part.at[k],
            send_sem=part_s.at[k],
            recv_sem=part_r.at[k],
            device_id=device,
            device_id_type=MESH,
        )

    def plane_copy(k):
        return pltpu.make_async_remote_copy(
            src_ref=plane.at[me_z],
            dst_ref=plane.at[me_z],
            send_sem=plane_s.at[k],
            recv_sem=plane_r.at[k],
            device_id=plane_peer(k),
            device_id_type=MESH,
        )

    def full_copy(k):
        return pltpu.make_async_remote_copy(
            src_ref=full.at[mine],
            dst_ref=full.at[mine],
            send_sem=full_s.at[k],
            recv_sem=full_r.at[k],
            device_id=group_peer(k)[0],
            device_id_type=MESH,
        )

    def each(count, make, act):
        def step(k, c):
            getattr(make(k), act)()
            return c

        lax.fori_loop(1, count, step, 0)

    each(group, part_copy, "start")

    for c in range(chunks):
        here = pl.ds(c * BLOCK, BLOCK)
        step = dot(gradb[...], wpad[:, here], NN)
        dmixed[:, here] = step
        dmixedb[:, here] = step.astype(BF16)
    for c in range(chunks):
        here = pl.ds(c * BLOCK, BLOCK)
        dattn[:, here] = dot(dmixedb[...], wout[here, :], NT).astype(BF16)

    scale = (width // HEADS) ** -0.5

    def backward(m, carry):
        rows = pl.ds(pl.multiple_of(m * points, points), points)
        number = cnt[...]
        outs = [spread_heads(dattn[rows, here]) for here in heres]
        dprobs = [dot(kv[m, :, there], out, NT) for there, out in zip(theres, outs)]
        shares = [probs[m, h] for h in pack_range]
        leans = [
            jnp.sum(number * one * share, axis=0, keepdims=True)
            for one, share in zip(dprobs, shares)
        ]
        dscores = [
            (share * (one - lean)).astype(BF16) for share, one, lean in zip(shares, dprobs, leans)
        ]
        dscores = [(number * one.astype(F32)).astype(BF16) for one in dscores]
        weights = [(number * one.astype(BF16).astype(F32)).astype(BF16) for one in shares]
        dqs = [dot(one, kv[m, :, here], TN) for one, here in zip(dscores, heres)]
        dks = [
            dot(one, spread_heads(query[rows, here]), NN) for one, here in zip(dscores, heres)
        ]
        dvs = [dot(one, out, NN) for one, out in zip(weights, outs)]
        for h in pack_range:
            dquery[rows, heres[h]] = (pick_heads(dqs[h]) * scale).astype(BF16)
            dkv[m, :, heres[h]] = dks[h].astype(BF16)
            dkv[m, :, theres[h]] = dvs[h].astype(BF16)
        return carry

    lax.fori_loop(0, members, backward, 0)

    def back_copy(side, c):
        return pltpu.make_async_remote_copy(
            src_ref=dsend.at[side, c],
            dst_ref=drecv.at[side, c],
            send_sem=back_s.at[side, c],
            recv_sem=back_r.at[side, c],
            device_id=(me_m, down if side == 0 else up),
            device_id_type=MESH,
        )

    for c in range(chunks):
        here = pl.ds(c * BLOCK, BLOCK)
        step = dot(dkv[...].reshape(members * window, 2 * width), wqkv[here, pl.ds(width, 2 * width)], NT)
        step = step.reshape(members, window, BLOCK)
        for side, start in ((0, 0), (1, 2 * points)):
            dsend[side, c] = step[:, start : start + points].astype(BF16)
            back_copy(side, c).start()
        dhid[:, :, here] = step[:, points : 2 * points]

    each(group, part_copy, "wait_recv")
    piece_sum = local[mine].astype(F32)
    for k in range(1, group):
        piece_sum = piece_sum + part[k].astype(F32)
    plane[me_z] = split_loss(piece_sum).astype(BF16)
    each(n_z, plane_copy, "start")

    for c in range(chunks):
        here = pl.ds(c * BLOCK, BLOCK)
        step = dot(dquery[...], wqkv[here, pl.ds(0, width)], NT)
        dhid[:, :, here] = dhid[:, :, here] + step.reshape(members, points, BLOCK)

    for c in range(chunks):
        here = pl.ds(c * BLOCK, BLOCK)
        for side in range(2):
            back_copy(side, c).wait_recv()
        extra = drecv[0, c].astype(F32) + drecv[1, c].astype(F32)
        dhid[:, :, here] = dhid[:, :, here] + extra

    for m in range(members):
        dnormed = dhid[m] * gain[...]
        norm = normed[m]
        first = jnp.mean(dnormed, axis=-1, keepdims=True)
        second = jnp.mean(dnormed * norm, axis=-1, keepdims=True)
        dstates = inverse[m] * (dnormed - first - norm * second)
        grad[m] = (dstates + dmixed[pl.ds(m * points, points), :]).astype(BF16)

    each(n_z, plane_copy, "wait_recv")
    plane_sum = plane[0].astype(F32)
    for k in range(1, n_z):
        plane_sum = plane_sum + plane[k].astype(F32)
    full[mine] = (split_loss(plane_sum) * (1.0 / (points * n_grid))).astype(BF16)
    each(group, full_copy, "start")
    each(group, full_copy, "wait_recv")
    for t in range(bands * LANES // 32):
        r, b = t // bands, t % bands
        count = min(32, VARS - 32 * r)
        here = (pl.ds(32 * r, count), pl.ds(b * LANES, LANES))
        head_out[here] = full[t // per, t % per][:count].astype(F32)
    t = (VARS // 32) * bands
    sums = full[t // per, t % per].astype(F32)
    total = sums[spot : spot + 1, 0:1] + sums[spot + 1 : spot + 2, 0:1]
    loss[...] = total * (1.0 / (VARS * total_members))

    for copy in halo:
        copy.wait_send()
    for k in range(1, n_member):
        pred_copy(k).wait_send()
    each(group, part_copy, "wait_send")
    each(n_z, plane_copy, "wait_send")
    each(group, full_copy, "wait_send")
    for c in range(chunks):
        for side in range(2):
            back_copy(side, c).wait_send()


def body(sizes, states, ln_gain, w_qkv, w_out, w_head, targets, neighbours, counts):
    n_member, n_y, n_z, n_core = sizes
    members, points, width = states.shape
    flat = members * points
    window = 3 * points
    group = n_member * n_y * n_core
    chunks = width // BLOCK
    cols = PACK * (width // HEADS)
    tiles = (LANES // 32) * (width // LANES)
    per = tiles // group
    vmem = pl.BlockSpec(memory_space=pltpu.VMEM)
    hbm = pl.BlockSpec(memory_space=pl.ANY)
    dma = pltpu.SemaphoreType.DMA
    loss, grad, head = pl.pallas_call(
        functools.partial(kernel, sizes),
        out_shape=(
            jax.ShapeDtypeStruct((1, 1), F32),
            jax.ShapeDtypeStruct((members, points, width), BF16),
            jax.ShapeDtypeStruct((VARS, width), F32),
        ),
        in_specs=[hbm] * 8,
        out_specs=(vmem, vmem, vmem),
        scratch_shapes=[
            pltpu.VMEM((members, points, width), BF16),
            pltpu.VMEM((1, width), F32),
            pltpu.VMEM((width, 3 * width), BF16),
            pltpu.VMEM((width, width), BF16),
            pltpu.VMEM((VARS, width), BF16),
            pltpu.VMEM((points, VARS), F32),
            pltpu.SMEM(neighbours.shape, jnp.int32),
            pltpu.SMEM((1,), jnp.int32),
            pltpu.VMEM((LANES, width), BF16),
            pltpu.VMEM((points, LANES), F32),
            pltpu.VMEM((members, window, width), BF16),
            pltpu.VMEM((flat, width), BF16),
            pltpu.VMEM((members, window, 2 * width), BF16),
            pltpu.VMEM((members, points, width), F32),
            pltpu.VMEM((members, points, 1), F32),
            pltpu.VMEM((window, LANES), F32),
            pltpu.VMEM((PACK * points, cols), F32),
            pltpu.VMEM((members, HEADS // PACK, window, PACK * points), F32),
            pltpu.VMEM((flat, width), BF16),
            pltpu.VMEM((flat, width), BF16),
            pltpu.VMEM((n_member, flat, LANES), BF16),
            pltpu.VMEM((flat, LANES), BF16),
            pltpu.VMEM((group, per, 32, LANES), BF16),
            pltpu.VMEM((group, per, 32, LANES), BF16),
            pltpu.VMEM((n_z, per, 32, LANES), BF16),
            pltpu.VMEM((group, per, 32, LANES), BF16),
            pltpu.VMEM((flat, width), F32),
            pltpu.VMEM((flat, width), BF16),
            pltpu.VMEM((flat, width), BF16),
            pltpu.VMEM((flat, width), BF16),
            pltpu.VMEM((members, window, 2 * width), BF16),
            pltpu.VMEM((2, chunks, members, points, BLOCK), BF16),
            pltpu.VMEM((2, chunks, members, points, BLOCK), BF16),
            pltpu.VMEM((members, points, width), F32),
            dma((6,)),
            dma((3 * width // (2 * BLOCK) + 1,)),
            dma((2,)),
            dma((2,)),
            dma((n_member,)),
            dma((n_member,)),
            dma((group,)),
            dma((group,)),
            dma((n_z,)),
            dma((n_z,)),
            dma((group,)),
            dma((group,)),
            dma((2, chunks)),
            dma((2, chunks)),
        ],
        compiler_params=pltpu.CompilerParams(
            collective_id=0, has_side_effects=True, vmem_limit_bytes=VMEM_BYTES
        ),
    )(states, ln_gain.reshape(1, width), w_qkv, w_out, w_head.T, targets, neighbours, counts)
    return (loss.reshape(()), grad, head.T)


def solution(mesh):
    placed = (
        P("member", "grid", None),
        P(),
        P(),
        P(),
        P(),
        P("grid", None),
        P("grid", None),
        P("grid"),
    )
    n_core = 2
    n_z = min(8, mesh.shape["grid"] // n_core)
    sizes = (mesh.shape["member"], mesh.shape["grid"] // (n_z * n_core), n_z, n_core)
    return jax.shard_map(
        functools.partial(body, sizes),
        mesh=mesh,
        in_specs=placed,
        out_specs=(P(), P("member", "grid", None), P()),
        check_vma=False,
    )
```

```python
import functools

import jax
import jax.numpy as jnp
from jax import lax
from jax.experimental import pallas as pl
from jax.experimental.pallas import tpu as pltpu
from jax.sharding import PartitionSpec as P

HEADS = 16
VARS = 100
TILE = 16
EPS = 1e-05
DELTA = 0.1
LANES = 128
PACK = 4
VMEM_BYTES = 40 * 1024 * 1024
BLOCK = 256
MESH = pl.DeviceIdType.MESH
F32 = jnp.float32
BF16 = jnp.bfloat16

NN = (((1,), (0,)), ((), ()))
NT = (((1,), (1,)), ((), ()))
TN = (((0,), (0,)), ((), ()))


def dot(a, b, dims):
    return lax.dot_general(a, b, dims, preferred_element_type=F32)


def kernel(
    sizes,
    states_hbm,
    gain_hbm,
    wqkv_hbm,
    wout_hbm,
    whead_hbm,
    targets_hbm,
    neighbours_hbm,
    counts_hbm,
    loss,
    grad,
    head_out,
    states,
    gain,
    wqkv,
    wout,
    whead,
    targets,
    neighbours,
    counts,
    wpad,
    tpad,
    hidden,
    beside,
    query,
    kv,
    normed,
    inverse,
    cnt,
    hmask,
    probs,
    attn,
    mixed,
    ens,
    gradb,
    local,
    part,
    plane,
    full,
    dmixed,
    dmixedb,
    dattn,
    dquery,
    dkv,
    dsend,
    drecv,
    dhid,
    insem,
    wsem,
    halo_s,
    halo_r,
    pred_s,
    pred_r,
    part_s,
    part_r,
    plane_s,
    plane_r,
    full_s,
    full_r,
    back_s,
    back_r,
):
    n_member, n_y, n_z, n_core = sizes
    n_grid = n_y * n_z * n_core
    group = n_member * n_y * n_core
    members, points, width = states.shape
    window = kv.shape[1]
    flat = members * points
    cols = PACK * (width // HEADS)
    chunks = width // BLOCK
    packs = HEADS // PACK
    total_members = members * n_member
    per = local.shape[1]
    bands = width // LANES

    me_m = lax.axis_index("member")
    me_g = lax.axis_index("grid")
    core = lax.rem(me_g, n_core)
    me_z = lax.rem(me_g // n_core, n_z)
    me_y = me_g // (n_core * n_z)
    up = lax.rem(me_g + 1, n_grid)
    down = lax.rem(me_g + n_grid - 1, n_grid)
    mine = (me_m * n_y + me_y) * n_core + core

    def grid_at(y, z, c):
        return (y * n_z + z) * n_core + c

    def group_peer(k):
        m = lax.rem(me_m + k // (n_y * n_core), n_member)
        y = lax.rem(me_y + lax.rem(k // n_core, n_y), n_y)
        c = lax.rem(core + lax.rem(k, n_core), n_core)
        return (m, grid_at(y, me_z, c)), (m * n_y + y) * n_core + c

    def plane_peer(k):
        return (me_m, grid_at(me_y, lax.rem(me_z + k, n_z), core))

    barrier = pltpu.get_barrier_semaphore()

    def greet(device):
        pl.semaphore_signal(barrier, inc=1, device_id=device, device_id_type=MESH)

    def greet_group(k, c):
        greet(group_peer(k)[0])
        return c

    def greet_plane(k, c):
        greet(plane_peer(k))
        return c

    greet((me_m, up))
    greet((me_m, down))
    lax.fori_loop(1, n_z, greet_plane, 0)
    lax.fori_loop(1, group, greet_group, 0)

    wide = 2 * BLOCK
    n_wide = 3 * width // wide
    small_copies = [
        pltpu.make_async_copy(source, target, insem.at[i])
        for i, (source, target) in enumerate(
            (
                (states_hbm, states),
                (gain_hbm, gain),
                (neighbours_hbm, neighbours),
                (counts_hbm, counts),
                (whead_hbm, whead),
                (targets_hbm, targets),
            )
        )
    ]
    weight_copies = [
        pltpu.make_async_copy(
            wqkv_hbm.at[:, pl.ds(c * wide, wide)], wqkv.at[:, pl.ds(c * wide, wide)], wsem.at[c]
        )
        for c in range(n_wide)
    ]
    weight_copies.append(pltpu.make_async_copy(wout_hbm, wout, wsem.at[n_wide]))
    for copy in small_copies + weight_copies:
        copy.start()
    small_copies[0].wait()
    small_copies[1].wait()

    for m in range(members):
        values = states[m].astype(F32)
        centre = jnp.mean(values, axis=-1, keepdims=True)
        centred = values - centre
        spread = jnp.mean(centred * centred, axis=-1, keepdims=True)
        inv = lax.rsqrt(spread + EPS)
        norm = centred * inv
        normed[m] = norm
        inverse[m] = inv
        hidden[pl.ds(m * points, points), :] = (norm * gain[...]).astype(BF16)

    pl.semaphore_wait(barrier, 2 + (group - 1) + (n_z - 1))

    halo = [
        pltpu.make_async_remote_copy(
            src_ref=hidden,
            dst_ref=beside.at[i],
            send_sem=halo_s.at[i],
            recv_sem=halo_r.at[i],
            device_id=(me_m, side),
            device_id_type=MESH,
        )
        for i, side in enumerate((up, down))
    ]
    for copy in halo:
        copy.start()

    for copy in small_copies[2:]:
        copy.wait()

    key_tile = 2 * me_g - 2 + lax.broadcasted_iota(jnp.int32, (window, LANES), 0) // TILE
    lane = lax.broadcasted_iota(jnp.int32, (window, LANES), 1)
    query_tile = lax.rem(lane, points) // TILE
    number = jnp.zeros((window, LANES), F32)
    for t in range(points // TILE):
        for e in range(neighbours.shape[1]):
            hit = (key_tile == neighbours[t, e]) & (query_tile == t)
            number = number + jnp.where(hit, 1.0, 0.0)
    cnt[...] = number
    rows_i = lax.broadcasted_iota(jnp.int32, (PACK * points, cols), 0) // points
    cols_i = lax.broadcasted_iota(jnp.int32, (PACK * points, cols), 1) // (cols // PACK)
    hmask[...] = jnp.where(rows_i == cols_i, 1.0, 0.0)
    wpad[...] = jnp.zeros_like(wpad)
    wpad[pl.ds(0, VARS), :] = whead[...]
    tpad[...] = jnp.zeros_like(tpad)
    tpad[:, pl.ds(0, VARS)] = targets[...]

    for c in range(n_wide):
        weight_copies[c].wait()
        step = dot(hidden[...], wqkv[:, pl.ds(c * wide, wide)], NN).astype(BF16)
        if c * wide < width:
            query[:, pl.ds(c * wide, wide)] = step * jnp.asarray((width // HEADS) ** -0.5, BF16)
        else:
            there = pl.ds(c * wide - width, wide)
            kv[:, pl.ds(points, points), there] = step.reshape(members, points, wide)

    for copy in halo:
        copy.wait_recv()

    for c in range(2 * width // wide):
        here = pl.ds(c * wide, wide)
        step = dot(beside[...].reshape(2 * flat, width), wqkv[:, pl.ds(width + c * wide, wide)], NN)
        step = step.astype(BF16).reshape(2, members, points, wide)
        kv[:, pl.ds(0, points), here] = step[0]
        kv[:, pl.ds(2 * points, points), here] = step[1]

    def spread_heads(rows):
        return jnp.concatenate([rows] * PACK, axis=0) * hmask[...].astype(BF16)

    def pick_heads(rows):
        rows = rows * hmask[...]
        return jnp.sum(rows.reshape(PACK, points, cols), axis=0)

    pack_range = range(packs)
    heres = [pl.ds(h * cols, cols) for h in pack_range]
    theres = [pl.ds(width + h * cols, cols) for h in pack_range]

    def forward(m, carry):
        rows = pl.ds(pl.multiple_of(m * points, points), points)
        number = cnt[...]
        scores = [dot(kv[m, :, here], spread_heads(query[rows, here]), NT) for here in heres]
        scores = [jnp.where(number > 0.0, one, -3e38) for one in scores]
        tops = [jnp.max(one, axis=0, keepdims=True) for one in scores]
        expos = [jnp.exp(one - top) for one, top in zip(scores, tops)]
        totals = [jnp.sum(number * expo, axis=0, keepdims=True) for expo in expos]
        shares = [expo / total for expo, total in zip(expos, totals)]
        weights = [(number * one.astype(BF16).astype(F32)).astype(BF16) for one in shares]
        outs = [dot(one, kv[m, :, there], TN) for one, there in zip(weights, theres)]
        for h in pack_range:
            probs[m, h] = shares[h]
            attn[rows, heres[h]] = pick_heads(outs[h]).astype(BF16)
        return carry

    lax.fori_loop(0, members, forward, 0)
    weight_copies[n_wide].wait()

    flat_states = states[...].reshape(flat, width)
    for c in range(chunks):
        here = pl.ds(c * BLOCK, BLOCK)
        proj = dot(attn[...], wout[:, here], NN)
        mixed[:, here] = (flat_states[:, c * BLOCK : (c + 1) * BLOCK].astype(F32) + proj).astype(BF16)
    ens[0] = dot(mixed[...], wpad[...], NT).astype(BF16)

    def pred_copy(k):
        return pltpu.make_async_remote_copy(
            src_ref=ens.at[0],
            dst_ref=ens.at[k],
            send_sem=pred_s.at[k],
            recv_sem=pred_r.at[k],
            device_id=(lax.rem(me_m + k, n_member), me_g),
            device_id_type=MESH,
        )

    for k in range(1, n_member):
        pred_copy(k).start()

    row = lax.broadcasted_iota(jnp.int32, (points, LANES), 0)
    column = lax.broadcasted_iota(jnp.int32, (points, LANES), 1)
    valid = (row < counts[0]) & (column < VARS)

    def pair_sums(k, carry):
        def add(j, sums):
            other = ens[k, pl.ds(pl.multiple_of(j * points, points), points), :].astype(F32)
            pulls, apart = sums
            new = []
            for i in range(members):
                gap = ens[0, pl.ds(i * points, points), :].astype(F32) - other
                square = gap * gap + DELTA * DELTA
                root = lax.rsqrt(square)
                new.append(pulls[i] + gap * root)
                apart = apart + square * root
            return (tuple(new), apart)

        return lax.fori_loop(0, members, add, carry)

    blank = jnp.zeros((points, LANES), F32)
    sums = pair_sums(0, ((blank,) * members, blank))
    for k in sorted(range(1, n_member), key=lambda k: min(k, n_member - k)):
        pred_copy(k).wait_recv()
        sums = pair_sums(k, sums)
    pulls, apart = sums
    terms = (members * DELTA - apart) * (0.5 / (total_members - 1))
    for i in range(members):
        rows = pl.ds(i * points, points)
        miss = ens[0, rows, :].astype(F32) - tpad[...]
        square = miss * miss + DELTA * DELTA
        root = lax.rsqrt(square)
        slope = miss * root - pulls[i] * (1.0 / (total_members - 1))
        gradb[rows, :] = jnp.where(valid, slope, 0.0).astype(BF16)
        terms = terms + square * root
    terms = jnp.where(valid, terms, 0.0)
    loss_part = jnp.sum(jnp.sum(terms, axis=1, keepdims=True), axis=0, keepdims=True)

    tile_row = lax.broadcasted_iota(jnp.int32, (per, 32, LANES), 1)
    tile_at = mine * per + lax.broadcasted_iota(jnp.int32, (per, 32, LANES), 0)
    variable = (tile_at // bands) * 32 + tile_row
    spot = VARS % 32

    def split_loss(tiles):
        value = tiles[:, spot : spot + 1, :] + tiles[:, spot + 1 : spot + 2, :]
        high = value.astype(BF16).astype(F32)
        return jnp.where(
            variable == VARS, high, jnp.where(variable == VARS + 1, value - high, tiles)
        )

    row_all = lax.broadcasted_iota(jnp.int32, (LANES, 1), 0)
    loss_high = loss_part.astype(BF16).astype(F32)
    tail = jnp.where(
        row_all == VARS, loss_high, jnp.where(row_all == VARS + 1, loss_part - loss_high, 0.0)
    )
    for b in range(bands):
        band = dot(gradb[...], mixed[:, pl.ds(b * LANES, LANES)], TN) + tail
        for r in range(LANES // 32):
            t = r * bands + b
            local[t // per, t % per] = band[r * 32 : (r + 1) * 32].astype(BF16)

    def part_copy(k):
        device, owner = group_peer(k)
        return pltpu.make_async_remote_copy(
            src_ref=local.at[owner],
            dst_ref=part.at[k],
            send_sem=part_s.at[k],
            recv_sem=part_r.at[k],
            device_id=device,
            device_id_type=MESH,
        )

    def plane_copy(k):
        return pltpu.make_async_remote_copy(
            src_ref=plane.at[me_z],
            dst_ref=plane.at[me_z],
            send_sem=plane_s.at[k],
            recv_sem=plane_r.at[k],
            device_id=plane_peer(k),
            device_id_type=MESH,
        )

    def full_copy(k):
        return pltpu.make_async_remote_copy(
            src_ref=full.at[mine],
            dst_ref=full.at[mine],
            send_sem=full_s.at[k],
            recv_sem=full_r.at[k],
            device_id=group_peer(k)[0],
            device_id_type=MESH,
        )

    def apart_by(k):
        m, y = k // (n_y * n_core), k // n_core % n_y
        return min(m, n_member - m) + min(y, n_y - y)

    far_first = sorted(range(1, group), key=lambda k: -apart_by(k))

    def each(count, make, act):
        def step(k, c):
            getattr(make(k), act)()
            return c

        lax.fori_loop(1, count, step, 0)

    for k in far_first:
        part_copy(k).start()

    for c in range(chunks):
        here = pl.ds(c * BLOCK, BLOCK)
        step = dot(gradb[...], wpad[:, here], NN)
        dmixed[:, here] = step
        dmixedb[:, here] = step.astype(BF16)
    for c in range(chunks):
        here = pl.ds(c * BLOCK, BLOCK)
        dattn[:, here] = dot(dmixedb[...], wout[here, :], NT).astype(BF16)

    scale = (width // HEADS) ** -0.5

    def backward(m, carry):
        rows = pl.ds(pl.multiple_of(m * points, points), points)
        number = cnt[...]
        outs = [spread_heads(dattn[rows, here]) for here in heres]
        dprobs = [dot(kv[m, :, there], out, NT) for there, out in zip(theres, outs)]
        shares = [probs[m, h] for h in pack_range]
        leans = [
            jnp.sum(number * one * share, axis=0, keepdims=True)
            for one, share in zip(dprobs, shares)
        ]
        dscores = [
            (share * (one - lean)).astype(BF16) for share, one, lean in zip(shares, dprobs, leans)
        ]
        dscores = [(number * one.astype(F32)).astype(BF16) for one in dscores]
        weights = [(number * one.astype(BF16).astype(F32)).astype(BF16) for one in shares]
        dqs = [dot(one, kv[m, :, here], TN) for one, here in zip(dscores, heres)]
        dks = [
            dot(one, spread_heads(query[rows, here]), NN) for one, here in zip(dscores, heres)
        ]
        dvs = [dot(one, out, NN) for one, out in zip(weights, outs)]
        for h in pack_range:
            dquery[rows, heres[h]] = (pick_heads(dqs[h]) * scale).astype(BF16)
            dkv[m, :, heres[h]] = dks[h].astype(BF16)
            dkv[m, :, theres[h]] = dvs[h].astype(BF16)
        return carry

    lax.fori_loop(0, members, backward, 0)

    def back_copy(side, c):
        return pltpu.make_async_remote_copy(
            src_ref=dsend.at[side, c],
            dst_ref=drecv.at[side, c],
            send_sem=back_s.at[side, c],
            recv_sem=back_r.at[side, c],
            device_id=(me_m, down if side == 0 else up),
            device_id_type=MESH,
        )

    for c in range(chunks):
        here = pl.ds(c * BLOCK, BLOCK)
        step = dot(dkv[...].reshape(members * window, 2 * width), wqkv[here, pl.ds(width, 2 * width)], NT)
        step = step.reshape(members, window, BLOCK)
        for side, start in ((0, 0), (1, 2 * points)):
            dsend[side, c] = step[:, start : start + points].astype(BF16)
            back_copy(side, c).start()
        dhid[:, :, here] = step[:, points : 2 * points]

    each(group, part_copy, "wait_recv")
    piece_sum = local[mine].astype(F32)
    for k in range(1, group):
        piece_sum = piece_sum + part[k].astype(F32)
    plane[me_z] = split_loss(piece_sum).astype(BF16)
    each(n_z, plane_copy, "start")

    for c in range(chunks):
        here = pl.ds(c * BLOCK, BLOCK)
        step = dot(dquery[...], wqkv[here, pl.ds(0, width)], NT)
        dhid[:, :, here] = dhid[:, :, here] + step.reshape(members, points, BLOCK)

    for c in range(chunks):
        here = pl.ds(c * BLOCK, BLOCK)
        for side in range(2):
            back_copy(side, c).wait_recv()
        extra = drecv[0, c].astype(F32) + drecv[1, c].astype(F32)
        dhid[:, :, here] = dhid[:, :, here] + extra

    for m in range(members):
        dnormed = dhid[m] * gain[...]
        norm = normed[m]
        first = jnp.mean(dnormed, axis=-1, keepdims=True)
        second = jnp.mean(dnormed * norm, axis=-1, keepdims=True)
        dstates = inverse[m] * (dnormed - first - norm * second)
        grad[m] = (dstates + dmixed[pl.ds(m * points, points), :]).astype(BF16)

    each(n_z, plane_copy, "wait_recv")
    plane_sum = plane[0].astype(F32)
    for k in range(1, n_z):
        plane_sum = plane_sum + plane[k].astype(F32)
    full[mine] = (split_loss(plane_sum) * (1.0 / (points * n_grid))).astype(BF16)
    for k in far_first:
        full_copy(k).start()
    each(group, full_copy, "wait_recv")
    for t in range(bands * LANES // 32):
        r, b = t // bands, t % bands
        count = min(32, VARS - 32 * r)
        here = (pl.ds(32 * r, count), pl.ds(b * LANES, LANES))
        head_out[here] = full[t // per, t % per][:count].astype(F32)
    t = (VARS // 32) * bands
    sums = full[t // per, t % per].astype(F32)
    total = sums[spot : spot + 1, 0:1] + sums[spot + 1 : spot + 2, 0:1]
    loss[...] = total * (1.0 / (VARS * total_members))

    for copy in halo:
        copy.wait_send()
    for k in range(1, n_member):
        pred_copy(k).wait_send()
    each(group, part_copy, "wait_send")
    each(n_z, plane_copy, "wait_send")
    each(group, full_copy, "wait_send")
    for c in range(chunks):
        for side in range(2):
            back_copy(side, c).wait_send()


def body(sizes, states, ln_gain, w_qkv, w_out, w_head, targets, neighbours, counts):
    n_member, n_y, n_z, n_core = sizes
    members, points, width = states.shape
    flat = members * points
    window = 3 * points
    group = n_member * n_y * n_core
    chunks = width // BLOCK
    cols = PACK * (width // HEADS)
    tiles = (LANES // 32) * (width // LANES)
    per = tiles // group
    vmem = pl.BlockSpec(memory_space=pltpu.VMEM)
    hbm = pl.BlockSpec(memory_space=pl.ANY)
    dma = pltpu.SemaphoreType.DMA
    operands = (states, ln_gain.reshape(1, width), w_qkv, w_out, w_head.T, targets, neighbours, counts)
    loss, grad, head = pl.pallas_call(
        functools.partial(kernel, sizes),
        out_shape=(
            jax.ShapeDtypeStruct((1, 1), F32),
            jax.ShapeDtypeStruct((members, points, width), BF16),
            jax.ShapeDtypeStruct((VARS, width), F32),
        ),
        in_specs=[hbm] * 8,
        out_specs=(vmem, vmem, vmem),
        scratch_shapes=[
            pltpu.VMEM((members, points, width), BF16),
            pltpu.VMEM((1, width), F32),
            pltpu.VMEM((width, 3 * width), BF16),
            pltpu.VMEM((width, width), BF16),
            pltpu.VMEM((VARS, width), BF16),
            pltpu.VMEM((points, VARS), F32),
            pltpu.SMEM(neighbours.shape, jnp.int32),
            pltpu.SMEM((1,), jnp.int32),
            pltpu.VMEM((LANES, width), BF16),
            pltpu.VMEM((points, LANES), F32),
            pltpu.VMEM((flat, width), BF16),
            pltpu.VMEM((2, flat, width), BF16),
            pltpu.VMEM((flat, width), BF16),
            pltpu.VMEM((members, window, 2 * width), BF16),
            pltpu.VMEM((members, points, width), F32),
            pltpu.VMEM((members, points, 1), F32),
            pltpu.VMEM((window, LANES), F32),
            pltpu.VMEM((PACK * points, cols), F32),
            pltpu.VMEM((members, HEADS // PACK, window, PACK * points), F32),
            pltpu.VMEM((flat, width), BF16),
            pltpu.VMEM((flat, width), BF16),
            pltpu.VMEM((n_member, flat, LANES), BF16),
            pltpu.VMEM((flat, LANES), BF16),
            pltpu.VMEM((group, per, 32, LANES), BF16),
            pltpu.VMEM((group, per, 32, LANES), BF16),
            pltpu.VMEM((n_z, per, 32, LANES), BF16),
            pltpu.VMEM((group, per, 32, LANES), BF16),
            pltpu.VMEM((flat, width), F32),
            pltpu.VMEM((flat, width), BF16),
            pltpu.VMEM((flat, width), BF16),
            pltpu.VMEM((flat, width), BF16),
            pltpu.VMEM((members, window, 2 * width), BF16),
            pltpu.VMEM((2, chunks, members, points, BLOCK), BF16),
            pltpu.VMEM((2, chunks, members, points, BLOCK), BF16),
            pltpu.VMEM((members, points, width), F32),
            dma((6,)),
            dma((3 * width // (2 * BLOCK) + 1,)),
            dma((2,)),
            dma((2,)),
            dma((n_member,)),
            dma((n_member,)),
            dma((group,)),
            dma((group,)),
            dma((n_z,)),
            dma((n_z,)),
            dma((group,)),
            dma((group,)),
            dma((2, chunks)),
            dma((2, chunks)),
        ],
        compiler_params=pltpu.CompilerParams(
            collective_id=0, has_side_effects=True, vmem_limit_bytes=VMEM_BYTES
        ),
    )(*(pltpu.with_memory_space_constraint(x, pltpu.HBM) for x in operands[:-1]), operands[-1])
    return (loss.reshape(()), grad, head.T)


def solution(mesh):
    placed = (
        P("member", "grid", None),
        P(),
        P(),
        P(),
        P(),
        P("grid", None),
        P("grid", None),
        P("grid"),
    )
    n_core = 2
    n_z = min(8, mesh.shape["grid"] // n_core)
    sizes = (mesh.shape["member"], mesh.shape["grid"] // (n_z * n_core), n_z, n_core)
    return jax.shard_map(
        functools.partial(body, sizes),
        mesh=mesh,
        in_specs=placed,
        out_specs=(P(), P("member", "grid", None), P()),
        check_vma=False,
    )
```

```python
import functools

import jax
import jax.numpy as jnp
from jax import lax
from jax.experimental import pallas as pl
from jax.experimental.pallas import tpu as pltpu
from jax.sharding import PartitionSpec as P

HEADS = 16
VARS = 100
TILE = 16
EPS = 1e-05
DELTA = 0.1
LANES = 128
PACK = 4
HALVES = 2
VMEM_BYTES = 40 * 1024 * 1024
BLOCK = 256
MESH = pl.DeviceIdType.MESH
F32 = jnp.float32
BF16 = jnp.bfloat16

NN = (((1,), (0,)), ((), ()))
NT = (((1,), (1,)), ((), ()))
TN = (((0,), (0,)), ((), ()))


def dot(a, b, dims):
    return lax.dot_general(a, b, dims, preferred_element_type=F32)


def kernel(
    sizes,
    states_hbm,
    gain_hbm,
    wqkv_hbm,
    wout_hbm,
    whead_hbm,
    targets_hbm,
    neighbours_hbm,
    counts_hbm,
    loss,
    grad,
    head_out,
    states,
    gain,
    wqkv,
    wout,
    whead,
    targets,
    neighbours,
    counts,
    wpad,
    tpad,
    hidden,
    beside,
    query,
    kv,
    normed,
    inverse,
    cnt,
    hmask,
    probs,
    attn,
    mixed,
    mix,
    ens,
    pens,
    slopes,
    gradall,
    gradb,
    local,
    part,
    plane,
    full,
    dmixed,
    dmixedb,
    dattn,
    dquery,
    dkv,
    dsend,
    drecv,
    dhid,
    insem,
    wsem,
    halo_s,
    halo_r,
    pred_s,
    pred_r,
    mix_s,
    mix_r,
    part_s,
    part_r,
    plane_s,
    plane_r,
    full_s,
    full_r,
    back_s,
    back_r,
):
    n_member, n_y, n_z, n_core = sizes
    n_grid = n_y * n_z * n_core
    group = n_member * n_y * n_core
    members, points, width = states.shape
    window = kv.shape[1]
    flat = members * points
    cols = PACK * (width // HEADS)
    chunks = width // BLOCK
    packs = HEADS // PACK
    total_members = members * n_member
    per = local.shape[1]
    bands = width // LANES
    parts = n_y * n_core
    held = n_member * members

    me_m = lax.axis_index("member")
    me_g = lax.axis_index("grid")
    core = lax.rem(me_g, n_core)
    me_z = lax.rem(me_g // n_core, n_z)
    me_y = me_g // (n_core * n_z)
    up = lax.rem(me_g + 1, n_grid)
    down = lax.rem(me_g + n_grid - 1, n_grid)
    my_part = me_y * n_core + core
    mine = me_m * parts + my_part

    def grid_at(y, z, c):
        return (y * n_z + z) * n_core + c

    def group_peer(k):
        m = lax.rem(me_m + k // (n_y * n_core), n_member)
        y = lax.rem(me_y + lax.rem(k // n_core, n_y), n_y)
        c = lax.rem(core + lax.rem(k, n_core), n_core)
        return (m, grid_at(y, me_z, c))

    def part_peer(k):
        y = lax.rem(me_y + k // n_core, n_y)
        c = lax.rem(core + lax.rem(k, n_core), n_core)
        return (me_m, grid_at(y, me_z, c)), y * n_core + c

    def plane_peer(k):
        return (me_m, grid_at(me_y, lax.rem(me_z + k, n_z), core))

    barrier = pltpu.get_barrier_semaphore()

    def greet(device):
        pl.semaphore_signal(barrier, inc=1, device_id=device, device_id_type=MESH)

    def greet_group(k, c):
        greet(group_peer(k))
        return c

    def greet_plane(k, c):
        greet(plane_peer(k))
        return c

    greet((me_m, up))
    greet((me_m, down))
    lax.fori_loop(1, n_z, greet_plane, 0)
    lax.fori_loop(1, group, greet_group, 0)

    wide = 2 * BLOCK
    n_wide = 3 * width // wide
    small_copies = [
        pltpu.make_async_copy(source, target, insem.at[i])
        for i, (source, target) in enumerate(
            (
                (states_hbm, states),
                (gain_hbm, gain),
                (neighbours_hbm, neighbours),
                (counts_hbm, counts),
                (whead_hbm, whead),
                (targets_hbm, targets),
            )
        )
    ]
    weight_copies = [
        pltpu.make_async_copy(
            wqkv_hbm.at[:, pl.ds(c * wide, wide)], wqkv.at[:, pl.ds(c * wide, wide)], wsem.at[c]
        )
        for c in range(n_wide)
    ]
    weight_copies.append(pltpu.make_async_copy(wout_hbm, wout, wsem.at[n_wide]))
    for copy in small_copies + weight_copies:
        copy.start()
    small_copies[0].wait()
    small_copies[1].wait()

    for m in range(members):
        values = states[m].astype(F32)
        centre = jnp.mean(values, axis=-1, keepdims=True)
        centred = values - centre
        spread = jnp.mean(centred * centred, axis=-1, keepdims=True)
        inv = lax.rsqrt(spread + EPS)
        norm = centred * inv
        normed[m] = norm
        inverse[m] = inv
        hidden[pl.ds(m * points, points), :] = (norm * gain[...]).astype(BF16)

    pl.semaphore_wait(barrier, 2 + (group - 1) + (n_z - 1))

    some = members // HALVES
    band_rows = [pl.ds(h * some * points, some * points) for h in range(HALVES)]
    halo = [
        [
            pltpu.make_async_remote_copy(
                src_ref=hidden.at[rows],
                dst_ref=beside.at[i, rows],
                send_sem=halo_s.at[h, i],
                recv_sem=halo_r.at[h, i],
                device_id=(me_m, side),
                device_id_type=MESH,
            )
            for i, side in enumerate((up, down))
        ]
        for h, rows in enumerate(band_rows)
    ]
    for pair in halo:
        for copy in pair:
            copy.start()

    for copy in small_copies[2:]:
        copy.wait()

    key_tile = 2 * me_g - 2 + lax.broadcasted_iota(jnp.int32, (window, LANES), 0) // TILE
    lane = lax.broadcasted_iota(jnp.int32, (window, LANES), 1)
    query_tile = lax.rem(lane, points) // TILE
    number = jnp.zeros((window, LANES), F32)
    for t in range(points // TILE):
        for e in range(neighbours.shape[1]):
            hit = (key_tile == neighbours[t, e]) & (query_tile == t)
            number = number + jnp.where(hit, 1.0, 0.0)
    cnt[...] = number
    rows_i = lax.broadcasted_iota(jnp.int32, (PACK * points, cols), 0) // points
    cols_i = lax.broadcasted_iota(jnp.int32, (PACK * points, cols), 1) // (cols // PACK)
    hmask[...] = jnp.where(rows_i == cols_i, 1.0, 0.0)
    wpad[...] = jnp.zeros_like(wpad)
    wpad[pl.ds(0, VARS), :] = whead[...]
    tpad[...] = jnp.zeros_like(tpad)
    tpad[:, pl.ds(0, VARS)] = targets[...]

    for c in range(n_wide):
        weight_copies[c].wait()
        step = dot(hidden[...], wqkv[:, pl.ds(c * wide, wide)], NN).astype(BF16)
        if c * wide < width:
            query[:, pl.ds(c * wide, wide)] = step * jnp.asarray((width // HEADS) ** -0.5, BF16)
        else:
            there = pl.ds(c * wide - width, wide)
            kv[:, pl.ds(points, points), there] = step.reshape(members, points, wide)

    def spread_heads(rows):
        return jnp.concatenate([rows] * PACK, axis=0) * hmask[...].astype(BF16)

    def pick_heads(rows):
        rows = rows * hmask[...]
        return jnp.sum(rows.reshape(PACK, points, cols), axis=0)

    pack_range = range(packs)
    heres = [pl.ds(h * cols, cols) for h in pack_range]
    theres = [pl.ds(width + h * cols, cols) for h in pack_range]

    share = chunks // n_member

    def mix_copy(h, k):
        return pltpu.make_async_remote_copy(
            src_ref=mixed.at[pl.ds(lax.rem(me_m + k, n_member) * share, share), band_rows[h]],
            dst_ref=mix.at[k, :, band_rows[h]],
            send_sem=mix_s.at[h, k],
            recv_sem=mix_r.at[h, k],
            device_id=(lax.rem(me_m + k, n_member), me_g),
            device_id_type=MESH,
        )

    def pred_copy(h, k):
        return pltpu.make_async_remote_copy(
            src_ref=ens.at[0, band_rows[h]],
            dst_ref=ens.at[k, band_rows[h]],
            send_sem=pred_s.at[h, k],
            recv_sem=pred_r.at[h, k],
            device_id=(lax.rem(me_m + k, n_member), me_g),
            device_id_type=MESH,
        )

    far_members = sorted(range(1, n_member), key=lambda k: -min(k, n_member - k))
    number = cnt[...]
    for h in range(HALVES):
        for copy in halo[h]:
            copy.wait_recv()
        near = beside[:, band_rows[h], :].reshape(2 * some * points, width)
        group_members = pl.ds(h * some, some)
        for c in range(2 * width // wide):
            here = pl.ds(c * wide, wide)
            step = dot(near, wqkv[:, pl.ds(width + c * wide, wide)], NN)
            step = step.astype(BF16).reshape(2, some, points, wide)
            kv[group_members, pl.ds(0, points), here] = step[0]
            kv[group_members, pl.ds(2 * points, points), here] = step[1]

        pairs = [(m, p) for m in range(h * some, (h + 1) * some) for p in pack_range]
        queries = [query[pl.ds(m * points, points), heres[p]] for m, p in pairs]
        scores = [dot(kv[m, :, heres[p]], spread_heads(q), NT) for (m, p), q in zip(pairs, queries)]
        scores = [jnp.where(number > 0.0, one, -3e38) for one in scores]
        tops = [jnp.max(one, axis=0, keepdims=True) for one in scores]
        expos = [jnp.exp(one - top) for one, top in zip(scores, tops)]
        totals = [jnp.sum(number * expo, axis=0, keepdims=True) for expo in expos]
        shares = [expo / total for expo, total in zip(expos, totals)]
        weights = [(number * one.astype(BF16).astype(F32)).astype(BF16) for one in shares]
        outs = [dot(one, kv[m, :, theres[p]], TN) for one, (m, p) in zip(weights, pairs)]
        for (m, p), one, out in zip(pairs, shares, outs):
            probs[m, p] = one
            attn[pl.ds(m * points, points), heres[p]] = pick_heads(out).astype(BF16)

        if h == 0:
            weight_copies[n_wide].wait()
        rows = band_rows[h]
        for k in (*far_members, 0):
            for c in range(share):
                block = lax.rem(me_m + k, n_member) * share + c
                here = pl.ds(pl.multiple_of(block * BLOCK, BLOCK), BLOCK)
                proj = dot(attn[rows, :], wout[:, here], NN)
                before = states[group_members, :, here].reshape(some * points, BLOCK).astype(F32)
                mixed[block, rows] = (before + proj).astype(BF16)
            if k != 0 and (h < HALVES - 1 or k == far_members[0]):
                mix_copy(h, k).start()
        pred = dot(mixed[0, rows], wpad[:, pl.ds(0, BLOCK)], NT)
        for c in range(1, chunks):
            pred = pred + dot(mixed[c, rows], wpad[:, pl.ds(c * BLOCK, BLOCK)], NT)
        ens[0, rows] = pred.astype(BF16)
        for k in far_members:
            pred_copy(h, k).start()
        if h == HALVES - 1:
            for k in far_members[1:]:
                mix_copy(h, k).start()
    mix[0] = mixed[pl.ds(me_m * share, share)]
    for h in range(HALVES):
        for k in range(1, n_member):
            pred_copy(h, k).wait_recv()

    step_rows = 8

    def crps(block, total):
        start = pl.multiple_of(block * step_rows, step_rows)
        row = start + lax.broadcasted_iota(jnp.int32, (step_rows, LANES), 0)
        column = lax.broadcasted_iota(jnp.int32, (step_rows, LANES), 1)
        valid = (row < counts[0]) & (column < VARS)
        target = tpad[pl.ds(start, step_rows), :]
        values = [pens[i, pl.ds(start, step_rows), :] for i in range(held)]
        pulls = [None] * held
        apart = jnp.zeros((step_rows, LANES), F32)
        for i in range(held):
            for j in range(i + 1, held):
                gap = values[i] - values[j]
                square = gap * gap + DELTA * DELTA
                root = lax.rsqrt(square)
                pull = gap * root
                pulls[i] = pull if pulls[i] is None else pulls[i] + pull
                pulls[j] = -pull if pulls[j] is None else pulls[j] - pull
                if i < members:
                    length = square * root
                    apart = apart + (length + length if j < members else length)
        terms = apart * (-0.5 / (total_members - 1))
        for i in range(held):
            miss = values[i] - target
            square = miss * miss + DELTA * DELTA
            root = lax.rsqrt(square)
            slope = miss * root - pulls[i] * (1.0 / (total_members - 1))
            slopes[i, pl.ds(start, step_rows), :] = jnp.where(valid, slope, 0.0)
            if i < members:
                terms = terms + square * root
        return total + jnp.where(valid, terms, 0.0)

    for k in range(n_member):
        pens[pl.ds(k * members, members)] = ens[k].astype(F32).reshape(members, points, LANES)
    terms = lax.fori_loop(0, points // step_rows, crps, jnp.zeros((step_rows, LANES), F32))
    loss_part = jnp.sum(jnp.sum(terms, axis=1, keepdims=True), axis=0, keepdims=True)
    gradall[...] = slopes[...].reshape(held * points, LANES).astype(BF16)
    gradb[...] = gradall[pl.ds(0, flat), :]

    quads = LANES // 32
    tile_row = lax.broadcasted_iota(jnp.int32, (per, 32, LANES), 1)
    tile_at = my_part * per + lax.broadcasted_iota(jnp.int32, (per, 32, LANES), 0)
    variable = lax.rem(tile_at, quads) * 32 + tile_row
    spot = VARS % 32

    def split_loss(tiles):
        value = tiles[:, spot : spot + 1, :] + tiles[:, spot + 1 : spot + 2, :]
        high = value.astype(BF16).astype(F32)
        return jnp.where(
            variable == VARS, high, jnp.where(variable == VARS + 1, value - high, tiles)
        )

    row_all = lax.broadcasted_iota(jnp.int32, (LANES, 1), 0)
    loss_high = loss_part.astype(BF16).astype(F32)
    tail = jnp.where(
        row_all == VARS, loss_high, jnp.where(row_all == VARS + 1, loss_part - loss_high, 0.0)
    )
    for h in range(HALVES):
        for k in range(1, n_member):
            mix_copy(h, k).wait_recv()
    per_block = BLOCK // LANES
    for c in range(share):
        block = dot(gradall[...], mix[:, c].reshape(held * points, BLOCK), TN) + tail
        for b in range(per_block):
            for r in range(quads):
                u = (c * per_block + b) * quads + r
                local[u // per, u % per] = block[
                    r * 32 : (r + 1) * 32, b * LANES : (b + 1) * LANES
                ].astype(BF16)

    def part_copy(k):
        device, owner = part_peer(k)
        return pltpu.make_async_remote_copy(
            src_ref=local.at[owner],
            dst_ref=part.at[k],
            send_sem=part_s.at[k],
            recv_sem=part_r.at[k],
            device_id=device,
            device_id_type=MESH,
        )

    def plane_copy(k):
        return pltpu.make_async_remote_copy(
            src_ref=plane.at[me_z],
            dst_ref=plane.at[me_z],
            send_sem=plane_s.at[k],
            recv_sem=plane_r.at[k],
            device_id=plane_peer(k),
            device_id_type=MESH,
        )

    def full_copy(k):
        return pltpu.make_async_remote_copy(
            src_ref=full.at[mine],
            dst_ref=full.at[mine],
            send_sem=full_s.at[k],
            recv_sem=full_r.at[k],
            device_id=group_peer(k),
            device_id_type=MESH,
        )

    def apart_by(k):
        m, y = k // (n_y * n_core), k // n_core % n_y
        return min(m, n_member - m) + min(y, n_y - y)

    far_first = sorted(range(1, group), key=lambda k: -apart_by(k))

    def each(count, make, act):
        def step(k, c):
            getattr(make(k), act)()
            return c

        lax.fori_loop(1, count, step, 0)

    for k in range(parts - 1, 0, -1):
        part_copy(k).start()

    for c in range(chunks):
        here = pl.ds(c * BLOCK, BLOCK)
        step = dot(gradb[...], wpad[:, here], NN)
        dmixed[:, here] = step
        dmixedb[:, here] = step.astype(BF16)
    for c in range(chunks):
        here = pl.ds(c * BLOCK, BLOCK)
        dattn[:, here] = dot(dmixedb[...], wout[here, :], NT).astype(BF16)

    scale = (width // HEADS) ** -0.5

    def backward(m, carry):
        rows = pl.ds(pl.multiple_of(m * points, points), points)
        number = cnt[...]
        outs = [spread_heads(dattn[rows, here]) for here in heres]
        dprobs = [dot(kv[m, :, there], out, NT) for there, out in zip(theres, outs)]
        shares = [probs[m, h] for h in pack_range]
        leans = [
            jnp.sum(number * one * share, axis=0, keepdims=True)
            for one, share in zip(dprobs, shares)
        ]
        dscores = [
            (share * (one - lean)).astype(BF16) for share, one, lean in zip(shares, dprobs, leans)
        ]
        dscores = [(number * one.astype(F32)).astype(BF16) for one in dscores]
        weights = [(number * one.astype(BF16).astype(F32)).astype(BF16) for one in shares]
        dqs = [dot(one, kv[m, :, here], TN) for one, here in zip(dscores, heres)]
        dks = [
            dot(one, spread_heads(query[rows, here]), NN) for one, here in zip(dscores, heres)
        ]
        dvs = [dot(one, out, NN) for one, out in zip(weights, outs)]
        for h in pack_range:
            dquery[rows, heres[h]] = (pick_heads(dqs[h]) * scale).astype(BF16)
            dkv[m, :, heres[h]] = dks[h].astype(BF16)
            dkv[m, :, theres[h]] = dvs[h].astype(BF16)
        return carry

    lax.fori_loop(0, members, backward, 0)

    def back_copy(side, c):
        return pltpu.make_async_remote_copy(
            src_ref=dsend.at[side, c],
            dst_ref=drecv.at[side, c],
            send_sem=back_s.at[side, c],
            recv_sem=back_r.at[side, c],
            device_id=(me_m, down if side == 0 else up),
            device_id_type=MESH,
        )

    def second_stage():
        each(parts, part_copy, "wait_recv")
        piece_sum = local[my_part].astype(F32)
        for k in range(1, parts):
            piece_sum = piece_sum + part[k].astype(F32)
        plane[me_z] = split_loss(piece_sum).astype(BF16)
        for k in sorted(range(1, n_z), key=lambda k: -min(k, n_z - k)):
            plane_copy(k).start()

    for c in range(chunks):
        if c == chunks // 2:
            second_stage()
        here = pl.ds(c * BLOCK, BLOCK)
        step = dot(dkv[...].reshape(members * window, 2 * width), wqkv[here, pl.ds(width, 2 * width)], NT)
        step = step.reshape(members, window, BLOCK)
        for side, start in ((0, 0), (1, 2 * points)):
            dsend[side, c] = step[:, start : start + points].astype(BF16)
            back_copy(side, c).start()
        dhid[:, :, here] = step[:, points : 2 * points]

    for c in range(chunks):
        here = pl.ds(c * BLOCK, BLOCK)
        step = dot(dquery[...], wqkv[here, pl.ds(0, width)], NT)
        dhid[:, :, here] = dhid[:, :, here] + step.reshape(members, points, BLOCK)

    each(n_z, plane_copy, "wait_recv")
    plane_sum = plane[0].astype(F32)
    for k in range(1, n_z):
        plane_sum = plane_sum + plane[k].astype(F32)
    full[mine] = (split_loss(plane_sum) * (1.0 / (points * n_grid))).astype(BF16)
    for k in far_first:
        full_copy(k).start()
    for c in range(chunks):
        here = pl.ds(c * BLOCK, BLOCK)
        for side in range(2):
            back_copy(side, c).wait_recv()
        extra = drecv[0, c].astype(F32) + drecv[1, c].astype(F32)
        dhid[:, :, here] = dhid[:, :, here] + extra

    for m in range(members):
        dnormed = dhid[m] * gain[...]
        norm = normed[m]
        first = jnp.mean(dnormed, axis=-1, keepdims=True)
        second = jnp.mean(dnormed * norm, axis=-1, keepdims=True)
        dstates = inverse[m] * (dnormed - first - norm * second)
        grad[m] = (dstates + dmixed[pl.ds(m * points, points), :]).astype(BF16)

    each(group, full_copy, "wait_recv")
    total = jnp.zeros((1, 1), F32)
    for m in range(n_member):
        for u in range(parts * per):
            b, r = m * (bands // n_member) + u // quads, u % quads
            tile = full[m * parts + u // per, u % per].astype(F32)
            count = min(32, VARS - 32 * r)
            head_out[pl.ds(32 * r, count), pl.ds(b * LANES, LANES)] = tile[:count]
            if u == VARS // 32:
                total = total + tile[spot : spot + 1, 0:1] + tile[spot + 1 : spot + 2, 0:1]
    loss[...] = total * (1.0 / (VARS * total_members))

    for h in range(HALVES):
        for copy in halo[h]:
            copy.wait_send()
        for k in range(1, n_member):
            pred_copy(h, k).wait_send()
            mix_copy(h, k).wait_send()
    each(parts, part_copy, "wait_send")
    each(n_z, plane_copy, "wait_send")
    each(group, full_copy, "wait_send")
    for c in range(chunks):
        for side in range(2):
            back_copy(side, c).wait_send()


def results(loss, grad, head, loss_hbm, grad_hbm, head_hbm, sem):
    copies = [
        pltpu.make_async_copy(source, target, sem.at[i])
        for i, (source, target) in enumerate(((grad, grad_hbm), (head, head_hbm), (loss, loss_hbm)))
    ]
    for copy in copies:
        copy.start()
    for copy in copies:
        copy.wait()


def body(sizes, states, ln_gain, w_qkv, w_out, w_head, targets, neighbours, counts):
    n_member, n_y, n_z, n_core = sizes
    members, points, width = states.shape
    flat = members * points
    window = 3 * points
    group = n_member * n_y * n_core
    chunks = width // BLOCK
    cols = PACK * (width // HEADS)
    tiles = (LANES // 32) * (width // LANES)
    per = tiles // group
    vmem = pl.BlockSpec(memory_space=pltpu.VMEM)
    hbm = pl.BlockSpec(memory_space=pl.ANY)
    dma = pltpu.SemaphoreType.DMA
    operands = (states, ln_gain.reshape(1, width), w_qkv, w_out, w_head.T, targets, neighbours, counts)
    loss, grad, head = pl.pallas_call(
        functools.partial(kernel, sizes),
        out_shape=(
            jax.ShapeDtypeStruct((1, 1), F32),
            jax.ShapeDtypeStruct((members, points, width), BF16),
            jax.ShapeDtypeStruct((VARS, width), F32),
        ),
        in_specs=[hbm] * 8,
        out_specs=(vmem, vmem, vmem),
        scratch_shapes=[
            pltpu.VMEM((members, points, width), BF16),
            pltpu.VMEM((1, width), F32),
            pltpu.VMEM((width, 3 * width), BF16),
            pltpu.VMEM((width, width), BF16),
            pltpu.VMEM((VARS, width), BF16),
            pltpu.VMEM((points, VARS), F32),
            pltpu.SMEM(neighbours.shape, jnp.int32),
            pltpu.SMEM((1,), jnp.int32),
            pltpu.VMEM((LANES, width), BF16),
            pltpu.VMEM((points, LANES), F32),
            pltpu.VMEM((flat, width), BF16),
            pltpu.VMEM((2, flat, width), BF16),
            pltpu.VMEM((flat, width), BF16),
            pltpu.VMEM((members, window, 2 * width), BF16),
            pltpu.VMEM((members, points, width), F32),
            pltpu.VMEM((members, points, 1), F32),
            pltpu.VMEM((window, LANES), F32),
            pltpu.VMEM((PACK * points, cols), F32),
            pltpu.VMEM((members, HEADS // PACK, window, PACK * points), F32),
            pltpu.VMEM((flat, width), BF16),
            pltpu.VMEM((chunks, flat, BLOCK), BF16),
            pltpu.VMEM((n_member, chunks // n_member, flat, BLOCK), BF16),
            pltpu.VMEM((n_member, flat, LANES), BF16),
            pltpu.VMEM((n_member * members, points, LANES), F32),
            pltpu.VMEM((n_member * members, points, LANES), F32),
            pltpu.VMEM((n_member * flat, LANES), BF16),
            pltpu.VMEM((flat, LANES), BF16),
            pltpu.VMEM((n_y * n_core, per, 32, LANES), BF16),
            pltpu.VMEM((n_y * n_core, per, 32, LANES), BF16),
            pltpu.VMEM((n_z, per, 32, LANES), BF16),
            pltpu.VMEM((group, per, 32, LANES), BF16),
            pltpu.VMEM((flat, width), F32),
            pltpu.VMEM((flat, width), BF16),
            pltpu.VMEM((flat, width), BF16),
            pltpu.VMEM((flat, width), BF16),
            pltpu.VMEM((members, window, 2 * width), BF16),
            pltpu.VMEM((2, chunks, members, points, BLOCK), BF16),
            pltpu.VMEM((2, chunks, members, points, BLOCK), BF16),
            pltpu.VMEM((members, points, width), F32),
            dma((6,)),
            dma((3 * width // (2 * BLOCK) + 1,)),
            dma((HALVES, 2)),
            dma((HALVES, 2)),
            dma((HALVES, n_member)),
            dma((HALVES, n_member)),
            dma((HALVES, n_member)),
            dma((HALVES, n_member)),
            dma((n_y * n_core,)),
            dma((n_y * n_core,)),
            dma((n_z,)),
            dma((n_z,)),
            dma((group,)),
            dma((group,)),
            dma((2, chunks)),
            dma((2, chunks)),
        ],
        compiler_params=pltpu.CompilerParams(
            collective_id=0, has_side_effects=True, vmem_limit_bytes=VMEM_BYTES
        ),
    )(*(pltpu.with_memory_space_constraint(x, pltpu.HBM) for x in operands[:-1]), operands[-1])
    held = [pltpu.with_memory_space_constraint(x, pltpu.VMEM) for x in (loss, grad, head)]
    loss, grad, head = pl.pallas_call(
        results,
        out_shape=tuple(jax.ShapeDtypeStruct(x.shape, x.dtype) for x in held),
        in_specs=[vmem] * 3,
        out_specs=(hbm,) * 3,
        scratch_shapes=[dma((3,))],
    )(*held)
    return (loss.reshape(()), grad, head.T)


def solution(mesh):
    placed = (
        P("member", "grid", None),
        P(),
        P(),
        P(),
        P(),
        P("grid", None),
        P("grid", None),
        P("grid"),
    )
    n_core = 2
    n_z = min(8, mesh.shape["grid"] // n_core)
    sizes = (mesh.shape["member"], mesh.shape["grid"] // (n_z * n_core), n_z, n_core)
    return jax.shard_map(
        functools.partial(body, sizes),
        mesh=mesh,
        in_specs=placed,
        out_specs=(P(), P("member", "grid", None), P()),
        check_vma=False,
    )
```

```python
import functools

import jax
import jax.numpy as jnp
from jax import lax
from jax.experimental import pallas as pl
from jax.experimental.pallas import tpu as pltpu
from jax.sharding import PartitionSpec as P

HEADS = 16
VARS = 100
TILE = 16
EPS = 1e-05
DELTA = 0.1
LANES = 128
PACK = 4
SPLIT = (2, 2)
HALVES = len(SPLIT)
VMEM_BYTES = 40 * 1024 * 1024
BLOCK = 256
MESH = pl.DeviceIdType.MESH
F32 = jnp.float32
BF16 = jnp.bfloat16

NN = (((1,), (0,)), ((), ()))
NT = (((1,), (1,)), ((), ()))
TN = (((0,), (0,)), ((), ()))


def dot(a, b, dims):
    return lax.dot_general(a, b, dims, preferred_element_type=F32)


def kernel(
    sizes,
    states_hbm,
    gain_hbm,
    wqkv_hbm,
    wout_hbm,
    whead_hbm,
    targets_hbm,
    neighbours_hbm,
    counts_hbm,
    loss,
    grad,
    head_out,
    states,
    gain,
    wqkv,
    wout,
    whead,
    targets,
    neighbours,
    counts,
    wpad,
    tpad,
    hidden,
    beside,
    query,
    kv,
    normed,
    inverse,
    cnt,
    hmask,
    probs,
    attn,
    mixed,
    mix,
    ens,
    pens,
    slopes,
    gradall,
    gradb,
    local,
    part,
    plane,
    full,
    dmixed,
    dmixedb,
    dattn,
    dquery,
    dkv,
    dsend,
    drecv,
    dhid,
    insem,
    wsem,
    halo_s,
    halo_r,
    pred_s,
    pred_r,
    mix_s,
    mix_r,
    part_s,
    part_r,
    plane_s,
    plane_r,
    full_s,
    full_r,
    pass_s,
    pass_r,
    back_s,
    back_r,
):
    n_member, n_y, n_z, n_core = sizes
    n_grid = n_y * n_z * n_core
    group = n_member * n_y * n_core
    members, points, width = states.shape
    window = kv.shape[1]
    flat = members * points
    cols = PACK * (width // HEADS)
    chunks = width // BLOCK
    packs = HEADS // PACK
    total_members = members * n_member
    per = local.shape[1]
    bands = width // LANES
    parts = n_y * n_core
    held = n_member * members

    me_m = lax.axis_index("member")
    me_g = lax.axis_index("grid")
    core = lax.rem(me_g, n_core)
    me_z = lax.rem(me_g // n_core, n_z)
    me_y = me_g // (n_core * n_z)
    up = lax.rem(me_g + 1, n_grid)
    down = lax.rem(me_g + n_grid - 1, n_grid)
    my_part = me_y * n_core + core
    mine = me_m * parts + my_part

    def grid_at(y, z, c):
        return (y * n_z + z) * n_core + c

    def group_peer(k):
        m = lax.rem(me_m + k // (n_y * n_core), n_member)
        y = lax.rem(me_y + lax.rem(k // n_core, n_y), n_y)
        c = lax.rem(core + lax.rem(k, n_core), n_core)
        return (m, grid_at(y, me_z, c))

    def part_peer(k):
        y = lax.rem(me_y + k // n_core, n_y)
        c = lax.rem(core + lax.rem(k, n_core), n_core)
        return (me_m, grid_at(y, me_z, c)), y * n_core + c

    def plane_peer(k):
        return (me_m, grid_at(me_y, lax.rem(me_z + k, n_z), core))

    barrier = pltpu.get_barrier_semaphore()

    def greet(device):
        pl.semaphore_signal(barrier, inc=1, device_id=device, device_id_type=MESH)

    def ring(k, n):
        return min(k, n - k)

    greetings = [(0.5, (me_m, up)), (0.5, (me_m, down))]
    greetings += [(ring(k, n_z), plane_peer(k)) for k in range(1, n_z)]
    greetings += [
        (ring(k // (n_y * n_core), n_member) + ring(k // n_core % n_y, n_y), group_peer(k))
        for k in range(1, group)
    ]
    for _, device in sorted(greetings, key=lambda pair: -pair[0]):
        greet(device)

    wide = 2 * BLOCK
    n_wide = 3 * width // wide
    small_copies = [
        pltpu.make_async_copy(source, target, insem.at[i])
        for i, (source, target) in enumerate(
            (
                (states_hbm, states),
                (gain_hbm, gain),
                (neighbours_hbm, neighbours),
                (counts_hbm, counts),
                (whead_hbm, whead),
                (targets_hbm, targets),
            )
        )
    ]
    weight_copies = [
        pltpu.make_async_copy(
            wqkv_hbm.at[:, pl.ds(c * wide, wide)], wqkv.at[:, pl.ds(c * wide, wide)], wsem.at[c]
        )
        for c in range(n_wide)
    ]
    weight_copies.append(pltpu.make_async_copy(wout_hbm, wout, wsem.at[n_wide]))
    for copy in small_copies + weight_copies:
        copy.start()
    small_copies[0].wait()
    small_copies[1].wait()

    for m in range(members):
        values = states[m].astype(F32)
        centre = jnp.mean(values, axis=-1, keepdims=True)
        centred = values - centre
        spread = jnp.mean(centred * centred, axis=-1, keepdims=True)
        inv = lax.rsqrt(spread + EPS)
        norm = centred * inv
        normed[m] = norm
        inverse[m] = inv
        hidden[pl.ds(m * points, points), :] = (norm * gain[...]).astype(BF16)

    pl.semaphore_wait(barrier, 2 + (group - 1) + (n_z - 1))

    firsts = [sum(SPLIT[:h]) for h in range(HALVES)]
    band_rows = [pl.ds(first * points, some * points) for first, some in zip(firsts, SPLIT)]
    halo = [
        [
            pltpu.make_async_remote_copy(
                src_ref=hidden.at[rows],
                dst_ref=beside.at[i, rows],
                send_sem=halo_s.at[h, i],
                recv_sem=halo_r.at[h, i],
                device_id=(me_m, side),
                device_id_type=MESH,
            )
            for i, side in enumerate((up, down))
        ]
        for h, rows in enumerate(band_rows)
    ]
    for pair in halo:
        for copy in pair:
            copy.start()

    for copy in small_copies[2:]:
        copy.wait()

    key_tile = 2 * me_g - 2 + lax.broadcasted_iota(jnp.int32, (window, LANES), 0) // TILE
    lane = lax.broadcasted_iota(jnp.int32, (window, LANES), 1)
    query_tile = lax.rem(lane, points) // TILE
    number = jnp.zeros((window, LANES), F32)
    for t in range(points // TILE):
        for e in range(neighbours.shape[1]):
            hit = (key_tile == neighbours[t, e]) & (query_tile == t)
            number = number + jnp.where(hit, 1.0, 0.0)
    cnt[...] = number
    rows_i = lax.broadcasted_iota(jnp.int32, (PACK * points, cols), 0) // points
    cols_i = lax.broadcasted_iota(jnp.int32, (PACK * points, cols), 1) // (cols // PACK)
    hmask[...] = jnp.where(rows_i == cols_i, 1.0, 0.0)
    wpad[...] = jnp.zeros_like(wpad)
    wpad[pl.ds(0, VARS), :] = whead[...]
    tpad[...] = jnp.zeros_like(tpad)
    tpad[:, pl.ds(0, VARS)] = targets[...]

    for c in range(n_wide):
        weight_copies[c].wait()
        step = dot(hidden[...], wqkv[:, pl.ds(c * wide, wide)], NN).astype(BF16)
        if c * wide < width:
            query[:, pl.ds(c * wide, wide)] = step * jnp.asarray((width // HEADS) ** -0.5, BF16)
        else:
            there = pl.ds(c * wide - width, wide)
            kv[:, pl.ds(points, points), there] = step.reshape(members, points, wide)

    def spread_heads(rows):
        return jnp.concatenate([rows] * PACK, axis=0) * hmask[...].astype(BF16)

    def pick_heads(rows):
        rows = rows * hmask[...]
        return jnp.sum(rows.reshape(PACK, points, cols), axis=0)

    pack_range = range(packs)
    heres = [pl.ds(h * cols, cols) for h in pack_range]
    theres = [pl.ds(width + h * cols, cols) for h in pack_range]

    share = chunks // n_member

    def mix_copy(h, k):
        return pltpu.make_async_remote_copy(
            src_ref=mixed.at[pl.ds(lax.rem(me_m + k, n_member) * share, share), band_rows[h]],
            dst_ref=mix.at[k, :, band_rows[h]],
            send_sem=mix_s.at[h, k],
            recv_sem=mix_r.at[h, k],
            device_id=(lax.rem(me_m + k, n_member), me_g),
            device_id_type=MESH,
        )

    def pred_copy(h, k):
        return pltpu.make_async_remote_copy(
            src_ref=ens.at[0, band_rows[h]],
            dst_ref=ens.at[k, band_rows[h]],
            send_sem=pred_s.at[h, k],
            recv_sem=pred_r.at[h, k],
            device_id=(lax.rem(me_m + k, n_member), me_g),
            device_id_type=MESH,
        )

    far_members = sorted(range(1, n_member), key=lambda k: -min(k, n_member - k))
    number = cnt[...]
    for h, (first, some) in enumerate(zip(firsts, SPLIT)):
        for copy in halo[h]:
            copy.wait_recv()
        near = beside[:, band_rows[h], :].reshape(2 * some * points, width)
        group_members = pl.ds(first, some)
        for c in range(2 * width // wide):
            here = pl.ds(c * wide, wide)
            step = dot(near, wqkv[:, pl.ds(width + c * wide, wide)], NN)
            step = step.astype(BF16).reshape(2, some, points, wide)
            kv[group_members, pl.ds(0, points), here] = step[0]
            kv[group_members, pl.ds(2 * points, points), here] = step[1]

        pairs = [(m, p) for m in range(first, first + some) for p in pack_range]
        queries = [query[pl.ds(m * points, points), heres[p]] for m, p in pairs]
        scores = [dot(kv[m, :, heres[p]], spread_heads(q), NT) for (m, p), q in zip(pairs, queries)]
        scores = [jnp.where(number > 0.0, one, -3e38) for one in scores]
        tops = [jnp.max(one, axis=0, keepdims=True) for one in scores]
        expos = [jnp.exp(one - top) for one, top in zip(scores, tops)]
        totals = [jnp.sum(number * expo, axis=0, keepdims=True) for expo in expos]
        shares = [expo / total for expo, total in zip(expos, totals)]
        weights = [(number * one.astype(BF16).astype(F32)).astype(BF16) for one in shares]
        outs = [dot(one, kv[m, :, theres[p]], TN) for one, (m, p) in zip(weights, pairs)]
        for (m, p), one, out in zip(pairs, shares, outs):
            probs[m, p] = one
            attn[pl.ds(m * points, points), heres[p]] = pick_heads(out).astype(BF16)

        if h == 0:
            weight_copies[n_wide].wait()
        rows = band_rows[h]
        for k in (*far_members, 0):
            for c in range(share):
                block = lax.rem(me_m + k, n_member) * share + c
                here = pl.ds(pl.multiple_of(block * BLOCK, BLOCK), BLOCK)
                proj = dot(attn[rows, :], wout[:, here], NN)
                before = states[group_members, :, here].reshape(some * points, BLOCK).astype(F32)
                mixed[block, rows] = (before + proj).astype(BF16)
            if k != 0 and (h < HALVES - 1 or k == far_members[0]):
                mix_copy(h, k).start()
        pred = dot(mixed[0, rows], wpad[:, pl.ds(0, BLOCK)], NT)
        for c in range(1, chunks):
            pred = pred + dot(mixed[c, rows], wpad[:, pl.ds(c * BLOCK, BLOCK)], NT)
        ens[0, rows] = pred.astype(BF16)
        for k in far_members:
            pred_copy(h, k).start()
        if h == HALVES - 1:
            for k in far_members[1:]:
                mix_copy(h, k).start()
    mix[0] = mixed[pl.ds(me_m * share, share)]
    for h in range(HALVES):
        for k in range(1, n_member):
            pred_copy(h, k).wait_recv()

    step_rows = 8

    def crps(block, total):
        start = pl.multiple_of(block * step_rows, step_rows)
        row = start + lax.broadcasted_iota(jnp.int32, (step_rows, LANES), 0)
        column = lax.broadcasted_iota(jnp.int32, (step_rows, LANES), 1)
        valid = (row < counts[0]) & (column < VARS)
        target = tpad[pl.ds(start, step_rows), :]
        values = [pens[i, pl.ds(start, step_rows), :] for i in range(held)]
        pulls = [None] * held
        apart = jnp.zeros((step_rows, LANES), F32)
        for i in range(held):
            for j in range(i + 1, held):
                gap = values[i] - values[j]
                square = gap * gap + DELTA * DELTA
                root = lax.rsqrt(square)
                pull = gap * root
                pulls[i] = pull if pulls[i] is None else pulls[i] + pull
                pulls[j] = -pull if pulls[j] is None else pulls[j] - pull
                if i < members:
                    length = square * root
                    apart = apart + (length + length if j < members else length)
        terms = apart * (-0.5 / (total_members - 1))
        for i in range(held):
            miss = values[i] - target
            square = miss * miss + DELTA * DELTA
            root = lax.rsqrt(square)
            slope = miss * root - pulls[i] * (1.0 / (total_members - 1))
            slopes[i, pl.ds(start, step_rows), :] = jnp.where(valid, slope, 0.0)
            if i < members:
                terms = terms + square * root
        return total + jnp.where(valid, terms, 0.0)

    for k in range(n_member):
        pens[pl.ds(k * members, members)] = ens[k].astype(F32).reshape(members, points, LANES)
    terms = lax.fori_loop(0, points // step_rows, crps, jnp.zeros((step_rows, LANES), F32))
    loss_part = jnp.sum(jnp.sum(terms, axis=1, keepdims=True), axis=0, keepdims=True)
    gradall[...] = slopes[...].reshape(held * points, LANES).astype(BF16)
    gradb[...] = gradall[pl.ds(0, flat), :]

    quads = LANES // 32
    tile_row = lax.broadcasted_iota(jnp.int32, (per, 32, LANES), 1)
    tile_at = my_part * per + lax.broadcasted_iota(jnp.int32, (per, 32, LANES), 0)
    variable = lax.rem(tile_at, quads) * 32 + tile_row
    spot = VARS % 32

    def split_loss(tiles):
        value = tiles[:, spot : spot + 1, :] + tiles[:, spot + 1 : spot + 2, :]
        high = value.astype(BF16).astype(F32)
        return jnp.where(
            variable == VARS, high, jnp.where(variable == VARS + 1, value - high, tiles)
        )

    row_all = lax.broadcasted_iota(jnp.int32, (LANES, 1), 0)
    loss_high = loss_part.astype(BF16).astype(F32)
    tail = jnp.where(
        row_all == VARS, loss_high, jnp.where(row_all == VARS + 1, loss_part - loss_high, 0.0)
    )
    for h in range(HALVES):
        for k in range(1, n_member):
            mix_copy(h, k).wait_recv()
    per_block = BLOCK // LANES
    for c in range(share):
        block = dot(gradall[...], mix[:, c].reshape(held * points, BLOCK), TN) + tail
        for b in range(per_block):
            for r in range(quads):
                u = (c * per_block + b) * quads + r
                local[u // per, u % per] = block[
                    r * 32 : (r + 1) * 32, b * LANES : (b + 1) * LANES
                ].astype(BF16)

    def part_copy(k):
        device, owner = part_peer(k)
        return pltpu.make_async_remote_copy(
            src_ref=local.at[owner],
            dst_ref=part.at[k],
            send_sem=part_s.at[k],
            recv_sem=part_r.at[k],
            device_id=device,
            device_id_type=MESH,
        )

    def plane_copy(k):
        return pltpu.make_async_remote_copy(
            src_ref=plane.at[me_z],
            dst_ref=plane.at[me_z],
            send_sem=plane_s.at[k],
            recv_sem=plane_r.at[k],
            device_id=plane_peer(k),
            device_id_type=MESH,
        )

    def area_peer(k):
        m = lax.rem(me_m + k // n_y, n_member)
        y = lax.rem(me_y + lax.rem(k, n_y), n_y)
        return m, y

    def full_copy(k):
        m, y = area_peer(k)
        return pltpu.make_async_remote_copy(
            src_ref=full.at[mine],
            dst_ref=full.at[mine],
            send_sem=full_s.at[k],
            recv_sem=full_r.at[k],
            device_id=(m, grid_at(y, me_z, core)),
            device_id_type=MESH,
        )

    def pass_copy(k):
        m = lax.rem(me_m + n_member - k // n_y, n_member)
        y = lax.rem(me_y + n_y - k % n_y, n_y)
        slot = (m * n_y + y) * n_core + core
        return pltpu.make_async_remote_copy(
            src_ref=full.at[slot],
            dst_ref=full.at[slot],
            send_sem=pass_s.at[k],
            recv_sem=pass_r.at[k],
            device_id=(me_m, grid_at(me_y, me_z, lax.rem(core + 1, n_core))),
            device_id_type=MESH,
        )

    def apart_by(k):
        return ring(k // n_y, n_member) + ring(k % n_y, n_y)

    area = n_member * n_y
    far_first = sorted(range(1, area), key=lambda k: -apart_by(k))

    def each(count, make, act):
        def step(k, c):
            getattr(make(k), act)()
            return c

        lax.fori_loop(1, count, step, 0)

    for k in range(parts - 1, 0, -1):
        part_copy(k).start()

    for c in range(chunks):
        here = pl.ds(c * BLOCK, BLOCK)
        step = dot(gradb[...], wpad[:, here], NN)
        dmixed[:, here] = step
        dmixedb[:, here] = step.astype(BF16)
    for c in range(chunks):
        here = pl.ds(c * BLOCK, BLOCK)
        dattn[:, here] = dot(dmixedb[...], wout[here, :], NT).astype(BF16)

    scale = (width // HEADS) ** -0.5

    def backward(m, carry):
        rows = pl.ds(pl.multiple_of(m * points, points), points)
        number = cnt[...]
        outs = [spread_heads(dattn[rows, here]) for here in heres]
        dprobs = [dot(kv[m, :, there], out, NT) for there, out in zip(theres, outs)]
        shares = [probs[m, h] for h in pack_range]
        leans = [
            jnp.sum(number * one * share, axis=0, keepdims=True)
            for one, share in zip(dprobs, shares)
        ]
        dscores = [
            (share * (one - lean)).astype(BF16) for share, one, lean in zip(shares, dprobs, leans)
        ]
        dscores = [(number * one.astype(F32)).astype(BF16) for one in dscores]
        weights = [(number * one.astype(BF16).astype(F32)).astype(BF16) for one in shares]
        dqs = [dot(one, kv[m, :, here], TN) for one, here in zip(dscores, heres)]
        dks = [
            dot(one, spread_heads(query[rows, here]), NN) for one, here in zip(dscores, heres)
        ]
        dvs = [dot(one, out, NN) for one, out in zip(weights, outs)]
        for h in pack_range:
            dquery[rows, heres[h]] = (pick_heads(dqs[h]) * scale).astype(BF16)
            dkv[m, :, heres[h]] = dks[h].astype(BF16)
            dkv[m, :, theres[h]] = dvs[h].astype(BF16)
        return carry

    lax.fori_loop(0, members, backward, 0)

    def back_copy(side, c):
        return pltpu.make_async_remote_copy(
            src_ref=dsend.at[side, c],
            dst_ref=drecv.at[side, c],
            send_sem=back_s.at[side, c],
            recv_sem=back_r.at[side, c],
            device_id=(me_m, down if side == 0 else up),
            device_id_type=MESH,
        )

    def second_stage():
        each(parts, part_copy, "wait_recv")
        piece_sum = local[my_part].astype(F32)
        for k in range(1, parts):
            piece_sum = piece_sum + part[k].astype(F32)
        plane[me_z] = split_loss(piece_sum).astype(BF16)
        for k in sorted(range(1, n_z), key=lambda k: -min(k, n_z - k)):
            plane_copy(k).start()

    for c in range(chunks):
        here = pl.ds(c * BLOCK, BLOCK)
        rows = dkv[...].reshape(members * window, 2 * width)
        step = dot(rows, wqkv[here, pl.ds(width, 2 * width)], NT)
        step = step.reshape(members, window, BLOCK)
        for side, start in ((0, 0), (1, 2 * points)):
            dsend[side, c] = step[:, start : start + points].astype(BF16)
        if c == chunks // 2 - 1:
            second_stage()
        if c >= chunks // 2 - 1:
            for ready in range(c + 1) if c == chunks // 2 - 1 else (c,):
                back_copy(0, ready).start()
                back_copy(1, ready).start()
        dhid[:, :, here] = step[:, points : 2 * points]

    for c in range(chunks):
        here = pl.ds(c * BLOCK, BLOCK)
        step = dot(dquery[...], wqkv[here, pl.ds(0, width)], NT)
        dhid[:, :, here] = dhid[:, :, here] + step.reshape(members, points, BLOCK)

    each(n_z, plane_copy, "wait_recv")
    plane_sum = plane[0].astype(F32)
    for k in range(1, n_z):
        plane_sum = plane_sum + plane[k].astype(F32)
    full[mine] = (split_loss(plane_sum) * (1.0 / (points * n_grid))).astype(BF16)
    for k in far_first:
        full_copy(k).start()
    pass_copy(0).start()
    for c in range(chunks):
        here = pl.ds(c * BLOCK, BLOCK)
        for side in range(2):
            back_copy(side, c).wait_recv()
        extra = drecv[0, c].astype(F32) + drecv[1, c].astype(F32)
        dhid[:, :, here] = dhid[:, :, here] + extra

    for m in range(members):
        dnormed = dhid[m] * gain[...]
        norm = normed[m]
        first = jnp.mean(dnormed, axis=-1, keepdims=True)
        second = jnp.mean(dnormed * norm, axis=-1, keepdims=True)
        dstates = inverse[m] * (dnormed - first - norm * second)
        grad[m] = (dstates + dmixed[pl.ds(m * points, points), :]).astype(BF16)

    for k in reversed(far_first):
        full_copy(k).wait_recv()
        pass_copy(k).start()
    for k in range(area):
        pass_copy(k).wait_recv()
    total = jnp.zeros((1, 1), F32)
    for m in range(n_member):
        for u in range(parts * per):
            b, r = m * (bands // n_member) + u // quads, u % quads
            tile = full[m * parts + u // per, u % per].astype(F32)
            count = min(32, VARS - 32 * r)
            head_out[pl.ds(32 * r, count), pl.ds(b * LANES, LANES)] = tile[:count]
            if u == VARS // 32:
                total = total + tile[spot : spot + 1, 0:1] + tile[spot + 1 : spot + 2, 0:1]
    loss[...] = total * (1.0 / (VARS * total_members))

    for h in range(HALVES):
        for copy in halo[h]:
            copy.wait_send()
        for k in range(1, n_member):
            pred_copy(h, k).wait_send()
            mix_copy(h, k).wait_send()
    each(parts, part_copy, "wait_send")
    each(n_z, plane_copy, "wait_send")
    for k in range(area):
        pass_copy(k).wait_send()
    each(area, full_copy, "wait_send")
    for c in range(chunks):
        for side in range(2):
            back_copy(side, c).wait_send()


def results(loss, grad, head, loss_hbm, grad_hbm, head_hbm, sem):
    copies = [
        pltpu.make_async_copy(source, target, sem.at[i])
        for i, (source, target) in enumerate(((grad, grad_hbm), (head, head_hbm), (loss, loss_hbm)))
    ]
    for copy in copies:
        copy.start()
    for copy in copies:
        copy.wait()


def body(sizes, states, ln_gain, w_qkv, w_out, w_head, targets, neighbours, counts):
    n_member, n_y, n_z, n_core = sizes
    members, points, width = states.shape
    flat = members * points
    window = 3 * points
    group = n_member * n_y * n_core
    chunks = width // BLOCK
    cols = PACK * (width // HEADS)
    tiles = (LANES // 32) * (width // LANES)
    per = tiles // group
    vmem = pl.BlockSpec(memory_space=pltpu.VMEM)
    hbm = pl.BlockSpec(memory_space=pl.ANY)
    dma = pltpu.SemaphoreType.DMA
    operands = (states, ln_gain.reshape(1, width), w_qkv, w_out, w_head.T, targets, neighbours, counts)
    loss, grad, head = pl.pallas_call(
        functools.partial(kernel, sizes),
        out_shape=(
            jax.ShapeDtypeStruct((1, 1), F32),
            jax.ShapeDtypeStruct((members, points, width), BF16),
            jax.ShapeDtypeStruct((VARS, width), F32),
        ),
        in_specs=[hbm] * 8,
        out_specs=(vmem, vmem, vmem),
        scratch_shapes=[
            pltpu.VMEM((members, points, width), BF16),
            pltpu.VMEM((1, width), F32),
            pltpu.VMEM((width, 3 * width), BF16),
            pltpu.VMEM((width, width), BF16),
            pltpu.VMEM((VARS, width), BF16),
            pltpu.VMEM((points, VARS), F32),
            pltpu.SMEM(neighbours.shape, jnp.int32),
            pltpu.SMEM((1,), jnp.int32),
            pltpu.VMEM((LANES, width), BF16),
            pltpu.VMEM((points, LANES), F32),
            pltpu.VMEM((flat, width), BF16),
            pltpu.VMEM((2, flat, width), BF16),
            pltpu.VMEM((flat, width), BF16),
            pltpu.VMEM((members, window, 2 * width), BF16),
            pltpu.VMEM((members, points, width), F32),
            pltpu.VMEM((members, points, 1), F32),
            pltpu.VMEM((window, LANES), F32),
            pltpu.VMEM((PACK * points, cols), F32),
            pltpu.VMEM((members, HEADS // PACK, window, PACK * points), F32),
            pltpu.VMEM((flat, width), BF16),
            pltpu.VMEM((chunks, flat, BLOCK), BF16),
            pltpu.VMEM((n_member, chunks // n_member, flat, BLOCK), BF16),
            pltpu.VMEM((n_member, flat, LANES), BF16),
            pltpu.VMEM((n_member * members, points, LANES), F32),
            pltpu.VMEM((n_member * members, points, LANES), F32),
            pltpu.VMEM((n_member * flat, LANES), BF16),
            pltpu.VMEM((flat, LANES), BF16),
            pltpu.VMEM((n_y * n_core, per, 32, LANES), BF16),
            pltpu.VMEM((n_y * n_core, per, 32, LANES), BF16),
            pltpu.VMEM((n_z, per, 32, LANES), BF16),
            pltpu.VMEM((group, per, 32, LANES), BF16),
            pltpu.VMEM((flat, width), F32),
            pltpu.VMEM((flat, width), BF16),
            pltpu.VMEM((flat, width), BF16),
            pltpu.VMEM((flat, width), BF16),
            pltpu.VMEM((members, window, 2 * width), BF16),
            pltpu.VMEM((2, chunks, members, points, BLOCK), BF16),
            pltpu.VMEM((2, chunks, members, points, BLOCK), BF16),
            pltpu.VMEM((members, points, width), F32),
            dma((6,)),
            dma((3 * width // (2 * BLOCK) + 1,)),
            dma((HALVES, 2)),
            dma((HALVES, 2)),
            dma((HALVES, n_member)),
            dma((HALVES, n_member)),
            dma((HALVES, n_member)),
            dma((HALVES, n_member)),
            dma((n_y * n_core,)),
            dma((n_y * n_core,)),
            dma((n_z,)),
            dma((n_z,)),
            dma((n_member * n_y,)),
            dma((n_member * n_y,)),
            dma((n_member * n_y,)),
            dma((n_member * n_y,)),
            dma((2, chunks)),
            dma((2, chunks)),
        ],
        compiler_params=pltpu.CompilerParams(
            collective_id=0, has_side_effects=True, vmem_limit_bytes=VMEM_BYTES
        ),
    )(*(pltpu.with_memory_space_constraint(x, pltpu.HBM) for x in operands[:-1]), operands[-1])
    held = [loss, *(pltpu.with_memory_space_constraint(x, pltpu.VMEM) for x in (grad, head))]
    loss, grad, head = pl.pallas_call(
        results,
        out_shape=tuple(jax.ShapeDtypeStruct(x.shape, x.dtype) for x in held),
        in_specs=[hbm] * 3,
        out_specs=(hbm,) * 3,
        scratch_shapes=[dma((3,))],
    )(*held)
    return (loss.reshape(()), grad, head.T)


def solution(mesh):
    placed = (
        P("member", "grid", None),
        P(),
        P(),
        P(),
        P(),
        P("grid", None),
        P("grid", None),
        P("grid"),
    )
    n_core = 2
    n_z = min(8, mesh.shape["grid"] // n_core)
    sizes = (mesh.shape["member"], mesh.shape["grid"] // (n_z * n_core), n_z, n_core)
    return jax.shard_map(
        functools.partial(body, sizes),
        mesh=mesh,
        in_specs=placed,
        out_specs=(P(), P("member", "grid", None), P()),
        check_vma=False,
    )
```

```python
import functools

import jax
import jax.numpy as jnp
from jax import lax
from jax.experimental import pallas as pl
from jax.experimental.pallas import tpu as pltpu
from jax.sharding import PartitionSpec as P

HEADS = 16
VARS = 100
TILE = 16
EPS = 1e-05
DELTA = 0.1
LANES = 128
PACK = 4
SPLIT = (2, 2)
HALVES = len(SPLIT)
RELAYS = 3
VMEM_BYTES = 40 * 1024 * 1024
BLOCK = 256
MESH = pl.DeviceIdType.MESH
F32 = jnp.float32
BF16 = jnp.bfloat16

NN = (((1,), (0,)), ((), ()))
NT = (((1,), (1,)), ((), ()))
TN = (((0,), (0,)), ((), ()))


def dot(a, b, dims):
    return lax.dot_general(a, b, dims, preferred_element_type=F32)


def kernel(
    sizes,
    states_hbm,
    gain_hbm,
    wqkv_hbm,
    wout_hbm,
    whead_hbm,
    targets_hbm,
    neighbours_hbm,
    counts_hbm,
    loss,
    grad,
    head_out,
    states,
    gain,
    wqkv,
    wout,
    whead,
    targets,
    neighbours,
    counts,
    wpad,
    tpad,
    hidden,
    beside,
    query,
    kv,
    normed,
    inverse,
    cnt,
    hmask,
    probs,
    attn,
    mixed,
    mix,
    ens,
    pens,
    slopes,
    gradall,
    gradb,
    local,
    part,
    plane,
    full,
    dmixed,
    dmixedb,
    dattn,
    dquery,
    dkv,
    dsend,
    drecv,
    dhid,
    relay,
    insem,
    wsem,
    halo_s,
    halo_r,
    pred_s,
    pred_r,
    mix_s,
    mix_r,
    part_s,
    part_r,
    plane_s,
    plane_r,
    full_s,
    full_r,
    pass_s,
    pass_r,
    back_s,
    back_r,
):
    n_member, n_y, n_z, n_core = sizes
    n_grid = n_y * n_z * n_core
    group = n_member * n_y * n_core
    members, points, width = states.shape
    window = kv.shape[1]
    flat = members * points
    cols = PACK * (width // HEADS)
    chunks = width // BLOCK
    packs = HEADS // PACK
    total_members = members * n_member
    per = local.shape[1]
    bands = width // LANES
    parts = n_y * n_core
    held = n_member * members

    me_m = lax.axis_index("member")
    me_g = lax.axis_index("grid")
    core = lax.rem(me_g, n_core)
    me_z = lax.rem(me_g // n_core, n_z)
    me_y = me_g // (n_core * n_z)
    up = lax.rem(me_g + 1, n_grid)
    down = lax.rem(me_g + n_grid - 1, n_grid)
    my_part = me_y * n_core + core
    mine = me_m * parts + my_part

    def grid_at(y, z, c):
        return (y * n_z + z) * n_core + c

    def group_peer(k):
        m = lax.rem(me_m + k // (n_y * n_core), n_member)
        y = lax.rem(me_y + lax.rem(k // n_core, n_y), n_y)
        c = lax.rem(core + lax.rem(k, n_core), n_core)
        return (m, grid_at(y, me_z, c))

    def part_peer(k):
        y = lax.rem(me_y + k // n_core, n_y)
        c = lax.rem(core + lax.rem(k, n_core), n_core)
        return (me_m, grid_at(y, me_z, c)), y * n_core + c

    def plane_peer(k):
        return (me_m, grid_at(me_y, lax.rem(me_z + k, n_z), core))

    def ring(k, n):
        return min(k, n - k)

    def around(n):
        return (1, n - 1) if n > 2 else (1,) * (n - 1)

    neighbours_of = [(me_m, up), (me_m, down)]
    neighbours_of += [(lax.rem(me_m + k, n_member), me_g) for k in around(n_member)]
    neighbours_of += [(me_m, grid_at(lax.rem(me_y + k, n_y), me_z, core)) for k in around(n_y)]
    neighbours_of += [(me_m, grid_at(me_y, lax.rem(me_z + k, n_z), core)) for k in around(n_z)]

    def tell(semaphore):
        for device in neighbours_of:
            pl.semaphore_signal(semaphore, inc=1, device_id=device, device_id_type=MESH)

    def heard(semaphore):
        pl.semaphore_wait(semaphore, len(neighbours_of))

    barrier = pltpu.get_barrier_semaphore()
    tell(barrier)

    wide = 2 * BLOCK
    n_wide = 3 * width // wide
    small_copies = [
        pltpu.make_async_copy(source, target, insem.at[i])
        for i, (source, target) in enumerate(
            (
                (states_hbm, states),
                (gain_hbm, gain),
                (neighbours_hbm, neighbours),
                (counts_hbm, counts),
                (whead_hbm, whead),
                (targets_hbm, targets),
            )
        )
    ]
    weight_copies = [
        pltpu.make_async_copy(
            wqkv_hbm.at[:, pl.ds(c * wide, wide)], wqkv.at[:, pl.ds(c * wide, wide)], wsem.at[c]
        )
        for c in range(n_wide)
    ]
    weight_copies.append(pltpu.make_async_copy(wout_hbm, wout, wsem.at[n_wide]))
    for copy in small_copies + weight_copies:
        copy.start()
    small_copies[0].wait()
    small_copies[1].wait()

    for m in range(members):
        values = states[m].astype(F32)
        centre = jnp.mean(values, axis=-1, keepdims=True)
        centred = values - centre
        spread = jnp.mean(centred * centred, axis=-1, keepdims=True)
        inv = lax.rsqrt(spread + EPS)
        norm = centred * inv
        normed[m] = norm
        inverse[m] = inv
        hidden[pl.ds(m * points, points), :] = (norm * gain[...]).astype(BF16)

    heard(barrier)

    firsts = [sum(SPLIT[:h]) for h in range(HALVES)]
    band_rows = [pl.ds(first * points, some * points) for first, some in zip(firsts, SPLIT)]
    halo = [
        [
            pltpu.make_async_remote_copy(
                src_ref=hidden.at[rows],
                dst_ref=beside.at[i, rows],
                send_sem=halo_s.at[h, i],
                recv_sem=halo_r.at[h, i],
                device_id=(me_m, side),
                device_id_type=MESH,
            )
            for i, side in enumerate((up, down))
        ]
        for h, rows in enumerate(band_rows)
    ]
    for pair in halo:
        for copy in pair:
            copy.start()
    tell(relay.at[0])

    for copy in small_copies[2:]:
        copy.wait()

    key_tile = 2 * me_g - 2 + lax.broadcasted_iota(jnp.int32, (window, LANES), 0) // TILE
    lane = lax.broadcasted_iota(jnp.int32, (window, LANES), 1)
    query_tile = lax.rem(lane, points) // TILE
    number = jnp.zeros((window, LANES), F32)
    for t in range(points // TILE):
        for e in range(neighbours.shape[1]):
            hit = (key_tile == neighbours[t, e]) & (query_tile == t)
            number = number + jnp.where(hit, 1.0, 0.0)
    cnt[...] = number
    rows_i = lax.broadcasted_iota(jnp.int32, (PACK * points, cols), 0) // points
    cols_i = lax.broadcasted_iota(jnp.int32, (PACK * points, cols), 1) // (cols // PACK)
    hmask[...] = jnp.where(rows_i == cols_i, 1.0, 0.0)
    wpad[...] = jnp.zeros_like(wpad)
    wpad[pl.ds(0, VARS), :] = whead[...]
    tpad[...] = jnp.zeros_like(tpad)
    tpad[:, pl.ds(0, VARS)] = targets[...]

    for c in range(n_wide):
        weight_copies[c].wait()
        step = dot(hidden[...], wqkv[:, pl.ds(c * wide, wide)], NN).astype(BF16)
        if c * wide < width:
            query[:, pl.ds(c * wide, wide)] = step * jnp.asarray((width // HEADS) ** -0.5, BF16)
        else:
            there = pl.ds(c * wide - width, wide)
            kv[:, pl.ds(points, points), there] = step.reshape(members, points, wide)

    heard(relay.at[0])
    tell(relay.at[1])

    def spread_heads(rows):
        return jnp.concatenate([rows] * PACK, axis=0) * hmask[...].astype(BF16)

    def pick_heads(rows):
        rows = rows * hmask[...]
        return jnp.sum(rows.reshape(PACK, points, cols), axis=0)

    pack_range = range(packs)
    heres = [pl.ds(h * cols, cols) for h in pack_range]
    theres = [pl.ds(width + h * cols, cols) for h in pack_range]

    share = chunks // n_member

    def mix_copy(h, k):
        return pltpu.make_async_remote_copy(
            src_ref=mixed.at[pl.ds(lax.rem(me_m + k, n_member) * share, share), band_rows[h]],
            dst_ref=mix.at[k, :, band_rows[h]],
            send_sem=mix_s.at[h, k],
            recv_sem=mix_r.at[h, k],
            device_id=(lax.rem(me_m + k, n_member), me_g),
            device_id_type=MESH,
        )

    def pred_copy(h, k):
        return pltpu.make_async_remote_copy(
            src_ref=ens.at[0, band_rows[h]],
            dst_ref=ens.at[k, band_rows[h]],
            send_sem=pred_s.at[h, k],
            recv_sem=pred_r.at[h, k],
            device_id=(lax.rem(me_m + k, n_member), me_g),
            device_id_type=MESH,
        )

    far_members = sorted(range(1, n_member), key=lambda k: -min(k, n_member - k))
    number = cnt[...]
    for h, (first, some) in enumerate(zip(firsts, SPLIT)):
        for copy in halo[h]:
            copy.wait_recv()
        near = beside[:, band_rows[h], :].reshape(2 * some * points, width)
        group_members = pl.ds(first, some)
        for c in range(2 * width // wide):
            here = pl.ds(c * wide, wide)
            step = dot(near, wqkv[:, pl.ds(width + c * wide, wide)], NN)
            step = step.astype(BF16).reshape(2, some, points, wide)
            kv[group_members, pl.ds(0, points), here] = step[0]
            kv[group_members, pl.ds(2 * points, points), here] = step[1]

        pairs = [(m, p) for m in range(first, first + some) for p in pack_range]
        queries = [query[pl.ds(m * points, points), heres[p]] for m, p in pairs]
        scores = [dot(kv[m, :, heres[p]], spread_heads(q), NT) for (m, p), q in zip(pairs, queries)]
        scores = [jnp.where(number > 0.0, one, -3e38) for one in scores]
        tops = [jnp.max(one, axis=0, keepdims=True) for one in scores]
        expos = [jnp.exp(one - top) for one, top in zip(scores, tops)]
        totals = [jnp.sum(number * expo, axis=0, keepdims=True) for expo in expos]
        shares = [expo / total for expo, total in zip(expos, totals)]
        weights = [(number * one.astype(BF16).astype(F32)).astype(BF16) for one in shares]
        outs = [dot(one, kv[m, :, theres[p]], TN) for one, (m, p) in zip(weights, pairs)]
        for (m, p), one, out in zip(pairs, shares, outs):
            probs[m, p] = one
            attn[pl.ds(m * points, points), heres[p]] = pick_heads(out).astype(BF16)

        if h == 0:
            weight_copies[n_wide].wait()
        rows = band_rows[h]
        for k in (*far_members, 0):
            for c in range(share):
                block = lax.rem(me_m + k, n_member) * share + c
                here = pl.ds(pl.multiple_of(block * BLOCK, BLOCK), BLOCK)
                proj = dot(attn[rows, :], wout[:, here], NN)
                before = states[group_members, :, here].reshape(some * points, BLOCK).astype(F32)
                mixed[block, rows] = (before + proj).astype(BF16)
            if k != 0 and (h < HALVES - 1 or k == far_members[0]):
                mix_copy(h, k).start()
        pred = dot(mixed[0, rows], wpad[:, pl.ds(0, BLOCK)], NT)
        for c in range(1, chunks):
            pred = pred + dot(mixed[c, rows], wpad[:, pl.ds(c * BLOCK, BLOCK)], NT)
        ens[0, rows] = pred.astype(BF16)
        for k in far_members:
            pred_copy(h, k).start()
        if h == HALVES - 1:
            for k in far_members[1:]:
                mix_copy(h, k).start()
        if h == 0:
            heard(relay.at[1])
            tell(relay.at[2])
    mix[0] = mixed[pl.ds(me_m * share, share)]
    for h in range(HALVES):
        for k in range(1, n_member):
            pred_copy(h, k).wait_recv()

    step_rows = 8

    def crps(block, total):
        start = pl.multiple_of(block * step_rows, step_rows)
        row = start + lax.broadcasted_iota(jnp.int32, (step_rows, LANES), 0)
        column = lax.broadcasted_iota(jnp.int32, (step_rows, LANES), 1)
        valid = (row < counts[0]) & (column < VARS)
        target = tpad[pl.ds(start, step_rows), :]
        values = [pens[i, pl.ds(start, step_rows), :] for i in range(held)]
        pulls = [None] * held
        apart = jnp.zeros((step_rows, LANES), F32)
        for i in range(held):
            for j in range(i + 1, held):
                gap = values[i] - values[j]
                square = gap * gap + DELTA * DELTA
                root = lax.rsqrt(square)
                pull = gap * root
                pulls[i] = pull if pulls[i] is None else pulls[i] + pull
                pulls[j] = -pull if pulls[j] is None else pulls[j] - pull
                if i < members:
                    length = square * root
                    apart = apart + (length + length if j < members else length)
        terms = apart * (-0.5 / (total_members - 1))
        for i in range(held):
            miss = values[i] - target
            square = miss * miss + DELTA * DELTA
            root = lax.rsqrt(square)
            slope = miss * root - pulls[i] * (1.0 / (total_members - 1))
            slopes[i, pl.ds(start, step_rows), :] = jnp.where(valid, slope, 0.0)
            if i < members:
                terms = terms + square * root
        return total + jnp.where(valid, terms, 0.0)

    for k in range(n_member):
        pens[pl.ds(k * members, members)] = ens[k].astype(F32).reshape(members, points, LANES)
    terms = lax.fori_loop(0, points // step_rows, crps, jnp.zeros((step_rows, LANES), F32))
    loss_part = jnp.sum(jnp.sum(terms, axis=1, keepdims=True), axis=0, keepdims=True)
    gradall[...] = slopes[...].reshape(held * points, LANES).astype(BF16)
    gradb[...] = gradall[pl.ds(0, flat), :]

    quads = LANES // 32
    tile_row = lax.broadcasted_iota(jnp.int32, (per, 32, LANES), 1)
    tile_at = my_part * per + lax.broadcasted_iota(jnp.int32, (per, 32, LANES), 0)
    variable = lax.rem(tile_at, quads) * 32 + tile_row
    spot = VARS % 32

    def split_loss(tiles):
        value = tiles[:, spot : spot + 1, :] + tiles[:, spot + 1 : spot + 2, :]
        high = value.astype(BF16).astype(F32)
        return jnp.where(
            variable == VARS, high, jnp.where(variable == VARS + 1, value - high, tiles)
        )

    row_all = lax.broadcasted_iota(jnp.int32, (LANES, 1), 0)
    loss_high = loss_part.astype(BF16).astype(F32)
    tail = jnp.where(
        row_all == VARS, loss_high, jnp.where(row_all == VARS + 1, loss_part - loss_high, 0.0)
    )
    for h in range(HALVES):
        for k in range(1, n_member):
            mix_copy(h, k).wait_recv()
    per_block = BLOCK // LANES
    for c in range(share):
        block = dot(gradall[...], mix[:, c].reshape(held * points, BLOCK), TN) + tail
        for b in range(per_block):
            for r in range(quads):
                u = (c * per_block + b) * quads + r
                local[u // per, u % per] = block[
                    r * 32 : (r + 1) * 32, b * LANES : (b + 1) * LANES
                ].astype(BF16)

    def part_copy(k):
        device, owner = part_peer(k)
        return pltpu.make_async_remote_copy(
            src_ref=local.at[owner],
            dst_ref=part.at[k],
            send_sem=part_s.at[k],
            recv_sem=part_r.at[k],
            device_id=device,
            device_id_type=MESH,
        )

    def plane_copy(k):
        return pltpu.make_async_remote_copy(
            src_ref=plane.at[me_z],
            dst_ref=plane.at[me_z],
            send_sem=plane_s.at[k],
            recv_sem=plane_r.at[k],
            device_id=plane_peer(k),
            device_id_type=MESH,
        )

    def area_peer(k):
        m = lax.rem(me_m + k // n_y, n_member)
        y = lax.rem(me_y + lax.rem(k, n_y), n_y)
        return m, y

    def full_copy(k):
        m, y = area_peer(k)
        return pltpu.make_async_remote_copy(
            src_ref=full.at[mine],
            dst_ref=full.at[mine],
            send_sem=full_s.at[k],
            recv_sem=full_r.at[k],
            device_id=(m, grid_at(y, me_z, core)),
            device_id_type=MESH,
        )

    def pass_copy(k):
        m = lax.rem(me_m + n_member - k // n_y, n_member)
        y = lax.rem(me_y + n_y - k % n_y, n_y)
        slot = (m * n_y + y) * n_core + core
        return pltpu.make_async_remote_copy(
            src_ref=full.at[slot],
            dst_ref=full.at[slot],
            send_sem=pass_s.at[k],
            recv_sem=pass_r.at[k],
            device_id=(me_m, grid_at(me_y, me_z, lax.rem(core + 1, n_core))),
            device_id_type=MESH,
        )

    def apart_by(k):
        return ring(k // n_y, n_member) + ring(k % n_y, n_y)

    area = n_member * n_y
    far_first = sorted(range(1, area), key=lambda k: -apart_by(k))

    def each(count, make, act):
        def step(k, c):
            getattr(make(k), act)()
            return c

        lax.fori_loop(1, count, step, 0)

    for k in range(parts - 1, 0, -1):
        part_copy(k).start()

    for c in range(chunks):
        here = pl.ds(c * BLOCK, BLOCK)
        step = dot(gradb[...], wpad[:, here], NN)
        dmixed[:, here] = step
        dmixedb[:, here] = step.astype(BF16)
    for c in range(chunks):
        here = pl.ds(c * BLOCK, BLOCK)
        dattn[:, here] = dot(dmixedb[...], wout[here, :], NT).astype(BF16)

    scale = (width // HEADS) ** -0.5

    def backward(m, carry):
        rows = pl.ds(pl.multiple_of(m * points, points), points)
        number = cnt[...]
        outs = [spread_heads(dattn[rows, here]) for here in heres]
        dprobs = [dot(kv[m, :, there], out, NT) for there, out in zip(theres, outs)]
        shares = [probs[m, h] for h in pack_range]
        leans = [
            jnp.sum(number * one * share, axis=0, keepdims=True)
            for one, share in zip(dprobs, shares)
        ]
        dscores = [
            (share * (one - lean)).astype(BF16) for share, one, lean in zip(shares, dprobs, leans)
        ]
        dscores = [(number * one.astype(F32)).astype(BF16) for one in dscores]
        weights = [(number * one.astype(BF16).astype(F32)).astype(BF16) for one in shares]
        dqs = [dot(one, kv[m, :, here], TN) for one, here in zip(dscores, heres)]
        dks = [
            dot(one, spread_heads(query[rows, here]), NN) for one, here in zip(dscores, heres)
        ]
        dvs = [dot(one, out, NN) for one, out in zip(weights, outs)]
        for h in pack_range:
            dquery[rows, heres[h]] = (pick_heads(dqs[h]) * scale).astype(BF16)
            dkv[m, :, heres[h]] = dks[h].astype(BF16)
            dkv[m, :, theres[h]] = dvs[h].astype(BF16)
        return carry

    lax.fori_loop(0, members, backward, 0)

    def back_copy(side, c):
        return pltpu.make_async_remote_copy(
            src_ref=dsend.at[side, c],
            dst_ref=drecv.at[side, c],
            send_sem=back_s.at[side, c],
            recv_sem=back_r.at[side, c],
            device_id=(me_m, down if side == 0 else up),
            device_id_type=MESH,
        )

    def second_stage():
        each(parts, part_copy, "wait_recv")
        piece_sum = local[my_part].astype(F32)
        for k in range(1, parts):
            piece_sum = piece_sum + part[k].astype(F32)
        plane[me_z] = split_loss(piece_sum).astype(BF16)
        heard(relay.at[2])
        for k in sorted(range(1, n_z), key=lambda k: -min(k, n_z - k)):
            plane_copy(k).start()

    for c in range(chunks):
        here = pl.ds(c * BLOCK, BLOCK)
        rows = dkv[...].reshape(members * window, 2 * width)
        step = dot(rows, wqkv[here, pl.ds(width, 2 * width)], NT)
        step = step.reshape(members, window, BLOCK)
        for side, start in ((0, 0), (1, 2 * points)):
            dsend[side, c] = step[:, start : start + points].astype(BF16)
        if c == chunks // 2 - 1:
            second_stage()
        if c >= chunks // 2 - 1:
            for ready in range(c + 1) if c == chunks // 2 - 1 else (c,):
                back_copy(0, ready).start()
                back_copy(1, ready).start()
        dhid[:, :, here] = step[:, points : 2 * points]

    for c in range(chunks):
        here = pl.ds(c * BLOCK, BLOCK)
        step = dot(dquery[...], wqkv[here, pl.ds(0, width)], NT)
        dhid[:, :, here] = dhid[:, :, here] + step.reshape(members, points, BLOCK)

    each(n_z, plane_copy, "wait_recv")
    plane_sum = plane[0].astype(F32)
    for k in range(1, n_z):
        plane_sum = plane_sum + plane[k].astype(F32)
    full[mine] = (split_loss(plane_sum) * (1.0 / (points * n_grid))).astype(BF16)
    for k in far_first:
        full_copy(k).start()
    pass_copy(0).start()
    for c in range(chunks):
        here = pl.ds(c * BLOCK, BLOCK)
        for side in range(2):
            back_copy(side, c).wait_recv()
        extra = drecv[0, c].astype(F32) + drecv[1, c].astype(F32)
        dhid[:, :, here] = dhid[:, :, here] + extra

    for m in range(members):
        dnormed = dhid[m] * gain[...]
        norm = normed[m]
        first = jnp.mean(dnormed, axis=-1, keepdims=True)
        second = jnp.mean(dnormed * norm, axis=-1, keepdims=True)
        dstates = inverse[m] * (dnormed - first - norm * second)
        grad[m] = (dstates + dmixed[pl.ds(m * points, points), :]).astype(BF16)

    for k in reversed(far_first):
        full_copy(k).wait_recv()
        pass_copy(k).start()
    for k in range(area):
        pass_copy(k).wait_recv()
    total = jnp.zeros((1, 1), F32)
    for m in range(n_member):
        for u in range(parts * per):
            b, r = m * (bands // n_member) + u // quads, u % quads
            tile = full[m * parts + u // per, u % per].astype(F32)
            count = min(32, VARS - 32 * r)
            head_out[pl.ds(32 * r, count), pl.ds(b * LANES, LANES)] = tile[:count]
            if u == VARS // 32:
                total = total + tile[spot : spot + 1, 0:1] + tile[spot + 1 : spot + 2, 0:1]
    loss[...] = total * (1.0 / (VARS * total_members))

    for h in range(HALVES):
        for copy in halo[h]:
            copy.wait_send()
        for k in range(1, n_member):
            pred_copy(h, k).wait_send()
            mix_copy(h, k).wait_send()
    each(parts, part_copy, "wait_send")
    each(n_z, plane_copy, "wait_send")
    for k in range(area):
        pass_copy(k).wait_send()
    each(area, full_copy, "wait_send")
    for c in range(chunks):
        for side in range(2):
            back_copy(side, c).wait_send()


def results(loss, grad, head, loss_hbm, grad_hbm, head_hbm, sem):
    copies = [
        pltpu.make_async_copy(source, target, sem.at[i])
        for i, (source, target) in enumerate(((grad, grad_hbm), (head, head_hbm), (loss, loss_hbm)))
    ]
    for copy in copies:
        copy.start()
    for copy in copies:
        copy.wait()


def body(sizes, states, ln_gain, w_qkv, w_out, w_head, targets, neighbours, counts):
    n_member, n_y, n_z, n_core = sizes
    members, points, width = states.shape
    flat = members * points
    window = 3 * points
    group = n_member * n_y * n_core
    chunks = width // BLOCK
    cols = PACK * (width // HEADS)
    tiles = (LANES // 32) * (width // LANES)
    per = tiles // group
    vmem = pl.BlockSpec(memory_space=pltpu.VMEM)
    hbm = pl.BlockSpec(memory_space=pl.ANY)
    dma = pltpu.SemaphoreType.DMA
    operands = (states, ln_gain.reshape(1, width), w_qkv, w_out, w_head.T, targets, neighbours, counts)
    loss, grad, head = pl.pallas_call(
        functools.partial(kernel, sizes),
        out_shape=(
            jax.ShapeDtypeStruct((1, 1), F32),
            jax.ShapeDtypeStruct((members, points, width), BF16),
            jax.ShapeDtypeStruct((VARS, width), F32),
        ),
        in_specs=[hbm] * 8,
        out_specs=(vmem, vmem, vmem),
        scratch_shapes=[
            pltpu.VMEM((members, points, width), BF16),
            pltpu.VMEM((1, width), F32),
            pltpu.VMEM((width, 3 * width), BF16),
            pltpu.VMEM((width, width), BF16),
            pltpu.VMEM((VARS, width), BF16),
            pltpu.VMEM((points, VARS), F32),
            pltpu.SMEM(neighbours.shape, jnp.int32),
            pltpu.SMEM((1,), jnp.int32),
            pltpu.VMEM((LANES, width), BF16),
            pltpu.VMEM((points, LANES), F32),
            pltpu.VMEM((flat, width), BF16),
            pltpu.VMEM((2, flat, width), BF16),
            pltpu.VMEM((flat, width), BF16),
            pltpu.VMEM((members, window, 2 * width), BF16),
            pltpu.VMEM((members, points, width), F32),
            pltpu.VMEM((members, points, 1), F32),
            pltpu.VMEM((window, LANES), F32),
            pltpu.VMEM((PACK * points, cols), F32),
            pltpu.VMEM((members, HEADS // PACK, window, PACK * points), F32),
            pltpu.VMEM((flat, width), BF16),
            pltpu.VMEM((chunks, flat, BLOCK), BF16),
            pltpu.VMEM((n_member, chunks // n_member, flat, BLOCK), BF16),
            pltpu.VMEM((n_member, flat, LANES), BF16),
            pltpu.VMEM((n_member * members, points, LANES), F32),
            pltpu.VMEM((n_member * members, points, LANES), F32),
            pltpu.VMEM((n_member * flat, LANES), BF16),
            pltpu.VMEM((flat, LANES), BF16),
            pltpu.VMEM((n_y * n_core, per, 32, LANES), BF16),
            pltpu.VMEM((n_y * n_core, per, 32, LANES), BF16),
            pltpu.VMEM((n_z, per, 32, LANES), BF16),
            pltpu.VMEM((group, per, 32, LANES), BF16),
            pltpu.VMEM((flat, width), F32),
            pltpu.VMEM((flat, width), BF16),
            pltpu.VMEM((flat, width), BF16),
            pltpu.VMEM((flat, width), BF16),
            pltpu.VMEM((members, window, 2 * width), BF16),
            pltpu.VMEM((2, chunks, members, points, BLOCK), BF16),
            pltpu.VMEM((2, chunks, members, points, BLOCK), BF16),
            pltpu.VMEM((members, points, width), F32),
            pltpu.SemaphoreType.REGULAR((RELAYS,)),
            dma((6,)),
            dma((3 * width // (2 * BLOCK) + 1,)),
            dma((HALVES, 2)),
            dma((HALVES, 2)),
            dma((HALVES, n_member)),
            dma((HALVES, n_member)),
            dma((HALVES, n_member)),
            dma((HALVES, n_member)),
            dma((n_y * n_core,)),
            dma((n_y * n_core,)),
            dma((n_z,)),
            dma((n_z,)),
            dma((n_member * n_y,)),
            dma((n_member * n_y,)),
            dma((n_member * n_y,)),
            dma((n_member * n_y,)),
            dma((2, chunks)),
            dma((2, chunks)),
        ],
        compiler_params=pltpu.CompilerParams(
            collective_id=0, has_side_effects=True, vmem_limit_bytes=VMEM_BYTES
        ),
    )(*(pltpu.with_memory_space_constraint(x, pltpu.HBM) for x in operands[:-1]), operands[-1])
    held = [loss, *(pltpu.with_memory_space_constraint(x, pltpu.VMEM) for x in (grad, head))]
    loss, grad, head = pl.pallas_call(
        results,
        out_shape=tuple(jax.ShapeDtypeStruct(x.shape, x.dtype) for x in held),
        in_specs=[hbm] * 3,
        out_specs=(hbm,) * 3,
        scratch_shapes=[dma((3,))],
    )(*held)
    return (loss.reshape(()), grad, head.T)


def solution(mesh):
    placed = (
        P("member", "grid", None),
        P(),
        P(),
        P(),
        P(),
        P("grid", None),
        P("grid", None),
        P("grid"),
    )
    n_core = 2
    n_z = min(8, mesh.shape["grid"] // n_core)
    sizes = (mesh.shape["member"], mesh.shape["grid"] // (n_z * n_core), n_z, n_core)
    return jax.shard_map(
        functools.partial(body, sizes),
        mesh=mesh,
        in_specs=placed,
        out_specs=(P(), P("member", "grid", None), P()),
        check_vma=False,
    )
```

```python
import functools

import jax
import jax.numpy as jnp
from jax import lax
from jax.experimental import pallas as pl
from jax.experimental.pallas import tpu as pltpu
from jax.sharding import PartitionSpec as P

HEADS = 16
VARS = 100
TILE = 16
EPS = 1e-05
DELTA = 0.1
LANES = 128
PACK = 4
HALVES = 2
RELAYS = 3
VMEM_BYTES = 40 * 1024 * 1024
BLOCK = 256
MESH = pl.DeviceIdType.MESH
F32 = jnp.float32
BF16 = jnp.bfloat16

NN = (((1,), (0,)), ((), ()))
NT = (((1,), (1,)), ((), ()))
TN = (((0,), (0,)), ((), ()))


def dot(a, b, dims):
    return lax.dot_general(a, b, dims, preferred_element_type=F32)


def kernel(
    sizes,
    states_hbm,
    gain_hbm,
    wqkv_hbm,
    wout_hbm,
    whead_hbm,
    targets_hbm,
    neighbours_hbm,
    counts_hbm,
    loss,
    grad,
    head_out,
    states,
    gain,
    wqkv,
    wout,
    whead,
    targets,
    neighbours,
    counts,
    wpad,
    tpad,
    hidden,
    beside,
    query,
    kv,
    normed,
    inverse,
    cnt,
    hmask,
    probs,
    attn,
    mixed,
    mix,
    ens,
    pens,
    slopes,
    gaps,
    gradall,
    gradb,
    local,
    part,
    plane,
    full,
    dmixed,
    dmixedb,
    dattn,
    dquery,
    dkv,
    dsend,
    drecv,
    dhid,
    relay,
    insem,
    wsem,
    halo_s,
    halo_r,
    pred_s,
    pred_r,
    mix_s,
    mix_r,
    part_s,
    part_r,
    plane_s,
    plane_r,
    full_s,
    full_r,
    pass_s,
    pass_r,
    back_s,
    back_r,
):
    n_member, n_y, n_z, n_core = sizes
    n_grid = n_y * n_z * n_core
    group = n_member * n_y * n_core
    members, points, width = states.shape
    window = kv.shape[1]
    flat = members * points
    cols = PACK * (width // HEADS)
    chunks = width // BLOCK
    packs = HEADS // PACK
    total_members = members * n_member
    per = local.shape[1]
    bands = width // LANES
    parts = n_y * n_core
    held = n_member * members

    me_m = lax.axis_index("member")
    me_g = lax.axis_index("grid")
    core = lax.rem(me_g, n_core)
    me_z = lax.rem(me_g // n_core, n_z)
    me_y = me_g // (n_core * n_z)
    up = lax.rem(me_g + 1, n_grid)
    down = lax.rem(me_g + n_grid - 1, n_grid)
    my_part = me_y * n_core + core
    mine = me_m * parts + my_part

    def grid_at(y, z, c):
        return (y * n_z + z) * n_core + c

    def group_peer(k):
        m = lax.rem(me_m + k // (n_y * n_core), n_member)
        y = lax.rem(me_y + lax.rem(k // n_core, n_y), n_y)
        c = lax.rem(core + lax.rem(k, n_core), n_core)
        return (m, grid_at(y, me_z, c))

    def part_peer(k):
        y = lax.rem(me_y + k // n_core, n_y)
        c = lax.rem(core + lax.rem(k, n_core), n_core)
        return (me_m, grid_at(y, me_z, c)), y * n_core + c

    def plane_peer(k):
        return (me_m, grid_at(me_y, lax.rem(me_z + k, n_z), core))

    def ring(k, n):
        return min(k, n - k)

    def around(n):
        return (1, n - 1) if n > 2 else (1,) * (n - 1)

    neighbours_of = [(me_m, up), (me_m, down)]
    neighbours_of += [(lax.rem(me_m + k, n_member), me_g) for k in around(n_member)]
    neighbours_of += [(me_m, grid_at(lax.rem(me_y + k, n_y), me_z, core)) for k in around(n_y)]
    neighbours_of += [(me_m, grid_at(me_y, lax.rem(me_z + k, n_z), core)) for k in around(n_z)]

    def tell(semaphore):
        for device in neighbours_of:
            pl.semaphore_signal(semaphore, inc=1, device_id=device, device_id_type=MESH)

    def heard(semaphore):
        pl.semaphore_wait(semaphore, len(neighbours_of))

    barrier = pltpu.get_barrier_semaphore()
    tell(barrier)

    wide = 2 * BLOCK
    n_wide = 3 * width // wide
    small_copies = [
        pltpu.make_async_copy(source, target, insem.at[i])
        for i, (source, target) in enumerate(
            (
                (states_hbm, states),
                (gain_hbm, gain),
                (neighbours_hbm, neighbours),
                (counts_hbm, counts),
                (whead_hbm, whead),
                (targets_hbm, targets),
            )
        )
    ]
    weight_copies = [
        pltpu.make_async_copy(
            wqkv_hbm.at[:, pl.ds(c * wide, wide)], wqkv.at[:, pl.ds(c * wide, wide)], wsem.at[c]
        )
        for c in range(n_wide)
    ]
    weight_copies.append(pltpu.make_async_copy(wout_hbm, wout, wsem.at[n_wide]))
    for copy in small_copies + weight_copies:
        copy.start()
    small_copies[0].wait()
    small_copies[1].wait()

    for m in range(members):
        values = states[m].astype(F32)
        centre = jnp.mean(values, axis=-1, keepdims=True)
        centred = values - centre
        spread = jnp.mean(centred * centred, axis=-1, keepdims=True)
        inv = lax.rsqrt(spread + EPS)
        norm = centred * inv
        normed[m] = norm
        inverse[m] = inv
        hidden[pl.ds(m * points, points), :] = (norm * gain[...]).astype(BF16)

    heard(barrier)

    some = members // HALVES

    def rows_of(h):
        return pl.ds(pl.multiple_of(h * (some * points), some * points), some * points)

    def halo_copy(h, i):
        return pltpu.make_async_remote_copy(
            src_ref=hidden.at[rows_of(h)],
            dst_ref=beside.at[i, rows_of(h)],
            send_sem=halo_s.at[h, i],
            recv_sem=halo_r.at[h, i],
            device_id=(me_m, (up, down)[i]),
            device_id_type=MESH,
        )

    for h in range(HALVES):
        for i in range(2):
            halo_copy(h, i).start()
    tell(relay.at[0])

    for copy in small_copies[2:]:
        copy.wait()

    key_tile = 2 * me_g - 2 + lax.broadcasted_iota(jnp.int32, (window, LANES), 0) // TILE
    lane = lax.broadcasted_iota(jnp.int32, (window, LANES), 1)
    query_tile = lax.rem(lane, points) // TILE
    number = jnp.zeros((window, LANES), F32)
    for t in range(points // TILE):
        for e in range(neighbours.shape[1]):
            hit = (key_tile == neighbours[t, e]) & (query_tile == t)
            number = number + jnp.where(hit, 1.0, 0.0)
    cnt[...] = number
    rows_i = lax.broadcasted_iota(jnp.int32, (PACK * points, cols), 0) // points
    cols_i = lax.broadcasted_iota(jnp.int32, (PACK * points, cols), 1) // (cols // PACK)
    hmask[...] = jnp.where(rows_i == cols_i, 1.0, 0.0)
    wpad[...] = jnp.zeros_like(wpad)
    wpad[pl.ds(0, VARS), :] = whead[...]
    tpad[...] = jnp.zeros_like(tpad)
    tpad[:, pl.ds(0, VARS)] = targets[...]

    for c in range(n_wide):
        weight_copies[c].wait()
        step = dot(hidden[...], wqkv[:, pl.ds(c * wide, wide)], NN).astype(BF16)
        if c * wide < width:
            query[:, pl.ds(c * wide, wide)] = step * jnp.asarray((width // HEADS) ** -0.5, BF16)
        else:
            there = pl.ds(c * wide - width, wide)
            kv[:, pl.ds(points, points), there] = step.reshape(members, points, wide)

    heard(relay.at[0])
    tell(relay.at[1])

    def spread_heads(rows):
        return jnp.concatenate([rows] * PACK, axis=0) * hmask[...].astype(BF16)

    def pick_heads(rows):
        rows = rows * hmask[...]
        return jnp.sum(rows.reshape(PACK, points, cols), axis=0)

    pack_range = range(packs)
    heres = [pl.ds(h * cols, cols) for h in pack_range]
    theres = [pl.ds(width + h * cols, cols) for h in pack_range]

    share = chunks // n_member

    def mix_copy(h, k):
        return pltpu.make_async_remote_copy(
            src_ref=mixed.at[pl.ds(lax.rem(me_m + k, n_member) * share, share), rows_of(h)],
            dst_ref=mix.at[k, :, rows_of(h)],
            send_sem=mix_s.at[h, k],
            recv_sem=mix_r.at[h, k],
            device_id=(lax.rem(me_m + k, n_member), me_g),
            device_id_type=MESH,
        )

    def pred_copy(h, k):
        return pltpu.make_async_remote_copy(
            src_ref=ens.at[0, rows_of(h)],
            dst_ref=ens.at[k, rows_of(h)],
            send_sem=pred_s.at[h, k],
            recv_sem=pred_r.at[h, k],
            device_id=(lax.rem(me_m + k, n_member), me_g),
            device_id_type=MESH,
        )

    far_members = sorted(range(1, n_member), key=lambda k: -min(k, n_member - k))
    number = cnt[...]

    def forward(h, carry):
        for i in range(2):
            halo_copy(h, i).wait_recv()
        first = h * some
        near = beside[:, rows_of(h), :].reshape(2 * some * points, width)
        group_members = pl.ds(first, some)
        for c in range(2 * width // wide):
            here = pl.ds(c * wide, wide)
            step = dot(near, wqkv[:, pl.ds(width + c * wide, wide)], NN)
            step = step.astype(BF16).reshape(2, some, points, wide)
            kv[group_members, pl.ds(0, points), here] = step[0]
            kv[group_members, pl.ds(2 * points, points), here] = step[1]

        pairs = [(first + m, p) for m in range(some) for p in pack_range]
        queries = [
            query[pl.ds(pl.multiple_of(m * points, points), points), heres[p]] for m, p in pairs
        ]
        scores = [dot(kv[m, :, heres[p]], spread_heads(q), NT) for (m, p), q in zip(pairs, queries)]
        scores = [jnp.where(number > 0.0, one, -3e38) for one in scores]
        tops = [jnp.max(one, axis=0, keepdims=True) for one in scores]
        expos = [jnp.exp(one - top) for one, top in zip(scores, tops)]
        totals = [jnp.sum(number * expo, axis=0, keepdims=True) for expo in expos]
        shares = [expo / total for expo, total in zip(expos, totals)]
        weights = [(number * one.astype(BF16).astype(F32)).astype(BF16) for one in shares]
        outs = [dot(one, kv[m, :, theres[p]], TN) for one, (m, p) in zip(weights, pairs)]
        for (m, p), one, out in zip(pairs, shares, outs):
            probs[m, p] = one
            there = pl.ds(pl.multiple_of(m * points, points), points)
            attn[there, heres[p]] = pick_heads(out).astype(BF16)

        @pl.when(h == 0)
        def _():
            weight_copies[n_wide].wait()

        rows = rows_of(h)
        for k in (*far_members, 0):
            for c in range(share):
                block = lax.rem(me_m + k, n_member) * share + c
                here = pl.ds(pl.multiple_of(block * BLOCK, BLOCK), BLOCK)
                proj = dot(attn[rows, :], wout[:, here], NN)
                before = states[group_members, :, here].reshape(some * points, BLOCK).astype(F32)
                mixed[block, rows] = (before + proj).astype(BF16)
        pred = dot(mixed[0, rows], wpad[:, pl.ds(0, BLOCK)], NT)
        for c in range(1, chunks):
            pred = pred + dot(mixed[c, rows], wpad[:, pl.ds(c * BLOCK, BLOCK)], NT)
        ens[0, rows] = pred.astype(BF16)
        for k in far_members:
            pred_copy(h, k).start()
        for k in far_members:
            mix_copy(h, k).start()

        @pl.when(h == 0)
        def _():
            heard(relay.at[1])
            tell(relay.at[2])

        return carry

    lax.fori_loop(0, HALVES, forward, 0)
    mix[0] = mixed[pl.ds(me_m * share, share)]

    step_rows = 8
    late = [i for i in range(held) if i >= members and i % members >= members - some]
    early = [i for i in range(held) if i not in late]
    everyone = [(i, j) for i in range(held) for j in range(i + 1, held)]
    early_pairs = [(i, j) for i, j in everyone if i not in late and j not in late]
    late_pairs = [pair for pair in everyone if pair not in early_pairs]

    def widen(k, first, count):
        rows = ens[k, pl.ds(first * points, count * points), :].astype(F32)
        pens[pl.ds(k * members + first, count)] = rows.reshape(count, points, LANES)

    def pair_sums(pairs, values, pulls, apart):
        for i, j in pairs:
            gap = values[i] - values[j]
            square = gap * gap + DELTA * DELTA
            root = lax.rsqrt(square)
            pull = gap * root
            pulls[i] = pull if pulls[i] is None else pulls[i] + pull
            pulls[j] = -pull if pulls[j] is None else pulls[j] - pull
            if i < members:
                length = square * root
                apart = apart + (length + length if j < members else length)
        return apart

    def crps_early(block, carry):
        here = pl.ds(pl.multiple_of(block * step_rows, step_rows), step_rows)
        values = {i: pens[i, here, :] for i in early}
        pulls = [None] * held
        gaps[here, :] = pair_sums(early_pairs, values, pulls, jnp.zeros((step_rows, LANES), F32))
        for i in early:
            slopes[i, here, :] = pulls[i]
        return carry

    def crps_late(block, total):
        start = pl.multiple_of(block * step_rows, step_rows)
        here = pl.ds(start, step_rows)
        row = start + lax.broadcasted_iota(jnp.int32, (step_rows, LANES), 0)
        column = lax.broadcasted_iota(jnp.int32, (step_rows, LANES), 1)
        valid = (row < counts[0]) & (column < VARS)
        target = tpad[here, :]
        values = [pens[i, here, :] for i in range(held)]
        pulls = [None if i in late else slopes[i, here, :] for i in range(held)]
        apart = pair_sums(late_pairs, values, pulls, gaps[here, :])
        terms = apart * (-0.5 / (total_members - 1))
        for i in range(held):
            miss = values[i] - target
            square = miss * miss + DELTA * DELTA
            root = lax.rsqrt(square)
            slope = miss * root - pulls[i] * (1.0 / (total_members - 1))
            slopes[i, here, :] = jnp.where(valid, slope, 0.0)
            if i < members:
                terms = terms + square * root
        return total + jnp.where(valid, terms, 0.0)

    for h in range(HALVES - 1):
        for k in range(1, n_member):
            pred_copy(h, k).wait_recv()
    widen(0, 0, members)
    for k in range(1, n_member):
        widen(k, 0, members - some)
    lax.fori_loop(0, points // step_rows, crps_early, 0)
    for k in range(1, n_member):
        pred_copy(HALVES - 1, k).wait_recv()
        widen(k, members - some, some)
    terms = lax.fori_loop(0, points // step_rows, crps_late, jnp.zeros((step_rows, LANES), F32))
    loss_part = jnp.sum(jnp.sum(terms, axis=1, keepdims=True), axis=0, keepdims=True)
    gradall[...] = slopes[...].reshape(held * points, LANES).astype(BF16)
    gradb[...] = gradall[pl.ds(0, flat), :]

    quads = LANES // 32
    tile_row = lax.broadcasted_iota(jnp.int32, (per, 32, LANES), 1)
    tile_at = my_part * per + lax.broadcasted_iota(jnp.int32, (per, 32, LANES), 0)
    variable = lax.rem(tile_at, quads) * 32 + tile_row
    spot = VARS % 32

    def split_loss(tiles):
        value = tiles[:, spot : spot + 1, :] + tiles[:, spot + 1 : spot + 2, :]
        high = value.astype(BF16).astype(F32)
        return jnp.where(
            variable == VARS, high, jnp.where(variable == VARS + 1, value - high, tiles)
        )

    row_all = lax.broadcasted_iota(jnp.int32, (LANES, 1), 0)
    loss_high = loss_part.astype(BF16).astype(F32)
    tail = jnp.where(
        row_all == VARS, loss_high, jnp.where(row_all == VARS + 1, loss_part - loss_high, 0.0)
    )
    for h in range(HALVES):
        for k in range(1, n_member):
            mix_copy(h, k).wait_recv()
    per_block = BLOCK // LANES
    for c in range(share):
        block = dot(gradall[...], mix[:, c].reshape(held * points, BLOCK), TN) + tail
        for b in range(per_block):
            for r in range(quads):
                u = (c * per_block + b) * quads + r
                local[u // per, u % per] = block[
                    r * 32 : (r + 1) * 32, b * LANES : (b + 1) * LANES
                ].astype(BF16)

    def part_copy(k):
        device, owner = part_peer(k)
        return pltpu.make_async_remote_copy(
            src_ref=local.at[owner],
            dst_ref=part.at[k],
            send_sem=part_s.at[k],
            recv_sem=part_r.at[k],
            device_id=device,
            device_id_type=MESH,
        )

    def plane_copy(k):
        return pltpu.make_async_remote_copy(
            src_ref=plane.at[me_z],
            dst_ref=plane.at[me_z],
            send_sem=plane_s.at[k],
            recv_sem=plane_r.at[k],
            device_id=plane_peer(k),
            device_id_type=MESH,
        )

    def area_peer(k):
        m = lax.rem(me_m + k // n_y, n_member)
        y = lax.rem(me_y + lax.rem(k, n_y), n_y)
        return m, y

    def full_copy(k):
        m, y = area_peer(k)
        return pltpu.make_async_remote_copy(
            src_ref=full.at[mine],
            dst_ref=full.at[mine],
            send_sem=full_s.at[k],
            recv_sem=full_r.at[k],
            device_id=(m, grid_at(y, me_z, core)),
            device_id_type=MESH,
        )

    def pass_copy(k):
        m = lax.rem(me_m + n_member - k // n_y, n_member)
        y = lax.rem(me_y + n_y - k % n_y, n_y)
        slot = (m * n_y + y) * n_core + core
        return pltpu.make_async_remote_copy(
            src_ref=full.at[slot],
            dst_ref=full.at[slot],
            send_sem=pass_s.at[k],
            recv_sem=pass_r.at[k],
            device_id=(me_m, grid_at(me_y, me_z, lax.rem(core + 1, n_core))),
            device_id_type=MESH,
        )

    def apart_by(k):
        return ring(k // n_y, n_member) + ring(k % n_y, n_y)

    area = n_member * n_y
    far_first = sorted(range(1, area), key=lambda k: -apart_by(k))

    def each(count, make, act):
        def step(k, c):
            getattr(make(k), act)()
            return c

        lax.fori_loop(1, count, step, 0)

    for k in range(parts - 1, 0, -1):
        part_copy(k).start()

    for c in range(chunks):
        here = pl.ds(c * BLOCK, BLOCK)
        step = dot(gradb[...], wpad[:, here], NN)
        dmixed[:, here] = step
        dmixedb[:, here] = step.astype(BF16)
    for c in range(chunks):
        here = pl.ds(c * BLOCK, BLOCK)
        dattn[:, here] = dot(dmixedb[...], wout[here, :], NT).astype(BF16)

    scale = (width // HEADS) ** -0.5

    def backward(m, carry):
        rows = pl.ds(pl.multiple_of(m * points, points), points)
        number = cnt[...]
        outs = [spread_heads(dattn[rows, here]) for here in heres]
        dprobs = [dot(kv[m, :, there], out, NT) for there, out in zip(theres, outs)]
        shares = [probs[m, h] for h in pack_range]
        leans = [
            jnp.sum(number * one * share, axis=0, keepdims=True)
            for one, share in zip(dprobs, shares)
        ]
        dscores = [
            (share * (one - lean)).astype(BF16) for share, one, lean in zip(shares, dprobs, leans)
        ]
        dscores = [(number * one.astype(F32)).astype(BF16) for one in dscores]
        weights = [(number * one.astype(BF16).astype(F32)).astype(BF16) for one in shares]
        dqs = [dot(one, kv[m, :, here], TN) for one, here in zip(dscores, heres)]
        dks = [
            dot(one, spread_heads(query[rows, here]), NN) for one, here in zip(dscores, heres)
        ]
        dvs = [dot(one, out, NN) for one, out in zip(weights, outs)]
        for h in pack_range:
            dquery[rows, heres[h]] = (pick_heads(dqs[h]) * scale).astype(BF16)
            dkv[m, :, heres[h]] = dks[h].astype(BF16)
            dkv[m, :, theres[h]] = dvs[h].astype(BF16)
        return carry

    lax.fori_loop(0, members, backward, 0)

    def back_copy(side, c):
        return pltpu.make_async_remote_copy(
            src_ref=dsend.at[side, c],
            dst_ref=drecv.at[side, c],
            send_sem=back_s.at[side, c],
            recv_sem=back_r.at[side, c],
            device_id=(me_m, down if side == 0 else up),
            device_id_type=MESH,
        )

    def second_stage():
        each(parts, part_copy, "wait_recv")
        piece_sum = local[my_part].astype(F32)
        for k in range(1, parts):
            piece_sum = piece_sum + part[k].astype(F32)
        plane[me_z] = split_loss(piece_sum).astype(BF16)
        heard(relay.at[2])
        for k in sorted(range(1, n_z), key=lambda k: -min(k, n_z - k)):
            plane_copy(k).start()

    for c in range(chunks):
        here = pl.ds(c * BLOCK, BLOCK)
        rows = dkv[...].reshape(members * window, 2 * width)
        step = dot(rows, wqkv[here, pl.ds(width, 2 * width)], NT)
        step = step.reshape(members, window, BLOCK)
        for side, start in ((0, 0), (1, 2 * points)):
            dsend[side, c] = step[:, start : start + points].astype(BF16)
        if c == chunks // 2 - 1:
            second_stage()
        if c >= chunks // 2 - 1:
            for ready in range(c + 1) if c == chunks // 2 - 1 else (c,):
                back_copy(0, ready).start()
                back_copy(1, ready).start()
        dhid[:, :, here] = step[:, points : 2 * points]

    for c in range(chunks):
        here = pl.ds(c * BLOCK, BLOCK)
        step = dot(dquery[...], wqkv[here, pl.ds(0, width)], NT)
        dhid[:, :, here] = dhid[:, :, here] + step.reshape(members, points, BLOCK)

    each(n_z, plane_copy, "wait_recv")
    plane_sum = plane[0].astype(F32)
    for k in range(1, n_z):
        plane_sum = plane_sum + plane[k].astype(F32)
    full[mine] = (split_loss(plane_sum) * (1.0 / (points * n_grid))).astype(BF16)
    for k in far_first:
        full_copy(k).start()
    pass_copy(0).start()
    for c in range(chunks):
        here = pl.ds(c * BLOCK, BLOCK)
        for side in range(2):
            back_copy(side, c).wait_recv()
        extra = drecv[0, c].astype(F32) + drecv[1, c].astype(F32)
        dhid[:, :, here] = dhid[:, :, here] + extra

    for m in range(members):
        dnormed = dhid[m] * gain[...]
        norm = normed[m]
        first = jnp.mean(dnormed, axis=-1, keepdims=True)
        second = jnp.mean(dnormed * norm, axis=-1, keepdims=True)
        dstates = inverse[m] * (dnormed - first - norm * second)
        grad[m] = (dstates + dmixed[pl.ds(m * points, points), :]).astype(BF16)

    for h in range(HALVES):
        for i in range(2):
            halo_copy(h, i).wait_send()
        for k in range(1, n_member):
            pred_copy(h, k).wait_send()
            mix_copy(h, k).wait_send()
    each(parts, part_copy, "wait_send")
    each(n_z, plane_copy, "wait_send")
    for c in range(chunks):
        for side in range(2):
            back_copy(side, c).wait_send()

    for k in reversed(far_first):
        full_copy(k).wait_recv()
        pass_copy(k).start()
    each(area, full_copy, "wait_send")
    for k in range(area):
        pass_copy(k).wait_recv()
    total = jnp.zeros((1, 1), F32)
    for m in range(n_member):
        for u in range(parts * per):
            b, r = m * (bands // n_member) + u // quads, u % quads
            tile = full[m * parts + u // per, u % per].astype(F32)
            count = min(32, VARS - 32 * r)
            head_out[pl.ds(32 * r, count), pl.ds(b * LANES, LANES)] = tile[:count]
            if u == VARS // 32:
                total = total + tile[spot : spot + 1, 0:1] + tile[spot + 1 : spot + 2, 0:1]
    loss[...] = total * (1.0 / (VARS * total_members))
    for k in range(area):
        pass_copy(k).wait_send()


def results(loss, grad, head, loss_hbm, grad_hbm, head_hbm, sem):
    copies = [
        pltpu.make_async_copy(source, target, sem.at[i])
        for i, (source, target) in enumerate(((grad, grad_hbm), (head, head_hbm), (loss, loss_hbm)))
    ]
    for copy in copies:
        copy.start()
    for copy in copies:
        copy.wait()


def body(sizes, states, ln_gain, w_qkv, w_out, w_head, targets, neighbours, counts):
    n_member, n_y, n_z, n_core = sizes
    members, points, width = states.shape
    flat = members * points
    window = 3 * points
    group = n_member * n_y * n_core
    chunks = width // BLOCK
    cols = PACK * (width // HEADS)
    tiles = (LANES // 32) * (width // LANES)
    per = tiles // group
    vmem = pl.BlockSpec(memory_space=pltpu.VMEM)
    hbm = pl.BlockSpec(memory_space=pl.ANY)
    dma = pltpu.SemaphoreType.DMA
    operands = (states, ln_gain.reshape(1, width), w_qkv, w_out, w_head.T, targets, neighbours, counts)
    loss, grad, head = pl.pallas_call(
        functools.partial(kernel, sizes),
        out_shape=(
            jax.ShapeDtypeStruct((1, 1), F32),
            jax.ShapeDtypeStruct((members, points, width), BF16),
            jax.ShapeDtypeStruct((VARS, width), F32),
        ),
        in_specs=[hbm] * 8,
        out_specs=(vmem, vmem, vmem),
        scratch_shapes=[
            pltpu.VMEM((members, points, width), BF16),
            pltpu.VMEM((1, width), F32),
            pltpu.VMEM((width, 3 * width), BF16),
            pltpu.VMEM((width, width), BF16),
            pltpu.VMEM((VARS, width), BF16),
            pltpu.VMEM((points, VARS), F32),
            pltpu.SMEM(neighbours.shape, jnp.int32),
            pltpu.SMEM((1,), jnp.int32),
            pltpu.VMEM((LANES, width), BF16),
            pltpu.VMEM((points, LANES), F32),
            pltpu.VMEM((flat, width), BF16),
            pltpu.VMEM((2, flat, width), BF16),
            pltpu.VMEM((flat, width), BF16),
            pltpu.VMEM((members, window, 2 * width), BF16),
            pltpu.VMEM((members, points, width), F32),
            pltpu.VMEM((members, points, 1), F32),
            pltpu.VMEM((window, LANES), F32),
            pltpu.VMEM((PACK * points, cols), F32),
            pltpu.VMEM((members, HEADS // PACK, window, PACK * points), F32),
            pltpu.VMEM((flat, width), BF16),
            pltpu.VMEM((chunks, flat, BLOCK), BF16),
            pltpu.VMEM((n_member, chunks // n_member, flat, BLOCK), BF16),
            pltpu.VMEM((n_member, flat, LANES), BF16),
            pltpu.VMEM((n_member * members, points, LANES), F32),
            pltpu.VMEM((n_member * members, points, LANES), F32),
            pltpu.VMEM((points, LANES), F32),
            pltpu.VMEM((n_member * flat, LANES), BF16),
            pltpu.VMEM((flat, LANES), BF16),
            pltpu.VMEM((n_y * n_core, per, 32, LANES), BF16),
            pltpu.VMEM((n_y * n_core, per, 32, LANES), BF16),
            pltpu.VMEM((n_z, per, 32, LANES), BF16),
            pltpu.VMEM((group, per, 32, LANES), BF16),
            pltpu.VMEM((flat, width), F32),
            pltpu.VMEM((flat, width), BF16),
            pltpu.VMEM((flat, width), BF16),
            pltpu.VMEM((flat, width), BF16),
            pltpu.VMEM((members, window, 2 * width), BF16),
            pltpu.VMEM((2, chunks, members, points, BLOCK), BF16),
            pltpu.VMEM((2, chunks, members, points, BLOCK), BF16),
            pltpu.VMEM((members, points, width), F32),
            pltpu.SemaphoreType.REGULAR((RELAYS,)),
            dma((6,)),
            dma((3 * width // (2 * BLOCK) + 1,)),
            dma((HALVES, 2)),
            dma((HALVES, 2)),
            dma((HALVES, n_member)),
            dma((HALVES, n_member)),
            dma((HALVES, n_member)),
            dma((HALVES, n_member)),
            dma((n_y * n_core,)),
            dma((n_y * n_core,)),
            dma((n_z,)),
            dma((n_z,)),
            dma((n_member * n_y,)),
            dma((n_member * n_y,)),
            dma((n_member * n_y,)),
            dma((n_member * n_y,)),
            dma((2, chunks)),
            dma((2, chunks)),
        ],
        compiler_params=pltpu.CompilerParams(
            collective_id=0, has_side_effects=True, vmem_limit_bytes=VMEM_BYTES
        ),
    )(*(pltpu.with_memory_space_constraint(x, pltpu.HBM) for x in operands[:-1]), operands[-1])
    held = [loss, *(pltpu.with_memory_space_constraint(x, pltpu.VMEM) for x in (grad, head))]
    loss, grad, head = pl.pallas_call(
        results,
        out_shape=tuple(jax.ShapeDtypeStruct(x.shape, x.dtype) for x in held),
        in_specs=[hbm] * 3,
        out_specs=(hbm,) * 3,
        scratch_shapes=[dma((3,))],
    )(*held)
    return (loss.reshape(()), grad, head.T)


def solution(mesh):
    placed = (
        P("member", "grid", None),
        P(),
        P(),
        P(),
        P(),
        P("grid", None),
        P("grid", None),
        P("grid"),
    )
    n_core = 2
    n_z = min(8, mesh.shape["grid"] // n_core)
    sizes = (mesh.shape["member"], mesh.shape["grid"] // (n_z * n_core), n_z, n_core)
    return jax.shard_map(
        functools.partial(body, sizes),
        mesh=mesh,
        in_specs=placed,
        out_specs=(P(), P("member", "grid", None), P()),
        check_vma=False,
    )
```

```python
import functools

import jax
import jax.numpy as jnp
from jax import lax
from jax.experimental import pallas as pl
from jax.experimental.pallas import tpu as pltpu
from jax.sharding import PartitionSpec as P

HEADS = 16
VARS = 100
TILE = 16
EPS = 1e-05
DELTA = 0.1
LANES = 128
PACK = 4
HALVES = 2
RELAYS = 3
VMEM_BYTES = 40 * 1024 * 1024
BLOCK = 256
MESH = pl.DeviceIdType.MESH
F32 = jnp.float32
BF16 = jnp.bfloat16

NN = (((1,), (0,)), ((), ()))
NT = (((1,), (1,)), ((), ()))
TN = (((0,), (0,)), ((), ()))


def dot(a, b, dims):
    return lax.dot_general(a, b, dims, preferred_element_type=F32)


def kernel(
    sizes,
    states_hbm,
    gain_hbm,
    wqkv_hbm,
    wout_hbm,
    whead_hbm,
    targets_hbm,
    neighbours_hbm,
    counts_hbm,
    loss,
    grad,
    head_out,
    states,
    gain,
    wqkv,
    wout,
    whead,
    targets,
    neighbours,
    counts,
    wpad,
    tpad,
    hidden,
    beside,
    query,
    kv,
    normed,
    inverse,
    cnt,
    hmask,
    probs,
    attn,
    mixed,
    mix,
    ens,
    pens,
    slopes,
    gaps,
    gradall,
    gradb,
    local,
    part,
    plane,
    full,
    dmixed,
    dmixedb,
    dattn,
    dquery,
    dkv,
    dsend,
    drecv,
    dhid,
    relay,
    insem,
    wsem,
    halo_s,
    halo_r,
    pred_s,
    pred_r,
    mix_s,
    mix_r,
    part_s,
    part_r,
    plane_s,
    plane_r,
    full_s,
    full_r,
    pass_s,
    pass_r,
    back_s,
    back_r,
):
    n_member, n_y, n_z, n_core = sizes
    n_grid = n_y * n_z * n_core
    group = n_member * n_y * n_core
    members, points, width = states.shape
    window = kv.shape[1]
    flat = members * points
    cols = PACK * (width // HEADS)
    chunks = width // BLOCK
    packs = HEADS // PACK
    total_members = members * n_member
    per = local.shape[1]
    bands = width // LANES
    parts = n_y * n_core
    held = n_member * members

    me_m = lax.axis_index("member")
    me_g = lax.axis_index("grid")
    core = lax.rem(me_g, n_core)
    me_z = lax.rem(me_g // n_core, n_z)
    me_y = me_g // (n_core * n_z)
    up = lax.rem(me_g + 1, n_grid)
    down = lax.rem(me_g + n_grid - 1, n_grid)
    my_part = me_y * n_core + core
    mine = me_m * parts + my_part

    def grid_at(y, z, c):
        return (y * n_z + z) * n_core + c

    def group_peer(k):
        m = lax.rem(me_m + k // (n_y * n_core), n_member)
        y = lax.rem(me_y + lax.rem(k // n_core, n_y), n_y)
        c = lax.rem(core + lax.rem(k, n_core), n_core)
        return (m, grid_at(y, me_z, c))

    def part_peer(k):
        y = lax.rem(me_y + k // n_core, n_y)
        c = lax.rem(core + lax.rem(k, n_core), n_core)
        return (me_m, grid_at(y, me_z, c)), y * n_core + c

    def plane_peer(k):
        return (me_m, grid_at(me_y, lax.rem(me_z + k, n_z), core))

    def ring(k, n):
        return min(k, n - k)

    def around(n):
        return (1, n - 1) if n > 2 else (1,) * (n - 1)

    neighbours_of = [(me_m, up), (me_m, down)]
    neighbours_of += [(lax.rem(me_m + k, n_member), me_g) for k in around(n_member)]
    neighbours_of += [(me_m, grid_at(lax.rem(me_y + k, n_y), me_z, core)) for k in around(n_y)]
    neighbours_of += [(me_m, grid_at(me_y, lax.rem(me_z + k, n_z), core)) for k in around(n_z)]

    def tell(semaphore):
        for device in neighbours_of:
            pl.semaphore_signal(semaphore, inc=1, device_id=device, device_id_type=MESH)

    def heard(semaphore):
        pl.semaphore_wait(semaphore, len(neighbours_of))

    barrier = pltpu.get_barrier_semaphore()
    tell(barrier)

    wide = 2 * BLOCK
    n_wide = 3 * width // wide
    small_copies = [
        pltpu.make_async_copy(source, target, insem.at[i])
        for i, (source, target) in enumerate(
            (
                (states_hbm, states),
                (gain_hbm, gain),
                (neighbours_hbm, neighbours),
                (counts_hbm, counts),
                (whead_hbm, whead),
                (targets_hbm, targets),
            )
        )
    ]
    weight_copies = [
        pltpu.make_async_copy(
            wqkv_hbm.at[:, pl.ds(c * wide, wide)], wqkv.at[:, pl.ds(c * wide, wide)], wsem.at[c]
        )
        for c in range(n_wide)
    ]
    weight_copies.append(pltpu.make_async_copy(wout_hbm, wout, wsem.at[n_wide]))
    for copy in small_copies + weight_copies:
        copy.start()
    small_copies[0].wait()
    small_copies[1].wait()

    for m in range(members):
        values = states[m].astype(F32)
        centre = jnp.mean(values, axis=-1, keepdims=True)
        centred = values - centre
        spread = jnp.mean(centred * centred, axis=-1, keepdims=True)
        inv = lax.rsqrt(spread + EPS)
        norm = centred * inv
        normed[m] = norm
        inverse[m] = inv
        hidden[pl.ds(m * points, points), :] = (norm * gain[...]).astype(BF16)

    heard(barrier)

    some = members // HALVES

    def rows_of(h):
        return pl.ds(pl.multiple_of(h * (some * points), some * points), some * points)

    def halo_copy(h, i):
        return pltpu.make_async_remote_copy(
            src_ref=hidden.at[rows_of(h)],
            dst_ref=beside.at[i, rows_of(h)],
            send_sem=halo_s.at[h, i],
            recv_sem=halo_r.at[h, i],
            device_id=(me_m, (up, down)[i]),
            device_id_type=MESH,
        )

    for h in range(HALVES):
        for i in range(2):
            halo_copy(h, i).start()
    tell(relay.at[0])

    for copy in small_copies[2:]:
        copy.wait()

    key_tile = 2 * me_g - 2 + lax.broadcasted_iota(jnp.int32, (window, LANES), 0) // TILE
    lane = lax.broadcasted_iota(jnp.int32, (window, LANES), 1)
    query_tile = lax.rem(lane, points) // TILE
    number = jnp.zeros((window, LANES), F32)
    for t in range(points // TILE):
        for e in range(neighbours.shape[1]):
            hit = (key_tile == neighbours[t, e]) & (query_tile == t)
            number = number + jnp.where(hit, 1.0, 0.0)
    cnt[...] = number
    rows_i = lax.broadcasted_iota(jnp.int32, (PACK * points, cols), 0) // points
    cols_i = lax.broadcasted_iota(jnp.int32, (PACK * points, cols), 1) // (cols // PACK)
    hmask[...] = jnp.where(rows_i == cols_i, 1.0, 0.0)
    wpad[...] = jnp.zeros_like(wpad)
    wpad[pl.ds(0, VARS), :] = whead[...]
    tpad[...] = jnp.zeros_like(tpad)
    tpad[:, pl.ds(0, VARS)] = targets[...]

    for c in range(n_wide):
        if c % 3 == 0:
            for d in range(c, c + 3):
                weight_copies[d].wait()
        step = dot(hidden[...], wqkv[:, pl.ds(c * wide, wide)], NN).astype(BF16)
        if c * wide < width:
            query[:, pl.ds(c * wide, wide)] = step * jnp.asarray((width // HEADS) ** -0.5, BF16)
        else:
            there = pl.ds(c * wide - width, wide)
            kv[:, pl.ds(points, points), there] = step.reshape(members, points, wide)

    heard(relay.at[0])
    tell(relay.at[1])

    def spread_heads(rows):
        return jnp.concatenate([rows] * PACK, axis=0) * hmask[...].astype(BF16)

    def pick_heads(rows):
        rows = rows * hmask[...]
        return jnp.sum(rows.reshape(PACK, points, cols), axis=0)

    pack_range = range(packs)
    heres = [pl.ds(h * cols, cols) for h in pack_range]
    theres = [pl.ds(width + h * cols, cols) for h in pack_range]

    share = chunks // n_member

    def mix_copy(h, k):
        return pltpu.make_async_remote_copy(
            src_ref=mixed.at[pl.ds(lax.rem(me_m + k, n_member) * share, share), rows_of(h)],
            dst_ref=mix.at[k, :, rows_of(h)],
            send_sem=mix_s.at[h, k],
            recv_sem=mix_r.at[h, k],
            device_id=(lax.rem(me_m + k, n_member), me_g),
            device_id_type=MESH,
        )

    def pred_copy(h, k):
        return pltpu.make_async_remote_copy(
            src_ref=ens.at[0, rows_of(h)],
            dst_ref=ens.at[k, rows_of(h)],
            send_sem=pred_s.at[h, k],
            recv_sem=pred_r.at[h, k],
            device_id=(lax.rem(me_m + k, n_member), me_g),
            device_id_type=MESH,
        )

    far_members = sorted(range(1, n_member), key=lambda k: -min(k, n_member - k))
    number = cnt[...]

    def forward(h, carry):
        for i in range(2):
            halo_copy(h, i).wait_recv()
        first = h * some
        near = beside[:, rows_of(h), :].reshape(2 * some * points, width)
        group_members = pl.ds(first, some)
        for c in range(2 * width // wide):
            here = pl.ds(c * wide, wide)
            step = dot(near, wqkv[:, pl.ds(width + c * wide, wide)], NN)
            step = step.astype(BF16).reshape(2, some, points, wide)
            kv[group_members, pl.ds(0, points), here] = step[0]
            kv[group_members, pl.ds(2 * points, points), here] = step[1]

        pairs = [(first + m, p) for m in range(some) for p in pack_range]
        queries = [
            query[pl.ds(pl.multiple_of(m * points, points), points), heres[p]] for m, p in pairs
        ]
        scores = [dot(kv[m, :, heres[p]], spread_heads(q), NT) for (m, p), q in zip(pairs, queries)]
        scores = [jnp.where(number > 0.0, one, -3e38) for one in scores]
        tops = [jnp.max(one, axis=0, keepdims=True) for one in scores]
        expos = [jnp.exp(one - top) for one, top in zip(scores, tops)]
        totals = [jnp.sum(number * expo, axis=0, keepdims=True) for expo in expos]
        shares = [expo / total for expo, total in zip(expos, totals)]
        weights = [(number * one.astype(BF16).astype(F32)).astype(BF16) for one in shares]
        outs = [dot(one, kv[m, :, theres[p]], TN) for one, (m, p) in zip(weights, pairs)]
        for (m, p), one, out in zip(pairs, shares, outs):
            probs[m, p] = one
            there = pl.ds(pl.multiple_of(m * points, points), points)
            attn[there, heres[p]] = pick_heads(out).astype(BF16)

        @pl.when(h == 0)
        def _():
            weight_copies[n_wide].wait()

        rows = rows_of(h)
        for k in (*far_members, 0):
            for c in range(share):
                block = lax.rem(me_m + k, n_member) * share + c
                here = pl.ds(pl.multiple_of(block * BLOCK, BLOCK), BLOCK)
                proj = dot(attn[rows, :], wout[:, here], NN)
                before = states[group_members, :, here].reshape(some * points, BLOCK).astype(F32)
                mixed[block, rows] = (before + proj).astype(BF16)
        pred = dot(mixed[0, rows], wpad[:, pl.ds(0, BLOCK)], NT)
        for c in range(1, chunks):
            pred = pred + dot(mixed[c, rows], wpad[:, pl.ds(c * BLOCK, BLOCK)], NT)
        ens[0, rows] = pred.astype(BF16)
        for k in far_members:
            pred_copy(h, k).start()
        for k in far_members:
            mix_copy(h, k).start()

        @pl.when(h == 0)
        def _():
            heard(relay.at[1])
            tell(relay.at[2])

        return carry

    lax.fori_loop(0, HALVES, forward, 0)
    mix[0] = mixed[pl.ds(me_m * share, share)]

    step_rows = 8
    late = [i for i in range(held) if i >= members and i % members >= members - some]
    early = [i for i in range(held) if i not in late]
    everyone = [(i, j) for i in range(held) for j in range(i + 1, held)]
    early_pairs = [(i, j) for i, j in everyone if i not in late and j not in late]
    late_pairs = [pair for pair in everyone if pair not in early_pairs]

    def widen(k, first, count):
        rows = ens[k, pl.ds(first * points, count * points), :].astype(F32)
        pens[pl.ds(k * members + first, count)] = rows.reshape(count, points, LANES)

    def pair_sums(pairs, values, pulls, apart):
        for i, j in pairs:
            gap = values[i] - values[j]
            square = gap * gap + DELTA * DELTA
            root = lax.rsqrt(square)
            pull = gap * root
            pulls[i] = pull if pulls[i] is None else pulls[i] + pull
            pulls[j] = -pull if pulls[j] is None else pulls[j] - pull
            if i < members:
                length = square * root
                apart = apart + (length + length if j < members else length)
        return apart

    def crps_early(block, carry):
        here = pl.ds(pl.multiple_of(block * step_rows, step_rows), step_rows)
        values = {i: pens[i, here, :] for i in early}
        pulls = [None] * held
        gaps[here, :] = pair_sums(early_pairs, values, pulls, jnp.zeros((step_rows, LANES), F32))
        for i in early:
            slopes[i, here, :] = pulls[i]
        return carry

    def crps_late(block, total):
        start = pl.multiple_of(block * step_rows, step_rows)
        here = pl.ds(start, step_rows)
        row = start + lax.broadcasted_iota(jnp.int32, (step_rows, LANES), 0)
        column = lax.broadcasted_iota(jnp.int32, (step_rows, LANES), 1)
        valid = (row < counts[0]) & (column < VARS)
        target = tpad[here, :]
        values = [pens[i, here, :] for i in range(held)]
        pulls = [None if i in late else slopes[i, here, :] for i in range(held)]
        apart = pair_sums(late_pairs, values, pulls, gaps[here, :])
        terms = apart * (-0.5 / (total_members - 1))
        for i in range(held):
            miss = values[i] - target
            square = miss * miss + DELTA * DELTA
            root = lax.rsqrt(square)
            slope = miss * root - pulls[i] * (1.0 / (total_members - 1))
            slopes[i, here, :] = jnp.where(valid, slope, 0.0)
            if i < members:
                terms = terms + square * root
        return total + jnp.where(valid, terms, 0.0)

    for h in range(HALVES - 1):
        for k in range(1, n_member):
            pred_copy(h, k).wait_recv()
    widen(0, 0, members)
    for k in range(1, n_member):
        widen(k, 0, members - some)
    lax.fori_loop(0, points // step_rows, crps_early, 0)
    for k in range(1, n_member):
        pred_copy(HALVES - 1, k).wait_recv()
        widen(k, members - some, some)
    terms = lax.fori_loop(0, points // step_rows, crps_late, jnp.zeros((step_rows, LANES), F32))
    loss_part = jnp.sum(jnp.sum(terms, axis=1, keepdims=True), axis=0, keepdims=True)
    gradall[...] = slopes[...].reshape(held * points, LANES).astype(BF16)
    gradb[...] = gradall[pl.ds(0, flat), :]

    quads = LANES // 32
    tile_row = lax.broadcasted_iota(jnp.int32, (per, 32, LANES), 1)
    tile_at = my_part * per + lax.broadcasted_iota(jnp.int32, (per, 32, LANES), 0)
    variable = lax.rem(tile_at, quads) * 32 + tile_row
    spot = VARS % 32

    def split_loss(tiles):
        value = tiles[:, spot : spot + 1, :] + tiles[:, spot + 1 : spot + 2, :]
        high = value.astype(BF16).astype(F32)
        return jnp.where(
            variable == VARS, high, jnp.where(variable == VARS + 1, value - high, tiles)
        )

    row_all = lax.broadcasted_iota(jnp.int32, (LANES, 1), 0)
    loss_high = loss_part.astype(BF16).astype(F32)
    tail = jnp.where(
        row_all == VARS, loss_high, jnp.where(row_all == VARS + 1, loss_part - loss_high, 0.0)
    )
    for h in range(HALVES):
        for k in range(1, n_member):
            mix_copy(h, k).wait_recv()
    per_block = BLOCK // LANES
    for c in range(share):
        block = dot(gradall[...], mix[:, c].reshape(held * points, BLOCK), TN) + tail
        for b in range(per_block):
            for r in range(quads):
                u = (c * per_block + b) * quads + r
                local[u // per, u % per] = block[
                    r * 32 : (r + 1) * 32, b * LANES : (b + 1) * LANES
                ].astype(BF16)

    def part_copy(k):
        device, owner = part_peer(k)
        return pltpu.make_async_remote_copy(
            src_ref=local.at[owner],
            dst_ref=part.at[k],
            send_sem=part_s.at[k],
            recv_sem=part_r.at[k],
            device_id=device,
            device_id_type=MESH,
        )

    def plane_copy(k):
        return pltpu.make_async_remote_copy(
            src_ref=plane.at[me_z],
            dst_ref=plane.at[me_z],
            send_sem=plane_s.at[k],
            recv_sem=plane_r.at[k],
            device_id=plane_peer(k),
            device_id_type=MESH,
        )

    def area_peer(k):
        m = lax.rem(me_m + k // n_y, n_member)
        y = lax.rem(me_y + lax.rem(k, n_y), n_y)
        return m, y

    def full_copy(k):
        m, y = area_peer(k)
        return pltpu.make_async_remote_copy(
            src_ref=full.at[mine],
            dst_ref=full.at[mine],
            send_sem=full_s.at[k],
            recv_sem=full_r.at[k],
            device_id=(m, grid_at(y, me_z, core)),
            device_id_type=MESH,
        )

    def pass_copy(k):
        m = lax.rem(me_m + n_member - k // n_y, n_member)
        y = lax.rem(me_y + n_y - k % n_y, n_y)
        slot = (m * n_y + y) * n_core + core
        return pltpu.make_async_remote_copy(
            src_ref=full.at[slot],
            dst_ref=full.at[slot],
            send_sem=pass_s.at[k],
            recv_sem=pass_r.at[k],
            device_id=(me_m, grid_at(me_y, me_z, lax.rem(core + 1, n_core))),
            device_id_type=MESH,
        )

    def apart_by(k):
        return ring(k // n_y, n_member) + ring(k % n_y, n_y)

    area = n_member * n_y
    far_first = sorted(range(1, area), key=lambda k: -apart_by(k))

    def each(count, make, act):
        def step(k, c):
            getattr(make(k), act)()
            return c

        lax.fori_loop(1, count, step, 0)

    for k in range(parts - 1, 0, -1):
        part_copy(k).start()

    for c in range(chunks):
        here = pl.ds(c * BLOCK, BLOCK)
        step = dot(gradb[...], wpad[:, here], NN)
        dmixed[:, here] = step
        dmixedb[:, here] = step.astype(BF16)
    for c in range(chunks):
        here = pl.ds(c * BLOCK, BLOCK)
        dattn[:, here] = dot(dmixedb[...], wout[here, :], NT).astype(BF16)

    scale = (width // HEADS) ** -0.5

    def backward(m, carry):
        rows = pl.ds(pl.multiple_of(m * points, points), points)
        number = cnt[...]
        outs = [spread_heads(dattn[rows, here]) for here in heres]
        dprobs = [dot(kv[m, :, there], out, NT) for there, out in zip(theres, outs)]
        shares = [probs[m, h] for h in pack_range]
        leans = [
            jnp.sum(number * one * share, axis=0, keepdims=True)
            for one, share in zip(dprobs, shares)
        ]
        dscores = [
            (share * (one - lean)).astype(BF16) for share, one, lean in zip(shares, dprobs, leans)
        ]
        dscores = [(number * one.astype(F32)).astype(BF16) for one in dscores]
        weights = [(number * one.astype(BF16).astype(F32)).astype(BF16) for one in shares]
        dqs = [dot(one, kv[m, :, here], TN) for one, here in zip(dscores, heres)]
        dks = [
            dot(one, spread_heads(query[rows, here]), NN) for one, here in zip(dscores, heres)
        ]
        dvs = [dot(one, out, NN) for one, out in zip(weights, outs)]
        for h in pack_range:
            dquery[rows, heres[h]] = (pick_heads(dqs[h]) * scale).astype(BF16)
            dkv[m, :, heres[h]] = dks[h].astype(BF16)
            dkv[m, :, theres[h]] = dvs[h].astype(BF16)
        return carry

    lax.fori_loop(0, members, backward, 0)

    def back_copy(side, c):
        return pltpu.make_async_remote_copy(
            src_ref=dsend.at[side, c],
            dst_ref=drecv.at[side, c],
            send_sem=back_s.at[side, c],
            recv_sem=back_r.at[side, c],
            device_id=(me_m, down if side == 0 else up),
            device_id_type=MESH,
        )

    def second_stage():
        each(parts, part_copy, "wait_recv")
        piece_sum = local[my_part].astype(F32)
        for k in range(1, parts):
            piece_sum = piece_sum + part[k].astype(F32)
        plane[me_z] = split_loss(piece_sum).astype(BF16)
        heard(relay.at[2])
        for k in sorted(range(1, n_z), key=lambda k: -min(k, n_z - k)):
            plane_copy(k).start()

    for c in range(chunks):
        here = pl.ds(c * BLOCK, BLOCK)
        rows = dkv[...].reshape(members * window, 2 * width)
        step = dot(rows, wqkv[here, pl.ds(width, 2 * width)], NT)
        step = step.reshape(members, window, BLOCK)
        for side, start in ((0, 0), (1, 2 * points)):
            dsend[side, c] = step[:, start : start + points].astype(BF16)
        if c == chunks // 2 - 1:
            second_stage()
        if c >= chunks // 2 - 1:
            for ready in range(c + 1) if c == chunks // 2 - 1 else (c,):
                back_copy(0, ready).start()
                back_copy(1, ready).start()
        dhid[:, :, here] = step[:, points : 2 * points]

    for c in range(chunks):
        here = pl.ds(c * BLOCK, BLOCK)
        step = dot(dquery[...], wqkv[here, pl.ds(0, width)], NT)
        dhid[:, :, here] = dhid[:, :, here] + step.reshape(members, points, BLOCK)

    each(n_z, plane_copy, "wait_recv")
    plane_sum = plane[0].astype(F32)
    for k in range(1, n_z):
        plane_sum = plane_sum + plane[k].astype(F32)
    full[mine] = (split_loss(plane_sum) * (1.0 / (points * n_grid))).astype(BF16)
    for k in far_first:
        full_copy(k).start()
    pass_copy(0).start()
    for c in range(chunks):
        here = pl.ds(c * BLOCK, BLOCK)
        for side in range(2):
            back_copy(side, c).wait_recv()
        extra = drecv[0, c].astype(F32) + drecv[1, c].astype(F32)
        dhid[:, :, here] = dhid[:, :, here] + extra

    for m in range(members):
        dnormed = dhid[m] * gain[...]
        norm = normed[m]
        first = jnp.mean(dnormed, axis=-1, keepdims=True)
        second = jnp.mean(dnormed * norm, axis=-1, keepdims=True)
        dstates = inverse[m] * (dnormed - first - norm * second)
        grad[m] = (dstates + dmixed[pl.ds(m * points, points), :]).astype(BF16)

    for h in range(HALVES):
        for i in range(2):
            halo_copy(h, i).wait_send()
        for k in range(1, n_member):
            pred_copy(h, k).wait_send()
            mix_copy(h, k).wait_send()
    each(parts, part_copy, "wait_send")
    each(n_z, plane_copy, "wait_send")
    for c in range(chunks):
        for side in range(2):
            back_copy(side, c).wait_send()

    for k in reversed(far_first):
        full_copy(k).wait_recv()
        pass_copy(k).start()
    each(area, full_copy, "wait_send")
    for k in range(area):
        pass_copy(k).wait_recv()
    total = jnp.zeros((1, 1), F32)
    for m in range(n_member):
        for u in range(parts * per):
            b, r = m * (bands // n_member) + u // quads, u % quads
            tile = full[m * parts + u // per, u % per].astype(F32)
            count = min(32, VARS - 32 * r)
            head_out[pl.ds(32 * r, count), pl.ds(b * LANES, LANES)] = tile[:count]
            if u == VARS // 32:
                total = total + tile[spot : spot + 1, 0:1] + tile[spot + 1 : spot + 2, 0:1]
    loss[...] = total * (1.0 / (VARS * total_members))
    for k in range(area):
        pass_copy(k).wait_send()


def results(loss, grad, head, loss_hbm, grad_hbm, head_hbm, sem):
    copies = [
        pltpu.make_async_copy(source, target, sem.at[i])
        for i, (source, target) in enumerate(((grad, grad_hbm), (head, head_hbm), (loss, loss_hbm)))
    ]
    for copy in copies:
        copy.start()
    for copy in copies:
        copy.wait()


def body(sizes, states, ln_gain, w_qkv, w_out, w_head, targets, neighbours, counts):
    n_member, n_y, n_z, n_core = sizes
    members, points, width = states.shape
    flat = members * points
    window = 3 * points
    group = n_member * n_y * n_core
    chunks = width // BLOCK
    cols = PACK * (width // HEADS)
    tiles = (LANES // 32) * (width // LANES)
    per = tiles // group
    vmem = pl.BlockSpec(memory_space=pltpu.VMEM)
    hbm = pl.BlockSpec(memory_space=pl.ANY)
    dma = pltpu.SemaphoreType.DMA
    operands = (states, ln_gain.reshape(1, width), w_qkv, w_out, w_head.T, targets, neighbours, counts)
    loss, grad, head = pl.pallas_call(
        functools.partial(kernel, sizes),
        out_shape=(
            jax.ShapeDtypeStruct((1, 1), F32),
            jax.ShapeDtypeStruct((members, points, width), BF16),
            jax.ShapeDtypeStruct((VARS, width), F32),
        ),
        in_specs=[hbm] * 8,
        out_specs=(vmem, vmem, vmem),
        scratch_shapes=[
            pltpu.VMEM((members, points, width), BF16),
            pltpu.VMEM((1, width), F32),
            pltpu.VMEM((width, 3 * width), BF16),
            pltpu.VMEM((width, width), BF16),
            pltpu.VMEM((VARS, width), BF16),
            pltpu.VMEM((points, VARS), F32),
            pltpu.SMEM(neighbours.shape, jnp.int32),
            pltpu.SMEM((1,), jnp.int32),
            pltpu.VMEM((LANES, width), BF16),
            pltpu.VMEM((points, LANES), F32),
            pltpu.VMEM((flat, width), BF16),
            pltpu.VMEM((2, flat, width), BF16),
            pltpu.VMEM((flat, width), BF16),
            pltpu.VMEM((members, window, 2 * width), BF16),
            pltpu.VMEM((members, points, width), F32),
            pltpu.VMEM((members, points, 1), F32),
            pltpu.VMEM((window, LANES), F32),
            pltpu.VMEM((PACK * points, cols), F32),
            pltpu.VMEM((members, HEADS // PACK, window, PACK * points), F32),
            pltpu.VMEM((flat, width), BF16),
            pltpu.VMEM((chunks, flat, BLOCK), BF16),
            pltpu.VMEM((n_member, chunks // n_member, flat, BLOCK), BF16),
            pltpu.VMEM((n_member, flat, LANES), BF16),
            pltpu.VMEM((n_member * members, points, LANES), F32),
            pltpu.VMEM((n_member * members, points, LANES), F32),
            pltpu.VMEM((points, LANES), F32),
            pltpu.VMEM((n_member * flat, LANES), BF16),
            pltpu.VMEM((flat, LANES), BF16),
            pltpu.VMEM((n_y * n_core, per, 32, LANES), BF16),
            pltpu.VMEM((n_y * n_core, per, 32, LANES), BF16),
            pltpu.VMEM((n_z, per, 32, LANES), BF16),
            pltpu.VMEM((group, per, 32, LANES), BF16),
            pltpu.VMEM((flat, width), F32),
            pltpu.VMEM((flat, width), BF16),
            pltpu.VMEM((flat, width), BF16),
            pltpu.VMEM((flat, width), BF16),
            pltpu.VMEM((members, window, 2 * width), BF16),
            pltpu.VMEM((2, chunks, members, points, BLOCK), BF16),
            pltpu.VMEM((2, chunks, members, points, BLOCK), BF16),
            pltpu.VMEM((members, points, width), F32),
            pltpu.SemaphoreType.REGULAR((RELAYS,)),
            dma((6,)),
            dma((3 * width // (2 * BLOCK) + 1,)),
            dma((HALVES, 2)),
            dma((HALVES, 2)),
            dma((HALVES, n_member)),
            dma((HALVES, n_member)),
            dma((HALVES, n_member)),
            dma((HALVES, n_member)),
            dma((n_y * n_core,)),
            dma((n_y * n_core,)),
            dma((n_z,)),
            dma((n_z,)),
            dma((n_member * n_y,)),
            dma((n_member * n_y,)),
            dma((n_member * n_y,)),
            dma((n_member * n_y,)),
            dma((2, chunks)),
            dma((2, chunks)),
        ],
        compiler_params=pltpu.CompilerParams(
            collective_id=0, has_side_effects=True, vmem_limit_bytes=VMEM_BYTES
        ),
    )(*(pltpu.with_memory_space_constraint(x, pltpu.HBM) for x in operands[:-1]), operands[-1])
    held = [loss, *(pltpu.with_memory_space_constraint(x, pltpu.VMEM) for x in (grad, head))]
    loss, grad, head = pl.pallas_call(
        results,
        out_shape=tuple(jax.ShapeDtypeStruct(x.shape, x.dtype) for x in held),
        in_specs=[hbm] * 3,
        out_specs=(hbm,) * 3,
        scratch_shapes=[dma((3,))],
    )(*held)
    return (loss.reshape(()), grad, head.T)


def solution(mesh):
    placed = (
        P("member", "grid", None),
        P(),
        P(),
        P(),
        P(),
        P("grid", None),
        P("grid", None),
        P("grid"),
    )
    n_core = 2
    n_z = min(8, mesh.shape["grid"] // n_core)
    sizes = (mesh.shape["member"], mesh.shape["grid"] // (n_z * n_core), n_z, n_core)
    return jax.shard_map(
        functools.partial(body, sizes),
        mesh=mesh,
        in_specs=placed,
        out_specs=(P(), P("member", "grid", None), P()),
        check_vma=False,
    )
```

```python
import functools

import jax
import jax.numpy as jnp
from jax import lax
from jax.experimental import pallas as pl
from jax.experimental.pallas import tpu as pltpu
from jax.sharding import PartitionSpec as P

HEADS = 16
VARS = 100
TILE = 16
EPS = 1e-05
DELTA = 0.1
LANES = 128
PACK = 4
HALVES = 2
RELAYS = 3
VMEM_BYTES = 40 * 1024 * 1024
BLOCK = 256
MESH = pl.DeviceIdType.MESH
F32 = jnp.float32
BF16 = jnp.bfloat16

NN = (((1,), (0,)), ((), ()))
NT = (((1,), (1,)), ((), ()))
TN = (((0,), (0,)), ((), ()))


def dot(a, b, dims):
    return lax.dot_general(a, b, dims, preferred_element_type=F32)


def kernel(
    sizes,
    states_hbm,
    gain_hbm,
    wqkv_hbm,
    wout_hbm,
    whead_hbm,
    targets_hbm,
    neighbours_hbm,
    counts_hbm,
    loss,
    grad,
    head_out,
    states,
    gain,
    wqkv,
    wout,
    whead,
    targets,
    neighbours,
    counts,
    wpad,
    tpad,
    hidden,
    beside,
    query,
    kv,
    normed,
    inverse,
    cnt,
    hmask,
    probs,
    attn,
    mixed,
    mix,
    ens,
    pens,
    slopes,
    gaps,
    gradall,
    gradb,
    local,
    part,
    plane,
    full,
    dmixed,
    dmixedb,
    dattn,
    dquery,
    dkv,
    dsend,
    drecv,
    dhid,
    relay,
    insem,
    wsem,
    halo_s,
    halo_r,
    pred_s,
    pred_r,
    mix_s,
    mix_r,
    part_s,
    part_r,
    plane_s,
    plane_r,
    full_s,
    full_r,
    pass_s,
    pass_r,
    back_s,
    back_r,
):
    n_member, n_y, n_z, n_core = sizes
    n_grid = n_y * n_z * n_core
    group = n_member * n_y * n_core
    members, points, width = states.shape
    window = kv.shape[1]
    flat = members * points
    cols = PACK * (width // HEADS)
    chunks = width // BLOCK
    packs = HEADS // PACK
    total_members = members * n_member
    per = local.shape[1]
    bands = width // LANES
    parts = n_y * n_core
    held = n_member * members

    me_m = lax.axis_index("member")
    me_g = lax.axis_index("grid")
    core = lax.rem(me_g, n_core)
    me_z = lax.rem(me_g // n_core, n_z)
    me_y = me_g // (n_core * n_z)
    up = lax.rem(me_g + 1, n_grid)
    down = lax.rem(me_g + n_grid - 1, n_grid)
    my_part = me_y * n_core + core
    mine = me_m * parts + my_part

    def grid_at(y, z, c):
        return (y * n_z + z) * n_core + c

    def group_peer(k):
        m = lax.rem(me_m + k // (n_y * n_core), n_member)
        y = lax.rem(me_y + lax.rem(k // n_core, n_y), n_y)
        c = lax.rem(core + lax.rem(k, n_core), n_core)
        return (m, grid_at(y, me_z, c))

    def part_peer(k):
        y = lax.rem(me_y + k // n_core, n_y)
        c = lax.rem(core + lax.rem(k, n_core), n_core)
        return (me_m, grid_at(y, me_z, c)), y * n_core + c

    def plane_peer(k):
        return (me_m, grid_at(me_y, lax.rem(me_z + k, n_z), core))

    def ring(k, n):
        return min(k, n - k)

    def around(n):
        return (1, n - 1) if n > 2 else (1,) * (n - 1)

    neighbours_of = [(me_m, up), (me_m, down)]
    neighbours_of += [(lax.rem(me_m + k, n_member), me_g) for k in around(n_member)]
    neighbours_of += [(me_m, grid_at(lax.rem(me_y + k, n_y), me_z, core)) for k in around(n_y)]
    neighbours_of += [(me_m, grid_at(me_y, lax.rem(me_z + k, n_z), core)) for k in around(n_z)]

    def tell(semaphore):
        for device in neighbours_of:
            pl.semaphore_signal(semaphore, inc=1, device_id=device, device_id_type=MESH)

    def heard(semaphore):
        pl.semaphore_wait(semaphore, len(neighbours_of))

    barrier = pltpu.get_barrier_semaphore()
    tell(barrier)

    wide = 2 * BLOCK
    n_wide = 3 * width // wide
    small_copies = [
        pltpu.make_async_copy(source, target, insem.at[i])
        for i, (source, target) in enumerate(
            (
                (states_hbm, states),
                (gain_hbm, gain),
                (neighbours_hbm, neighbours),
                (counts_hbm, counts),
                (whead_hbm, whead),
                (targets_hbm, targets),
            )
        )
    ]
    weight_copies = [
        pltpu.make_async_copy(
            wqkv_hbm.at[:, pl.ds(c * wide, wide)], wqkv.at[:, pl.ds(c * wide, wide)], wsem.at[c]
        )
        for c in range(n_wide)
    ]
    weight_copies.append(pltpu.make_async_copy(wout_hbm, wout, wsem.at[n_wide]))
    for copy in small_copies + weight_copies:
        copy.start()
    small_copies[0].wait()
    small_copies[1].wait()

    for m in range(members):
        values = states[m].astype(F32)
        centre = jnp.mean(values, axis=-1, keepdims=True)
        centred = values - centre
        spread = jnp.mean(centred * centred, axis=-1, keepdims=True)
        inv = lax.rsqrt(spread + EPS)
        norm = centred * inv
        normed[m] = norm
        inverse[m] = inv
        hidden[pl.ds(m * points, points), :] = (norm * gain[...]).astype(BF16)

    heard(barrier)

    some = members // HALVES

    def rows_of(h):
        return pl.ds(pl.multiple_of(h * (some * points), some * points), some * points)

    def halo_copy(h, i):
        return pltpu.make_async_remote_copy(
            src_ref=hidden.at[rows_of(h)],
            dst_ref=beside.at[i, rows_of(h)],
            send_sem=halo_s.at[h, i],
            recv_sem=halo_r.at[h, i],
            device_id=(me_m, (up, down)[i]),
            device_id_type=MESH,
        )

    for h in range(HALVES):
        for i in range(2):
            halo_copy(h, i).start()
    tell(relay.at[0])

    for copy in small_copies[2:]:
        copy.wait()

    key_tile = 2 * me_g - 2 + lax.broadcasted_iota(jnp.int32, (window, LANES), 0) // TILE
    lane = lax.broadcasted_iota(jnp.int32, (window, LANES), 1)
    query_tile = lax.rem(lane, points) // TILE
    number = jnp.zeros((window, LANES), F32)
    for t in range(points // TILE):
        for e in range(neighbours.shape[1]):
            hit = (key_tile == neighbours[t, e]) & (query_tile == t)
            number = number + jnp.where(hit, 1.0, 0.0)
    cnt[...] = number
    rows_i = lax.broadcasted_iota(jnp.int32, (PACK * points, cols), 0) // points
    cols_i = lax.broadcasted_iota(jnp.int32, (PACK * points, cols), 1) // (cols // PACK)
    hmask[...] = jnp.where(rows_i == cols_i, 1.0, 0.0)
    wpad[...] = jnp.zeros_like(wpad)
    wpad[pl.ds(0, VARS), :] = whead[...]
    tpad[...] = jnp.zeros_like(tpad)
    tpad[:, pl.ds(0, VARS)] = targets[...]

    for c in range(n_wide):
        weight_copies[c].wait()
        step = dot(hidden[...], wqkv[:, pl.ds(c * wide, wide)], NN).astype(BF16)
        if c * wide < width:
            query[:, pl.ds(c * wide, wide)] = step * jnp.asarray((width // HEADS) ** -0.5, BF16)
        else:
            there = pl.ds(c * wide - width, wide)
            kv[:, pl.ds(points, points), there] = step.reshape(members, points, wide)

    heard(relay.at[0])
    tell(relay.at[1])

    def spread_heads(rows):
        return jnp.concatenate([rows] * PACK, axis=0) * hmask[...].astype(BF16)

    def pick_heads(rows):
        rows = rows * hmask[...]
        return jnp.sum(rows.reshape(PACK, points, cols), axis=0)

    pack_range = range(packs)
    heres = [pl.ds(h * cols, cols) for h in pack_range]
    theres = [pl.ds(width + h * cols, cols) for h in pack_range]

    share = chunks // n_member

    def mix_copy(h, k):
        return pltpu.make_async_remote_copy(
            src_ref=mixed.at[pl.ds(lax.rem(me_m + k, n_member) * share, share), rows_of(h)],
            dst_ref=mix.at[k, :, rows_of(h)],
            send_sem=mix_s.at[h, k],
            recv_sem=mix_r.at[h, k],
            device_id=(lax.rem(me_m + k, n_member), me_g),
            device_id_type=MESH,
        )

    def pred_copy(h, k):
        return pltpu.make_async_remote_copy(
            src_ref=ens.at[0, rows_of(h)],
            dst_ref=ens.at[k, rows_of(h)],
            send_sem=pred_s.at[h, k],
            recv_sem=pred_r.at[h, k],
            device_id=(lax.rem(me_m + k, n_member), me_g),
            device_id_type=MESH,
        )

    far_members = sorted(range(1, n_member), key=lambda k: -min(k, n_member - k))
    number = cnt[...]

    def forward(h, carry):
        for i in range(2):
            halo_copy(h, i).wait_recv()
        first = h * some
        near = beside[:, rows_of(h), :].reshape(2 * some * points, width)
        group_members = pl.ds(first, some)
        for c in range(2 * width // wide):
            here = pl.ds(c * wide, wide)
            step = dot(near, wqkv[:, pl.ds(width + c * wide, wide)], NN)
            step = step.astype(BF16).reshape(2, some, points, wide)
            kv[group_members, pl.ds(0, points), here] = step[0]
            kv[group_members, pl.ds(2 * points, points), here] = step[1]

        pairs = [(first + m, p) for m in range(some) for p in pack_range]
        queries = [
            query[pl.ds(pl.multiple_of(m * points, points), points), heres[p]] for m, p in pairs
        ]
        scores = [dot(kv[m, :, heres[p]], spread_heads(q), NT) for (m, p), q in zip(pairs, queries)]
        scores = [jnp.where(number > 0.0, one, -3e38) for one in scores]
        tops = [jnp.max(one, axis=0, keepdims=True) for one in scores]
        expos = [jnp.exp(one - top) for one, top in zip(scores, tops)]
        totals = [jnp.sum(number * expo, axis=0, keepdims=True) for expo in expos]
        shares = [expo / total for expo, total in zip(expos, totals)]
        weights = [(number * one.astype(BF16).astype(F32)).astype(BF16) for one in shares]
        outs = [dot(one, kv[m, :, theres[p]], TN) for one, (m, p) in zip(weights, pairs)]
        for (m, p), one, out in zip(pairs, shares, outs):
            probs[m, p] = one
            there = pl.ds(pl.multiple_of(m * points, points), points)
            attn[there, heres[p]] = pick_heads(out).astype(BF16)

        @pl.when(h == 0)
        def _():
            weight_copies[n_wide].wait()

        rows = rows_of(h)
        for k in (*far_members, 0):
            for c in range(share):
                block = lax.rem(me_m + k, n_member) * share + c
                here = pl.ds(pl.multiple_of(block * BLOCK, BLOCK), BLOCK)
                proj = dot(attn[rows, :], wout[:, here], NN)
                before = states[group_members, :, here].reshape(some * points, BLOCK).astype(F32)
                mixed[block, rows] = (before + proj).astype(BF16)
        pred = dot(mixed[0, rows], wpad[:, pl.ds(0, BLOCK)], NT)
        for c in range(1, chunks):
            pred = pred + dot(mixed[c, rows], wpad[:, pl.ds(c * BLOCK, BLOCK)], NT)
        ens[0, rows] = pred.astype(BF16)
        for k in far_members:
            pred_copy(h, k).start()
        for k in far_members:
            mix_copy(h, k).start()

        @pl.when(h == 0)
        def _():
            heard(relay.at[1])
            tell(relay.at[2])

        return carry

    lax.fori_loop(0, HALVES, forward, 0)
    mix[0] = mixed[pl.ds(me_m * share, share)]

    step_rows = 8
    late = [i for i in range(held) if i >= members and i % members >= members - some]
    early = [i for i in range(held) if i not in late]
    everyone = [(i, j) for i in range(held) for j in range(i + 1, held)]
    early_pairs = [(i, j) for i, j in everyone if i not in late and j not in late]
    late_pairs = [pair for pair in everyone if pair not in early_pairs]

    def widen(k, first, count):
        rows = ens[k, pl.ds(first * points, count * points), :].astype(F32)
        pens[pl.ds(k * members + first, count)] = rows.reshape(count, points, LANES)

    def pair_sums(pairs, values, pulls, apart):
        for i, j in pairs:
            gap = values[i] - values[j]
            square = gap * gap + DELTA * DELTA
            root = lax.rsqrt(square)
            pull = gap * root
            pulls[i] = pull if pulls[i] is None else pulls[i] + pull
            pulls[j] = -pull if pulls[j] is None else pulls[j] - pull
            if i < members:
                length = square * root
                apart = apart + (length + length if j < members else length)
        return apart

    def crps_early(block, carry):
        here = pl.ds(pl.multiple_of(block * step_rows, step_rows), step_rows)
        values = {i: pens[i, here, :] for i in early}
        pulls = [None] * held
        gaps[here, :] = pair_sums(early_pairs, values, pulls, jnp.zeros((step_rows, LANES), F32))
        for i in early:
            slopes[i, here, :] = pulls[i]
        return carry

    def crps_late(block, total):
        start = pl.multiple_of(block * step_rows, step_rows)
        here = pl.ds(start, step_rows)
        row = start + lax.broadcasted_iota(jnp.int32, (step_rows, LANES), 0)
        column = lax.broadcasted_iota(jnp.int32, (step_rows, LANES), 1)
        valid = (row < counts[0]) & (column < VARS)
        target = tpad[here, :]
        values = [pens[i, here, :] for i in range(held)]
        pulls = [None if i in late else slopes[i, here, :] for i in range(held)]
        apart = pair_sums(late_pairs, values, pulls, gaps[here, :])
        terms = apart * (-0.5 / (total_members - 1))
        for i in range(held):
            miss = values[i] - target
            square = miss * miss + DELTA * DELTA
            root = lax.rsqrt(square)
            slope = miss * root - pulls[i] * (1.0 / (total_members - 1))
            slopes[i, here, :] = jnp.where(valid, slope, 0.0)
            if i < members:
                terms = terms + square * root
        return total + jnp.where(valid, terms, 0.0)

    for h in range(HALVES - 1):
        for k in range(1, n_member):
            pred_copy(h, k).wait_recv()
    widen(0, 0, members)
    for k in range(1, n_member):
        widen(k, 0, members - some)
    lax.fori_loop(0, points // step_rows, crps_early, 0)
    for k in range(1, n_member):
        pred_copy(HALVES - 1, k).wait_recv()
        widen(k, members - some, some)
    terms = lax.fori_loop(0, points // step_rows, crps_late, jnp.zeros((step_rows, LANES), F32))
    loss_part = jnp.sum(jnp.sum(terms, axis=1, keepdims=True), axis=0, keepdims=True)
    gradall[...] = slopes[...].reshape(held * points, LANES).astype(BF16)
    gradb[...] = gradall[pl.ds(0, flat), :]

    quads = LANES // 32
    tile_row = lax.broadcasted_iota(jnp.int32, (per, 32, LANES), 1)
    tile_at = my_part * per + lax.broadcasted_iota(jnp.int32, (per, 32, LANES), 0)
    variable = lax.rem(tile_at, quads) * 32 + tile_row
    spot = VARS % 32

    def split_loss(tiles):
        value = tiles[:, spot : spot + 1, :] + tiles[:, spot + 1 : spot + 2, :]
        high = value.astype(BF16).astype(F32)
        return jnp.where(
            variable == VARS, high, jnp.where(variable == VARS + 1, value - high, tiles)
        )

    row_all = lax.broadcasted_iota(jnp.int32, (LANES, 1), 0)
    loss_high = loss_part.astype(BF16).astype(F32)
    tail = jnp.where(
        row_all == VARS, loss_high, jnp.where(row_all == VARS + 1, loss_part - loss_high, 0.0)
    )
    for h in range(HALVES):
        for k in range(1, n_member):
            mix_copy(h, k).wait_recv()
    per_block = BLOCK // LANES
    for c in range(share):
        block = dot(gradall[...], mix[:, c].reshape(held * points, BLOCK), TN) + tail
        for b in range(per_block):
            for r in range(quads):
                u = (c * per_block + b) * quads + r
                local[u // per, u % per] = block[
                    r * 32 : (r + 1) * 32, b * LANES : (b + 1) * LANES
                ].astype(BF16)

    def part_copy(k):
        device, owner = part_peer(k)
        return pltpu.make_async_remote_copy(
            src_ref=local.at[owner],
            dst_ref=part.at[k],
            send_sem=part_s.at[k],
            recv_sem=part_r.at[k],
            device_id=device,
            device_id_type=MESH,
        )

    def plane_copy(k):
        return pltpu.make_async_remote_copy(
            src_ref=plane.at[me_z],
            dst_ref=plane.at[me_z],
            send_sem=plane_s.at[k],
            recv_sem=plane_r.at[k],
            device_id=plane_peer(k),
            device_id_type=MESH,
        )

    def area_peer(k):
        m = lax.rem(me_m + k // n_y, n_member)
        y = lax.rem(me_y + lax.rem(k, n_y), n_y)
        return m, y

    def full_copy(k):
        m, y = area_peer(k)
        return pltpu.make_async_remote_copy(
            src_ref=full.at[mine],
            dst_ref=full.at[mine],
            send_sem=full_s.at[k],
            recv_sem=full_r.at[k],
            device_id=(m, grid_at(y, me_z, core)),
            device_id_type=MESH,
        )

    def pass_copy(k):
        m = lax.rem(me_m + n_member - k // n_y, n_member)
        y = lax.rem(me_y + n_y - k % n_y, n_y)
        slot = (m * n_y + y) * n_core + core
        return pltpu.make_async_remote_copy(
            src_ref=full.at[slot],
            dst_ref=full.at[slot],
            send_sem=pass_s.at[k],
            recv_sem=pass_r.at[k],
            device_id=(me_m, grid_at(me_y, me_z, lax.rem(core + 1, n_core))),
            device_id_type=MESH,
        )

    def apart_by(k):
        return ring(k // n_y, n_member) + ring(k % n_y, n_y)

    area = n_member * n_y
    far_first = sorted(range(1, area), key=lambda k: -apart_by(k))

    def each(count, make, act):
        def step(k, c):
            getattr(make(k), act)()
            return c

        lax.fori_loop(1, count, step, 0)

    for k in sorted(range(1, parts), key=lambda k: -ring(k // n_core, n_y)):
        part_copy(k).start()

    for c in range(chunks):
        here = pl.ds(c * BLOCK, BLOCK)
        step = dot(gradb[...], wpad[:, here], NN)
        dmixed[:, here] = step
        dmixedb[:, here] = step.astype(BF16)
    for c in range(chunks):
        here = pl.ds(c * BLOCK, BLOCK)
        dattn[:, here] = dot(dmixedb[...], wout[here, :], NT).astype(BF16)

    scale = (width // HEADS) ** -0.5

    def backward(m, carry):
        rows = pl.ds(pl.multiple_of(m * points, points), points)
        number = cnt[...]
        outs = [spread_heads(dattn[rows, here]) for here in heres]
        dprobs = [dot(kv[m, :, there], out, NT) for there, out in zip(theres, outs)]
        shares = [probs[m, h] for h in pack_range]
        leans = [
            jnp.sum(number * one * share, axis=0, keepdims=True)
            for one, share in zip(dprobs, shares)
        ]
        dscores = [
            (share * (one - lean)).astype(BF16) for share, one, lean in zip(shares, dprobs, leans)
        ]
        dscores = [(number * one.astype(F32)).astype(BF16) for one in dscores]
        weights = [(number * one.astype(BF16).astype(F32)).astype(BF16) for one in shares]
        dqs = [dot(one, kv[m, :, here], TN) for one, here in zip(dscores, heres)]
        dks = [
            dot(one, spread_heads(query[rows, here]), NN) for one, here in zip(dscores, heres)
        ]
        dvs = [dot(one, out, NN) for one, out in zip(weights, outs)]
        for h in pack_range:
            dquery[rows, heres[h]] = (pick_heads(dqs[h]) * scale).astype(BF16)
            dkv[m, :, heres[h]] = dks[h].astype(BF16)
            dkv[m, :, theres[h]] = dvs[h].astype(BF16)
        return carry

    lax.fori_loop(0, members, backward, 0)

    def back_copy(side, c):
        return pltpu.make_async_remote_copy(
            src_ref=dsend.at[side, c],
            dst_ref=drecv.at[side, c],
            send_sem=back_s.at[side, c],
            recv_sem=back_r.at[side, c],
            device_id=(me_m, down if side == 0 else up),
            device_id_type=MESH,
        )

    def second_stage():
        each(parts, part_copy, "wait_recv")
        piece_sum = local[my_part].astype(F32)
        for k in range(1, parts):
            piece_sum = piece_sum + part[k].astype(F32)
        plane[me_z] = split_loss(piece_sum).astype(BF16)
        heard(relay.at[2])
        for k in sorted(range(1, n_z), key=lambda k: -min(k, n_z - k)):
            plane_copy(k).start()

    for c in range(chunks):
        here = pl.ds(c * BLOCK, BLOCK)
        rows = dkv[...].reshape(members * window, 2 * width)
        step = dot(rows, wqkv[here, pl.ds(width, 2 * width)], NT)
        step = step.reshape(members, window, BLOCK)
        for side, start in ((0, 0), (1, 2 * points)):
            dsend[side, c] = step[:, start : start + points].astype(BF16)
        if c == chunks // 2 - 1:
            second_stage()
        if c >= chunks // 2 - 1:
            for ready in range(c + 1) if c == chunks // 2 - 1 else (c,):
                back_copy(0, ready).start()
                back_copy(1, ready).start()
        dhid[:, :, here] = step[:, points : 2 * points]

    for c in range(chunks):
        here = pl.ds(c * BLOCK, BLOCK)
        step = dot(dquery[...], wqkv[here, pl.ds(0, width)], NT)
        dhid[:, :, here] = dhid[:, :, here] + step.reshape(members, points, BLOCK)

    each(n_z, plane_copy, "wait_recv")
    plane_sum = plane[0].astype(F32)
    for k in range(1, n_z):
        plane_sum = plane_sum + plane[k].astype(F32)
    full[mine] = (split_loss(plane_sum) * (1.0 / (points * n_grid))).astype(BF16)
    for k in far_first:
        full_copy(k).start()
    pass_copy(0).start()
    for c in range(chunks):
        here = pl.ds(c * BLOCK, BLOCK)
        for side in range(2):
            back_copy(side, c).wait_recv()
        extra = drecv[0, c].astype(F32) + drecv[1, c].astype(F32)
        dhid[:, :, here] = dhid[:, :, here] + extra

    for m in range(members):
        dnormed = dhid[m] * gain[...]
        norm = normed[m]
        first = jnp.mean(dnormed, axis=-1, keepdims=True)
        second = jnp.mean(dnormed * norm, axis=-1, keepdims=True)
        dstates = inverse[m] * (dnormed - first - norm * second)
        grad[m] = (dstates + dmixed[pl.ds(m * points, points), :]).astype(BF16)

    for h in range(HALVES):
        for i in range(2):
            halo_copy(h, i).wait_send()
        for k in range(1, n_member):
            pred_copy(h, k).wait_send()
            mix_copy(h, k).wait_send()
    each(parts, part_copy, "wait_send")
    each(n_z, plane_copy, "wait_send")
    for c in range(chunks):
        for side in range(2):
            back_copy(side, c).wait_send()

    for k in reversed(far_first):
        full_copy(k).wait_recv()
        pass_copy(k).start()
    each(area, full_copy, "wait_send")
    for k in range(area):
        pass_copy(k).wait_recv()
    total = jnp.zeros((1, 1), F32)
    for m in range(n_member):
        for u in range(parts * per):
            b, r = m * (bands // n_member) + u // quads, u % quads
            tile = full[m * parts + u // per, u % per].astype(F32)
            count = min(32, VARS - 32 * r)
            head_out[pl.ds(32 * r, count), pl.ds(b * LANES, LANES)] = tile[:count]
            if u == VARS // 32:
                total = total + tile[spot : spot + 1, 0:1] + tile[spot + 1 : spot + 2, 0:1]
    loss[...] = total * (1.0 / (VARS * total_members))
    for k in range(area):
        pass_copy(k).wait_send()


def results(loss, grad, head, loss_hbm, grad_hbm, head_hbm, sem):
    copies = [
        pltpu.make_async_copy(source, target, sem.at[i])
        for i, (source, target) in enumerate(((grad, grad_hbm), (head, head_hbm), (loss, loss_hbm)))
    ]
    for copy in copies:
        copy.start()
    for copy in copies:
        copy.wait()


def body(sizes, states, ln_gain, w_qkv, w_out, w_head, targets, neighbours, counts):
    n_member, n_y, n_z, n_core = sizes
    members, points, width = states.shape
    flat = members * points
    window = 3 * points
    group = n_member * n_y * n_core
    chunks = width // BLOCK
    cols = PACK * (width // HEADS)
    tiles = (LANES // 32) * (width // LANES)
    per = tiles // group
    vmem = pl.BlockSpec(memory_space=pltpu.VMEM)
    hbm = pl.BlockSpec(memory_space=pl.ANY)
    dma = pltpu.SemaphoreType.DMA
    operands = (states, ln_gain.reshape(1, width), w_qkv, w_out, w_head.T, targets, neighbours, counts)
    loss, grad, head = pl.pallas_call(
        functools.partial(kernel, sizes),
        out_shape=(
            jax.ShapeDtypeStruct((1, 1), F32),
            jax.ShapeDtypeStruct((members, points, width), BF16),
            jax.ShapeDtypeStruct((VARS, width), F32),
        ),
        in_specs=[hbm] * 8,
        out_specs=(vmem, vmem, vmem),
        scratch_shapes=[
            pltpu.VMEM((members, points, width), BF16),
            pltpu.VMEM((1, width), F32),
            pltpu.VMEM((width, 3 * width), BF16),
            pltpu.VMEM((width, width), BF16),
            pltpu.VMEM((VARS, width), BF16),
            pltpu.VMEM((points, VARS), F32),
            pltpu.SMEM(neighbours.shape, jnp.int32),
            pltpu.SMEM((1,), jnp.int32),
            pltpu.VMEM((LANES, width), BF16),
            pltpu.VMEM((points, LANES), F32),
            pltpu.VMEM((flat, width), BF16),
            pltpu.VMEM((2, flat, width), BF16),
            pltpu.VMEM((flat, width), BF16),
            pltpu.VMEM((members, window, 2 * width), BF16),
            pltpu.VMEM((members, points, width), F32),
            pltpu.VMEM((members, points, 1), F32),
            pltpu.VMEM((window, LANES), F32),
            pltpu.VMEM((PACK * points, cols), F32),
            pltpu.VMEM((members, HEADS // PACK, window, PACK * points), F32),
            pltpu.VMEM((flat, width), BF16),
            pltpu.VMEM((chunks, flat, BLOCK), BF16),
            pltpu.VMEM((n_member, chunks // n_member, flat, BLOCK), BF16),
            pltpu.VMEM((n_member, flat, LANES), BF16),
            pltpu.VMEM((n_member * members, points, LANES), F32),
            pltpu.VMEM((n_member * members, points, LANES), F32),
            pltpu.VMEM((points, LANES), F32),
            pltpu.VMEM((n_member * flat, LANES), BF16),
            pltpu.VMEM((flat, LANES), BF16),
            pltpu.VMEM((n_y * n_core, per, 32, LANES), BF16),
            pltpu.VMEM((n_y * n_core, per, 32, LANES), BF16),
            pltpu.VMEM((n_z, per, 32, LANES), BF16),
            pltpu.VMEM((group, per, 32, LANES), BF16),
            pltpu.VMEM((flat, width), F32),
            pltpu.VMEM((flat, width), BF16),
            pltpu.VMEM((flat, width), BF16),
            pltpu.VMEM((flat, width), BF16),
            pltpu.VMEM((members, window, 2 * width), BF16),
            pltpu.VMEM((2, chunks, members, points, BLOCK), BF16),
            pltpu.VMEM((2, chunks, members, points, BLOCK), BF16),
            pltpu.VMEM((members, points, width), F32),
            pltpu.SemaphoreType.REGULAR((RELAYS,)),
            dma((6,)),
            dma((3 * width // (2 * BLOCK) + 1,)),
            dma((HALVES, 2)),
            dma((HALVES, 2)),
            dma((HALVES, n_member)),
            dma((HALVES, n_member)),
            dma((HALVES, n_member)),
            dma((HALVES, n_member)),
            dma((n_y * n_core,)),
            dma((n_y * n_core,)),
            dma((n_z,)),
            dma((n_z,)),
            dma((n_member * n_y,)),
            dma((n_member * n_y,)),
            dma((n_member * n_y,)),
            dma((n_member * n_y,)),
            dma((2, chunks)),
            dma((2, chunks)),
        ],
        compiler_params=pltpu.CompilerParams(
            collective_id=0, has_side_effects=True, vmem_limit_bytes=VMEM_BYTES
        ),
    )(*(pltpu.with_memory_space_constraint(x, pltpu.HBM) for x in operands[:-1]), operands[-1])
    held = [loss, *(pltpu.with_memory_space_constraint(x, pltpu.VMEM) for x in (grad, head))]
    loss, grad, head = pl.pallas_call(
        results,
        out_shape=tuple(jax.ShapeDtypeStruct(x.shape, x.dtype) for x in held),
        in_specs=[hbm] * 3,
        out_specs=(hbm,) * 3,
        scratch_shapes=[dma((3,))],
    )(*held)
    return (loss.reshape(()), grad, head.T)


def solution(mesh):
    placed = (
        P("member", "grid", None),
        P(),
        P(),
        P(),
        P(),
        P("grid", None),
        P("grid", None),
        P("grid"),
    )
    n_core = 2
    n_z = min(8, mesh.shape["grid"] // n_core)
    sizes = (mesh.shape["member"], mesh.shape["grid"] // (n_z * n_core), n_z, n_core)
    return jax.shard_map(
        functools.partial(body, sizes),
        mesh=mesh,
        in_specs=placed,
        out_specs=(P(), P("member", "grid", None), P()),
        check_vma=False,
    )
```
